32 devices in a mesh: orb: 4 (over z), space: 8 (over y, x, core).
Axes of the slice: x: 2, y: 2, z: 4, core: 2. Of those that a mesh axis runs over, the one named last changes fastest.
Arguments:
- orbitals: float32 [32, 128, 128], P('orb', 'space'), may hold values from 0 to 0.25
- points: float32 [3, 128, 128], P(None, 'space')
- quad_weight: float32 [128, 128], P('space'), may hold values from 0.5 to 2
- external: float32 [128, 128], P('space'), may hold values from -3 to 1
- screening: float32 [32], replicated, may hold values from 0.05 to 2
- level_index: int32 [32], P('orb'), may hold values from 0 to 31
- near_cells: int32 [128, 27], P('space'), may hold values from -1 to 127, as said below
- far_cells: int32 [128, 42], P('space'), may hold values from -1 to 127, as said below
Outputs:
- new_orbitals: float32 [32, 128, 128], P('orb', 'space')
- hartree: float32 [128, 128], P('space')
The draws below stay inside these ranges and needn't reach their ends.
Inputs may be any that keep to these rules, and one draw needn't show every extreme that they name: `near_cells`: row t lists distinct cells in increasing order, then -1: every cell of its own plane whose first two box indices differ from those of t by at most one (t itself among them), the cells directly above and below t, and some of the other cells of the two adjacent planes whose first two box indices differ from those of t by at most one. Some row holds 27 cells. `far_cells`: row t lists in increasing order, then -1, all cells of the planes floor(t / 16) - 1 to floor(t / 16) + 1 that are not in row t of near_cells. Some row holds 42 cells.
All inputs are finite; a program needn't handle non-finite values.
Results may differ from the reference program's by a relative error of at most 0.0003.
Values sent between devices are 32-bit elements; how exact they have to be, the bound alone decides.
No kernel may reach another device: no remote copies, remote signals or barrier semaphores. Data moves between devices by JAX's collectives and lax.ppermute only.
A program may use at most 64 MiB of HBM per device.

```python
import math
import jax
import jax.numpy as jnp
from jax import lax

ORBS = 32
PTS = 128
NODES = 4
NKAPPA = 32
NNEAR = 27
NFAR = 42
CELLS = 128


def draw_points(key, part):
    scaled = jax.random.uniform(jax.random.fold_in(key, 4409), (3, CELLS, PTS), jnp.float32)
    cell_ids = jnp.arange(CELLS, dtype=jnp.int32)
    corners = jnp.stack([cell_ids % 4, cell_ids // 4 % 4, cell_ids // 16]).astype(jnp.float32)
    return (corners[:, :, None] + scaled) * 0.25


def neighbour_lists(key):
    keys = jax.random.split(jax.random.fold_in(key, 7301), 5)
    planes = CELLS // 16
    choices_bits = jax.random.randint(keys[0], (CELLS, 48), 0, 2)
    pick_inner = jax.random.randint(keys[1], (), 0, 4)
    plane_inner = jax.random.randint(keys[2], (), 1, planes - 1)
    pick_corner = jax.random.randint(keys[3], (), 0, 4)
    plane_corner = jax.random.randint(keys[4], (), 1, planes - 1)
    full_cell = 16 * plane_inner + 5 + pick_inner % 2 + 4 * (pick_inner // 2)
    empty_cell = 16 * plane_corner + 3 * (pick_corner % 2) + 12 * (pick_corner // 2)
    target = jnp.arange(CELLS, dtype=jnp.int32)[:, None]
    slot = jnp.arange(48, dtype=jnp.int32)[None, :]
    level = target // 16 + slot // 16 - 1
    within = slot % 16
    candidate = level * 16 + within
    valid = (level >= 0) & (level < planes)
    close_x = jnp.abs(within % 4 - target % 4) <= 1
    close_y = jnp.abs(within // 4 - target // 4 % 4) <= 1
    flat_plane = slot // 16 == 1
    face_cell = within == target % 16
    bits_now = jnp.where(target == full_cell, 1, jnp.where(target == empty_cell, 0, choices_bits))
    near_flag = valid & close_x & close_y & (flat_plane | face_cell | (bits_now == 1))
    far_flag = valid & jnp.logical_not(near_flag)
    near_order = jnp.argsort(jnp.where(near_flag, 0, 1), axis=1, stable=True)
    far_order = jnp.argsort(jnp.where(far_flag, 0, 1), axis=1, stable=True)
    near_list = jnp.take_along_axis(jnp.where(near_flag, candidate, -1), near_order, axis=1)[:, :NNEAR]
    far_list = jnp.take_along_axis(jnp.where(far_flag, candidate, -1), far_order, axis=1)[:, :NFAR]
    return (near_list.astype(jnp.int32), far_list.astype(jnp.int32))


def draw_near_cells(key, part):
    return neighbour_lists(key)[0]


def draw_far_cells(key, part):
    return neighbour_lists(key)[1]


def plant(result, stream_key, least, top_value):
    shape = result.shape
    index_at = [jax.random.randint(jax.random.fold_in(stream_key, axis), (), 0, shape[axis]) for axis in range(len(shape))]
    result = result.at[tuple(index_at)].set(least)
    longest = shape.index(max(shape))
    index_at[longest] = (index_at[longest] + 1) % shape[longest]
    return result.at[tuple(index_at)].set(top_value)


def shard_levels(rng, shape, pieces, smallest, high):
    gain, own = 1.0, jax.random.fold_in(rng, 6)
    for position, parts in pieces:
        steps = jnp.exp(jax.random.uniform(jax.random.fold_in(own, position), (parts,), jnp.float32, smallest / len(pieces), high / len(pieces)))
        gain = gain * jnp.repeat(steps, shape[position] // parts).reshape([-1 if axis == position else 1 for axis in range(len(shape))])
    return gain


def setup_inputs(seed: int = 0) -> dict:
    splits = jax.random.split(jax.random.key(seed), 9)
    orbitals = jnp.clip(0.25 * jax.random.uniform(splits[0], (ORBS, CELLS, PTS), jnp.float32) ** shard_levels(splits[0], (ORBS, CELLS, PTS), ((0, 4), (1, 8)), -0.2, 0.2), 0.0, 0.25)
    points = draw_points(jax.random.fold_in(splits[8], 71), 0)
    quad_weight = jnp.clip(jnp.exp(math.log(2.0) - 1.3862944 * jax.random.uniform(splits[2], (CELLS, PTS), jnp.float32) ** shard_levels(splits[2], (CELLS, PTS), ((0, 8),), -0.2, 0.2)), 0.5, 2.0)
    external = jnp.clip(-3.0 + 4.0 * jax.random.uniform(splits[3], (CELLS, PTS), jnp.float32) ** shard_levels(splits[3], (CELLS, PTS), ((0, 8),), -0.2, 0.2), -3.0, 1.0)
    screening = jnp.clip(jnp.exp(jax.random.uniform(splits[4], (NKAPPA,), jnp.float32, math.log(0.05), math.log(2.0))), 0.05, 2.0)
    level_index = plant(jax.random.randint(splits[5], (ORBS,), 0, NKAPPA), jax.random.fold_in(splits[5], 1), 0, NKAPPA - 1).astype(jnp.int32)
    near_cells = draw_near_cells(jax.random.fold_in(splits[8], 71), 0)
    far_cells = draw_far_cells(jax.random.fold_in(splits[8], 71), 0)
    return dict(orbitals=orbitals, points=points, quad_weight=quad_weight, external=external, screening=screening, level_index=level_index, near_cells=near_cells, far_cells=far_cells)


cell_side = 0.25
soften = 6.25e-06
green_scale = -0.5 / math.pi

def cheb_nodes(node_count):
    indices = jnp.arange(node_count, dtype=jnp.int32).astype(jnp.float32)
    return jnp.cos((2.0 * indices + 1.0) * (math.pi / (2.0 * node_count)))

def lagrange(scaled, node_set, node_count):
    factors = []
    for outer_node in range(node_count):
        running = jnp.ones_like(scaled)
        for inner_node in range(node_count):
            if inner_node != outer_node:
                running = running * ((scaled - node_set[inner_node]) / (node_set[outer_node] - node_set[inner_node]))
        factors.append(running)
    return jnp.stack(factors)

def anterp(locations, corners, extent):
    node_set = cheb_nodes(NODES)
    scaled = 2.0 * (locations - corners[:, :, None]) / extent[:, None, None] - 1.0
    basis_x = lagrange(scaled[0], node_set, NODES)
    basis_y = lagrange(scaled[1], node_set, NODES)
    basis_z = lagrange(scaled[2], node_set, NODES)
    weights = basis_x[:, None, None] * basis_y[None, :, None] * basis_z[None, None, :]
    return weights.reshape((NODES * NODES * NODES,) + locations.shape[1:])

def proxies(corners, extent):
    node_set = cheb_nodes(NODES)
    offset = 0.5 * (node_set + 1.0)
    grid_shape = (NODES, NODES, NODES) + corners.shape[1:]
    grid_x = jnp.broadcast_to((corners[0][None, :] + offset[:, None] * extent[0])[:, None, None], grid_shape)
    grid_y = jnp.broadcast_to((corners[1][None, :] + offset[:, None] * extent[1])[None, :, None], grid_shape)
    grid_z = jnp.broadcast_to((corners[2][None, :] + offset[:, None] * extent[2])[None, None, :], grid_shape)
    stacked = jnp.stack([grid_x, grid_y, grid_z]).reshape((3, NODES * NODES * NODES) + corners.shape[1:])
    return jnp.moveaxis(stacked, 1, 2)

def cell_lows(cell_ids):
    return jnp.stack([cell_ids % 4, cell_ids // 4 % 4, cell_ids // 16]).astype(jnp.float32) * cell_side

def plane_lows(levels):
    zeroes = jnp.zeros_like(levels)
    return jnp.stack([zeroes, zeroes, levels]).astype(jnp.float32) * cell_side

def cell_extent():
    return jnp.full((3,), cell_side, jnp.float32)

def plane_extent():
    return jnp.array([4.0 * cell_side, 4.0 * cell_side, cell_side], jnp.float32)

def kernel_sum(targets, locations, values, decay_rates):
    squared = jnp.zeros((targets.shape[1], locations.shape[1]), jnp.float32)
    for component in range(3):
        difference = targets[component][:, None] - locations[component][None, :]
        squared = squared + difference * difference
    distance = jnp.sqrt(squared + soften)
    kernel = jnp.exp(-decay_rates[:, None, None] * distance[None]) / distance[None]
    return lax.optimization_barrier(jnp.sum(kernel * values[:, None, :], axis=2))

def cell_moments(mapping, values):
    return jnp.einsum('pcj,rcj->rcp', mapping, values, precision=lax.Precision.HIGHEST)

def plane_moments(mapping, values):
    grouped = values.reshape(values.shape[0], mapping.shape[1], -1)
    return jnp.einsum('pgj,rgj->rgp', mapping, grouped, precision=lax.Precision.HIGHEST)

def evaluate(points, values, cell_mom, plane_proxy, plane_mom, near_cells, far_cells, decay_rates):
    kinds = values.shape[0]
    levels = jnp.arange(plane_mom.shape[1], dtype=jnp.int32)
    extent = cell_extent()

    def per_cell(target):
        near_ids = near_cells[target]
        near_live = (near_ids >= 0).astype(jnp.float32)
        near_slot = jnp.maximum(near_ids, 0)
        near_src = points[:, near_slot, :].reshape(3, -1)
        near_val = (values[:, near_slot, :] * near_live[None, :, None]).reshape(kinds, -1)
        far_ids = far_cells[target]
        far_live = (far_ids >= 0).astype(jnp.float32)
        far_slot = jnp.maximum(far_ids, 0)
        far_src = proxies(cell_lows(far_slot), extent).reshape(3, -1)
        far_val = (cell_mom[:, far_slot, :] * far_live[None, :, None]).reshape(kinds, -1)
        plane_keep = (jnp.abs(levels - target // 16) >= 2).astype(jnp.float32)
        coarse_val = (plane_mom * plane_keep[None, :, None]).reshape(kinds, -1)
        points_here = points[:, target, :]
        return kernel_sum(points_here, near_src, near_val, decay_rates) + kernel_sum(points_here, far_src, far_val, decay_rates) + kernel_sum(points_here, plane_proxy, coarse_val, decay_rates)
    return lax.map(per_cell, jnp.arange(points.shape[1], dtype=jnp.int32))

def reference(orbitals, points, quad_weight, external, screening, level_index, near_cells, far_cells):
    cell_count = points.shape[1]
    planes = cell_count // 16
    weight = quad_weight * (cell_side ** 3 / PTS)
    density = 2.0 * lax.optimization_barrier(jnp.sum(orbitals * orbitals, axis=0))
    cell_map = anterp(points, cell_lows(jnp.arange(cell_count, dtype=jnp.int32)), cell_extent())
    levels = jnp.arange(planes, dtype=jnp.int32)
    plane_map = anterp(points.reshape(3, planes, -1), plane_lows(levels), plane_extent())
    plane_proxy = proxies(plane_lows(levels), plane_extent()).reshape(3, -1)
    charge = (weight * density)[None]
    charge_mom = cell_moments(cell_map, charge)
    charge_plane = plane_moments(plane_map, charge)
    hartree = evaluate(points, charge, charge_mom, plane_proxy, charge_plane, near_cells, far_cells, jnp.zeros((1,), jnp.float32))[:, 0, :]
    potential = external + hartree
    sources = (weight * potential)[None] * orbitals
    source_mom = cell_moments(cell_map, sources)
    source_plane = plane_moments(plane_map, sources)
    decay_rates = screening[level_index]
    updated = green_scale * evaluate(points, sources, source_mom, plane_proxy, source_plane, near_cells, far_cells, decay_rates)
    return (jnp.transpose(updated, (1, 0, 2)), hartree)
```

```python
import functools
import math

import jax
import jax.numpy as jnp
import numpy as np
from jax import lax
from jax.experimental import pallas as pl
from jax.experimental.pallas import tpu as pltpu
from jax.sharding import PartitionSpec as P

NODES = 4
LANES = 128
PLANE = 16
ROWS = 8
HALF = NODES**3

cell_side = 0.25
soften = 6.25e-06
green_scale = -0.5 / math.pi
log2e = math.log2(math.e)
highest = lax.Precision.HIGHEST

node_set = np.cos((2.0 * np.arange(NODES) + 1.0) * (math.pi / (2.0 * NODES)))
roots = [[node_set[m] for m in range(NODES) if m != a] for a in range(NODES)]
scales = [1.0 / np.prod([node_set[a] - r for r in roots[a]]) for a in range(NODES)]


def basis_rows():
    row = np.arange(ROWS)
    out = []
    for pick in (row // 4, 2 + row // 4, row % 4):
        for k in range(NODES - 1):
            out.append([roots[a][k] for a in pick])
        out.append([scales[a] for a in pick])
    return np.broadcast_to(np.array(out, np.float32)[:, :, None], (12, ROWS, LANES)).copy()


def proxy_table(planes, window):
    offset = 0.5 * (node_set + 1.0)
    p = np.arange(LANES) % HALF
    offs = np.stack([offset[p // 16], offset[p // 4 % 4], offset[p % 4]])
    cells = np.arange(window)
    lows = np.stack([cells % 4, cells // 4 % 4, cells // 16]) * cell_side
    near = lows[:, :, None] + offs[:, None, :] * cell_side
    levels = np.arange(planes)
    lows = np.stack([0 * levels, 0 * levels, levels]) * cell_side
    far = lows[:, :, None] + offs[:, None, :] * np.array([1.0, 1.0, cell_side])[:, None, None]
    table = np.zeros((window + planes, ROWS, LANES), np.float32)
    table[:, :3] = np.moveaxis(np.concatenate([near, far], 1), 0, 1)
    return table


def poly(u, r0, r1, r2, scale):
    return ((u - r0) * (u - r1)) * ((u - r2) * scale)


def weights(cst, x, y, z, lows, sides):
    ux, uy, uz = (
        jnp.broadcast_to(2.0 * (c - lo) / e - 1.0, (ROWS, LANES)) for c, lo, e in zip((x, y, z), lows, sides)
    )
    pz = poly(uz, cst[8], cst[9], cst[10], cst[11])
    pyz = [poly(uy, cst[4 * k], cst[4 * k + 1], cst[4 * k + 2], cst[4 * k + 3]) * pz for k in range(2)]
    parts = []
    for a in range(NODES):
        px = poly(ux, *(float(r) for r in roots[a]), float(scales[a]))
        parts += [px * pyz[0], px * pyz[1]]
    return jnp.concatenate(parts + parts, axis=0)


def cell_low(cell):
    return [(cell % 4).astype(jnp.float32) * cell_side, (cell // 4 % 4).astype(jnp.float32) * cell_side]


def dot_nt(a, b):
    return lax.dot_general(a, b, (((1,), (1,)), ((), ())), precision=highest, preferred_element_type=jnp.float32)


def charge_kernel(meta, cst, own, density, out):
    z_low = meta[0].astype(jnp.float32) * cell_side
    cells = own.shape[0]

    def step(c, acc):
        charge = own[c, 4:5, :] * density[pl.ds(c, 1), :]
        out[pl.ds(c, 1), :] = charge
        w = weights(cst, own[c, 0:1, :], own[c, 1:2, :], own[c, 2:3, :], (0.0, 0.0, z_low), (1.0, 1.0, cell_side))
        return acc + w * charge

    acc = lax.fori_loop(0, cells, step, jnp.zeros((LANES, LANES), jnp.float32))
    out[cells:, :] = dot_nt(jnp.ones((ROWS, LANES), jnp.float32), acc)


def field(kinds, group, unroll, meta, counts, near, far, rate, table, win, val, mom, tgt, src, srcv, acc, write):
    cells = near.shape[0]
    window = win.shape[0]
    planes = table.shape[0] - window
    me = meta[0]
    base = me * cells - PLANE
    below = jnp.maximum(me - 1, 0)
    live_planes = below + jnp.maximum(planes - 2 - me, 0)
    low_half = lax.broadcasted_iota(jnp.int32, (1, LANES), 1) < HALF

    def per_cell(t, carry):
        n_near, n_far = counts[t, 0], counts[t, 1]
        n_items = n_far + live_planes

        def put_near(j, c):
            slot = near[t, j] - base
            src[j] = win[slot, :ROWS, :]
            srcv[j] = val[slot]
            return c

        lax.fori_loop(0, n_near, put_near, 0)

        def item(j):
            j = jnp.minimum(j, n_items - 1)
            p = j - n_far
            level = jnp.where(p < below, p, p + (me + 2 - below))
            cell = far[t, jnp.minimum(j, far.shape[1] - 1)] - base
            return jnp.where(j < n_far, cell, window + level)

        n_pairs = (n_items + 1) // 2

        def put_far(j, c):
            first, second = item(2 * j), item(2 * j + 1)
            live = (2 * j + 1 < n_items).astype(jnp.float32)
            src[n_near + j] = jnp.where(low_half, table[first], table[second])
            srcv[n_near + j] = jnp.where(low_half, mom[first], mom[second] * live)
            return c

        lax.fori_loop(0, n_pairs, put_far, 0)
        n_chunks = n_near + n_pairs
        for u in range(unroll - 1):
            src[n_chunks + u] = jnp.zeros(src.shape[1:], jnp.float32)
            srcv[n_chunks + u] = jnp.zeros(srcv.shape[1:], jnp.float32)
        for d in range(3):
            row = win[PLANE + t, d : d + 1, :]
            tgt[d] = jnp.broadcast_to(row, (LANES, LANES)).T

        height = group * ROWS

        def per_group(g, c):
            at = pl.multiple_of(g * height, height)
            tx, ty, tz = (tgt[d, pl.ds(at, height), :] for d in range(3))

            def step(k, accs):
                accs = list(accs)
                for u in range(unroll):
                    slot = k * unroll + u
                    dx = tx - src[slot, 0:1, :]
                    dy = ty - src[slot, 1:2, :]
                    dz = tz - src[slot, 2:3, :]
                    sq = (dx * dx + dy * dy) + (dz * dz + soften)
                    inv = lax.rsqrt(sq)
                    if rate is None:
                        accs[0] = accs[0] + inv * srcv[slot, 0:1, :]
                    else:
                        dist = sq * inv
                        for i in range(kinds):
                            accs[i] = accs[i] + (jnp.exp2(dist * rate[i]) * inv) * srcv[slot, i : i + 1, :]
                return tuple(accs)

            zero = jnp.zeros((height, LANES), jnp.float32)
            accs = lax.fori_loop(0, (n_chunks + unroll - 1) // unroll, step, (zero,) * kinds)
            for i in range(kinds):
                acc[i, pl.ds(at, height), :] = accs[i]
            return c

        lax.fori_loop(0, LANES // height, per_group, 0)
        ones = jnp.ones((ROWS, LANES), jnp.float32)
        for i in range(kinds):
            write(t, i, dot_nt(ones, acc[i])[0:1, :])
        return carry

    lax.fori_loop(0, cells, per_cell, 0)


def window_moments(cst, win, val, mom, me):
    kinds = val.shape[1]

    def step(c, carry):
        z_low = (me - 1 + c // PLANE).astype(jnp.float32) * cell_side
        w = weights(cst, win[c, 0:1, :], win[c, 1:2, :], win[c, 2:3, :], (*cell_low(c), z_low), (cell_side,) * 3)
        v = val[c]
        if kinds == 1:
            v = jnp.broadcast_to(v, (ROWS, LANES))
        mom[c] = dot_nt(v, w)[:kinds, :]
        return carry

    lax.fori_loop(0, win.shape[0], step, 0)


def plane_at(meta, g):
    return lax.bitwise_xor(meta[0], g)


def hartree_kernel(
    group, unroll, meta, counts, near, far, cst, table, win, gathered, out, val, mom, tgt, src, srcv, acc
):
    cells = near.shape[0]
    planes = gathered.shape[0]
    kinds = win.shape[1] - ROWS
    me = meta[0]
    for k in range(3):
        there = jnp.clip(me - 1 + k, 0, planes - 1)
        val[pl.ds(k * PLANE, PLANE), 0, :] = gathered[plane_at(meta, there), :PLANE, :]

    def put_plane(g, c):
        mom[win.shape[0] + g] = gathered[plane_at(meta, g), cells : cells + 1, :]
        return c

    lax.fori_loop(0, planes, put_plane, 0)
    window_moments(cst, win, val, mom, me)

    def write(t, i, row):
        out[pl.ds(t, 1), :] = row

    field(1, group, unroll, meta, counts, near, far, None, table, win, val, mom, tgt, src, srcv, acc, write)
    z_low = me.astype(jnp.float32) * cell_side

    def step(c, total):
        there = PLANE + c
        w = weights(
            cst, win[there, 0:1, :], win[there, 1:2, :], win[there, 2:3, :], (0.0, 0.0, z_low), (1.0, 1.0, cell_side)
        )
        v = win[there, ROWS:, :] * (win[there, 4:5, :] * (win[there, 3:4, :] + out[pl.ds(c, 1), :]))
        return total + dot_nt(v, w)

    out[cells:, :] = lax.fori_loop(0, cells, step, jnp.zeros((kinds, LANES), jnp.float32))


def orbital_kernel(
    group, unroll, meta, counts, near, far, rate, cst, table, win, gathered, out, val, mom, tgt, src, srcv, acc
):
    cells = near.shape[0]
    planes = gathered.shape[0]
    kinds = out.shape[0]
    me = meta[0]
    for k in range(3):
        there = plane_at(meta, jnp.clip(me - 1 + k, 0, planes - 1))

        def put(c, carry):
            at = k * PLANE + c
            scaled = win[at, 4:5, :] * (win[at, 3:4, :] + gathered[there, pl.ds(c, 1), :])
            val[at] = win[at, ROWS:, :] * scaled
            return carry

        lax.fori_loop(0, PLANE, put, 0)

    def put_plane(g, c):
        mom[win.shape[0] + g] = gathered[plane_at(meta, g), cells:, :]
        return c

    lax.fori_loop(0, planes, put_plane, 0)
    window_moments(cst, win, val, mom, me)

    def write(t, i, row):
        out[i, pl.ds(t, 1), :] = row * green_scale

    field(kinds, group, unroll, meta, counts, near, far, rate, table, win, val, mom, tgt, src, srcv, acc, write)


def gather_xor(block, axis):
    count = lax.axis_size(axis)
    out = block[None]
    bit = 1
    while bit < count:
        out = jnp.concatenate([out, lax.ppermute(out, axis, [(i, i ^ bit) for i in range(count)])], axis=0)
        bit *= 2
    return out


def sum_xor(value, axis):
    count = lax.axis_size(axis)
    bit = 1
    while bit < count:
        value = value + lax.ppermute(value, axis, [(i, i ^ bit) for i in range(count)])
        bit *= 2
    return value


def smem():
    return pl.BlockSpec(memory_space=pltpu.SMEM)


def vmem():
    return pl.BlockSpec(memory_space=pltpu.VMEM)


def scratch(kinds, window, planes, chunks):
    return [
        pltpu.VMEM((window, kinds, LANES), jnp.float32),
        pltpu.VMEM((window + planes, kinds, LANES), jnp.float32),
        pltpu.VMEM((3, LANES, LANES), jnp.float32),
        pltpu.VMEM((chunks, ROWS, LANES), jnp.float32),
        pltpu.VMEM((chunks, kinds, LANES), jnp.float32),
        pltpu.VMEM((kinds, LANES, LANES), jnp.float32),
    ]


def body(orbitals, points, quad_weight, external, screening, level_index, near_cells, far_cells):
    kinds, cells, point_count = orbitals.shape
    planes = lax.axis_size("space")
    window = cells + 2 * PLANE
    me = lax.axis_index("space")
    meta = jnp.full((1,), me, jnp.int32)
    params = pltpu.CompilerParams(vmem_limit_bytes=48 * 1024 * 1024)

    density = sum_xor(2.0 * jnp.sum(orbitals * orbitals, axis=0), "orb")
    weight = quad_weight * (cell_side**3 / point_count)
    own = jnp.concatenate(
        [
            jnp.transpose(points, (1, 0, 2)),
            external[:, None],
            weight[:, None],
            jnp.zeros((cells, 3, point_count), jnp.float32),
            jnp.transpose(orbitals, (1, 0, 2)),
        ],
        axis=1,
    )
    ends = planes - 1
    win = jnp.concatenate(
        [
            lax.ppermute(own, "space", [(i, i + 1) for i in range(ends)]),
            own,
            lax.ppermute(own, "space", [(i + 1, i) for i in range(ends)]),
        ],
        axis=0,
    )
    cst = jnp.asarray(basis_rows())
    base_table = proxy_table(planes, window)
    shift = np.zeros(base_table.shape, np.float32)
    shift[:window, 2] = cell_side
    table = jnp.asarray(base_table) + jnp.asarray(shift) * (me - 1).astype(jnp.float32)
    counts = jnp.stack(
        [jnp.sum((near_cells >= 0).astype(jnp.int32), 1), jnp.sum((far_cells >= 0).astype(jnp.int32), 1)], axis=1
    )
    level_match = level_index[:, None] == jnp.arange(screening.shape[0], dtype=jnp.int32)[None, :]
    rate = jnp.sum(jnp.where(level_match, screening[None, :], 0.0), axis=1) * (-log2e)

    charges = pl.pallas_call(
        charge_kernel,
        out_shape=jax.ShapeDtypeStruct((cells + ROWS, LANES), jnp.float32),
        in_specs=[smem(), vmem(), vmem(), vmem()],
        out_specs=vmem(),
        compiler_params=params,
        name="charge",
    )(meta, cst, own, density)
    charges = gather_xor(charges, "space")

    slots = near_cells.shape[1] + (far_cells.shape[1] + planes + 1) // 2
    group, unroll = 16, 2
    potentials = pl.pallas_call(
        functools.partial(hartree_kernel, group, unroll),
        out_shape=jax.ShapeDtypeStruct((cells + kinds, LANES), jnp.float32),
        in_specs=[smem()] * 4 + [vmem()] * 4,
        out_specs=vmem(),
        scratch_shapes=scratch(1, window, planes, slots + unroll),
        compiler_params=params,
        name="hartree",
    )(meta, counts, near_cells, far_cells, cst, table, win, charges)
    gathered = gather_xor(potentials, "space")

    group, unroll = 4, 4
    updated = pl.pallas_call(
        functools.partial(orbital_kernel, group, unroll),
        out_shape=jax.ShapeDtypeStruct((kinds, cells, LANES), jnp.float32),
        in_specs=[smem()] * 5 + [vmem()] * 4,
        out_specs=vmem(),
        scratch_shapes=scratch(kinds, window, planes, slots + unroll),
        compiler_params=params,
        name="orbitals",
    )(meta, counts, near_cells, far_cells, rate, cst, table, win, gathered)
    return updated, potentials[:cells]


def solution(mesh):
    in_specs = (
        P("orb", "space", None),
        P(None, "space", None),
        P("space", None),
        P("space", None),
        P(),
        P("orb"),
        P("space", None),
        P("space", None),
    )
    out_specs = (P("orb", "space", None), P("space", None))
    return jax.shard_map(body, mesh=mesh, in_specs=in_specs, out_specs=out_specs, check_vma=False)
```

```python
import functools
import math

import jax
import jax.numpy as jnp
import numpy as np
from jax import lax
from jax.experimental import pallas as pl
from jax.experimental.pallas import tpu as pltpu
from jax.sharding import PartitionSpec as P

NODES = 4
LANES = 128
PLANE = 16
ROWS = 8
HALF = NODES**3

cell_side = 0.25
soften = 6.25e-06
green_scale = -0.5 / math.pi
log2e = math.log2(math.e)
highest = lax.Precision.HIGHEST

node_set = np.cos((2.0 * np.arange(NODES) + 1.0) * (math.pi / (2.0 * NODES)))
roots = [[node_set[m] for m in range(NODES) if m != a] for a in range(NODES)]
scales = [1.0 / np.prod([node_set[a] - r for r in roots[a]]) for a in range(NODES)]


def basis_rows():
    row = np.arange(ROWS)
    out = []
    for pick in (row // 4, 2 + row // 4, row % 4):
        for k in range(NODES - 1):
            out.append([roots[a][k] for a in pick])
        out.append([scales[a] for a in pick])
    return np.broadcast_to(np.array(out, np.float32)[:, :, None], (12, ROWS, LANES)).copy()


def proxy_table(planes, window):
    offset = 0.5 * (node_set + 1.0)
    p = np.arange(LANES) % HALF
    offs = np.stack([offset[p // 16], offset[p // 4 % 4], offset[p % 4]])
    cells = np.arange(window)
    lows = np.stack([cells % 4, cells // 4 % 4, cells // 16]) * cell_side
    near = lows[:, :, None] + offs[:, None, :] * cell_side
    levels = np.arange(planes)
    lows = np.stack([0 * levels, 0 * levels, levels]) * cell_side
    far = lows[:, :, None] + offs[:, None, :] * np.array([1.0, 1.0, cell_side])[:, None, None]
    table = np.zeros((window + planes, ROWS, LANES), np.float32)
    table[:, :3] = np.moveaxis(np.concatenate([near, far], 1), 0, 1)
    return table


def poly(u, r0, r1, r2, scale):
    return ((u - r0) * (u - r1)) * ((u - r2) * scale)


def weights(cst, x, y, z, lows, sides):
    ux, uy, uz = (
        jnp.broadcast_to(2.0 * (c - lo) / e - 1.0, (ROWS, LANES)) for c, lo, e in zip((x, y, z), lows, sides)
    )
    pz = poly(uz, cst[8], cst[9], cst[10], cst[11])
    pyz = [poly(uy, cst[4 * k], cst[4 * k + 1], cst[4 * k + 2], cst[4 * k + 3]) * pz for k in range(2)]
    parts = []
    for a in range(NODES):
        px = poly(ux, *(float(r) for r in roots[a]), float(scales[a]))
        parts += [px * pyz[0], px * pyz[1]]
    return jnp.concatenate(parts + parts, axis=0)


def cell_low(cell):
    return [(cell % 4).astype(jnp.float32) * cell_side, (cell // 4 % 4).astype(jnp.float32) * cell_side]


def dot_nt(a, b):
    return lax.dot_general(a, b, (((1,), (1,)), ((), ())), precision=highest, preferred_element_type=jnp.float32)


def gather_xor(block, axis, pairs):
    count = lax.axis_size(axis)
    out = block[None]
    while out.shape[0] < count:
        have = out.shape[0]
        steps = range(1, 4 if (have > 1 or pairs) and have * 4 <= count else 2)
        parts = [lax.ppermute(out, axis, [(i, i ^ (have * j)) for i in range(count)]) for j in steps]
        out = jnp.concatenate([out] + parts, axis=0)
    return out


def target_cell(me, t, groups):
    return t * groups + lax.bitwise_xor(jnp.int32(t) if isinstance(t, int) else t, me)


def strided(phi, c, kinds):
    return phi[pl.ds(c, kinds, stride=PLANE), :]


def split(v):
    high = v.astype(jnp.bfloat16)
    return high, (v - high.astype(jnp.float32)).astype(jnp.bfloat16)


def dot_bf16(a, b):
    return lax.dot_general(a, b, (((1,), (1,)), ((), ())), preferred_element_type=jnp.float32)


def dot_split(v, w):
    vh, vl = split(v)
    wh, wl = split(w)
    rows = v.shape[0]
    both = dot_bf16(jnp.concatenate([vh, vl], axis=0), wh)
    return both[:rows] + both[rows:] + dot_bf16(vh, wl)


def charge_kernel(meta, cst, own, phi, out):
    z_low = meta[0].astype(jnp.float32) * cell_side
    groups = phi.shape[0]
    kinds = (phi.shape[1] - ROWS) // PLANE
    density = jnp.zeros((PLANE, LANES), jnp.float32)
    for g in range(groups):
        for j in range(kinds):
            v = phi[g, j * PLANE : (j + 1) * PLANE, :]
            density = density + v * v
    out[:PLANE, :] = density
    acc = jnp.zeros((LANES, LANES), jnp.float32)
    ones = jnp.ones((ROWS, LANES), jnp.float32)
    for c in range(PLANE):
        charge = own[c, 4:5, :] * (2.0 * out[c : c + 1, :])
        out[c : c + 1, :] = charge
        x, y, z = own[c, 0:1, :], own[c, 1:2, :], own[c, 2:3, :]
        low = (cell_side * (c % 4), cell_side * (c // 4), z_low)
        acc = acc + weights(cst, x, y, z, (0.0, 0.0, z_low), (1.0, 1.0, cell_side)) * charge
        moments = dot_nt(ones, weights(cst, x, y, z, low, (cell_side,) * 3) * charge)
        out[PLANE + c : PLANE + c + 1, :] = moments[0:1, :]
    out[2 * PLANE :, :] = dot_nt(ones, acc)


def live_planes(me, planes):
    below = jnp.maximum(me - 1, 0)
    return below, below + jnp.maximum(planes - 2 - me, 0)


def list_sources(me, cell, counts, near, far, planes, table, pts, src, put_near, put_far, put_none, multiple):
    window = 3 * PLANE
    base = (me - 1) * PLANE
    below, n_planes = live_planes(me, planes)
    low_half = lax.broadcasted_iota(jnp.int32, (1, LANES), 1) < HALF
    n_near, n_far = counts[cell, 0], counts[cell, 1]
    n_items = n_far + n_planes
    n_pairs = (n_items + 1) // 2

    def near_step(j, c):
        slot = near[cell, j] - base
        src[j] = pts[slot]
        put_near(j, slot)
        return c

    lax.fori_loop(0, n_near, near_step, 0)

    def item(j):
        j = jnp.minimum(j, n_items - 1)
        p = j - n_far
        level = jnp.where(p < below, p, p + (me + 2 - below))
        slot = far[cell, jnp.minimum(j, far.shape[1] - 1)] - base
        return jnp.where(j < n_far, slot, window + level)

    def far_step(j, c):
        first, second = item(2 * j), item(2 * j + 1)
        src[n_near + j] = jnp.where(low_half, table[first], table[second])
        put_far(n_near + j, first, second, 2 * j + 1 < n_items, low_half)
        return c

    lax.fori_loop(0, n_pairs, far_step, 0)
    n_blocks = n_near + n_pairs
    for u in range(multiple - 1):
        src[n_blocks + u] = jnp.zeros(src.shape[1:], jnp.float32)
        put_none(n_blocks + u)
    return n_blocks


def put_targets(pts, cell, tgt):
    for d in range(3):
        tgt[d] = jnp.broadcast_to(pts[PLANE + cell, d : d + 1, :], (LANES, LANES)).T


def square(tgt, src, slot, rows):
    dx = tgt[0, rows, :] - src[slot, 0:1, :]
    dy = tgt[1, rows, :] - src[slot, 1:2, :]
    dz = tgt[2, rows, :] - src[slot, 2:3, :]
    return (dx * dx + dy * dy) + (dz * dz + soften)


def hartree_kernel(unroll, meta, counts, near, far, cst, table, pts, phi, gathered, out, val, mom, tgt, src, srcv):
    planes = gathered.shape[0]
    groups = phi.shape[0]
    kinds = (phi.shape[1] - ROWS) // PLANE
    cells = PLANE // groups
    me, group = meta[0], meta[1]
    for k in range(3):
        there = lax.bitwise_xor(me, jnp.clip(me - 1 + k, 0, planes - 1))
        val[k * PLANE : (k + 1) * PLANE, 0, :] = gathered[there, :PLANE, :]
        mom[k * PLANE : (k + 1) * PLANE, 0, :] = gathered[there, PLANE : 2 * PLANE, :]

    def put_plane(g, c):
        mom[3 * PLANE + g] = gathered[lax.bitwise_xor(me, g), 2 * PLANE : 2 * PLANE + 1, :]
        return c

    lax.fori_loop(0, planes, put_plane, 0)

    def put_near(j, slot):
        srcv[j] = val[slot]

    def put_far(j, first, second, live, low_half):
        srcv[j] = jnp.where(low_half, mom[first], mom[second] * live.astype(jnp.float32))

    def put_none(j):
        srcv[j] = jnp.zeros((1, LANES), jnp.float32)

    z_low = me.astype(jnp.float32) * cell_side
    total = jnp.zeros((groups * kinds, LANES), jnp.float32)
    out[0] = jnp.zeros((ROWS, LANES), jnp.float32)
    for t in range(cells):
        cell = target_cell(group, t, groups)
        n_blocks = list_sources(
            me, cell, counts, near, far, planes, table, pts, src, put_near, put_far, put_none, unroll
        )
        put_targets(pts, cell, tgt)

        def step(k, acc):
            for u in range(unroll):
                slot = k * unroll + u
                acc = acc + lax.rsqrt(square(tgt, src, slot, slice(None))) * srcv[slot]
            return acc

        acc = lax.fori_loop(0, (n_blocks + unroll - 1) // unroll, step, jnp.zeros((LANES, LANES), jnp.float32))
        row = dot_nt(jnp.ones((ROWS, LANES), jnp.float32), acc)[0:1, :]
        out[0, t : t + 1, :] = row
        there = PLANE + cell
        scaled = pts[there, 4:5, :] * (pts[there, 3:4, :] + row)
        v = jnp.concatenate([strided(phi.at[k], cell, kinds) for k in range(groups)], axis=0) * scaled
        w = weights(
            cst, pts[there, 0:1, :], pts[there, 1:2, :], pts[there, 2:3, :], (0.0, 0.0, z_low), (1.0, 1.0, cell_side)
        )
        total = total + dot_split(v, w)
    for k in range(groups):
        out[1 + lax.bitwise_xor(group, k), :kinds, :] = total[k * kinds : (k + 1) * kinds, :]


def orbital_kernel(
    batch, meta, counts, near, far, levels, screening, cst, table, pts, phi, before, after, gathered,
    out, hartree, rate, slot_of, val, mom, tgt, src, srcv, dist, inv, even, odd, acc, total,
):
    planes = gathered.shape[0]
    groups, cells, kinds, _ = out.shape
    orbs = groups * kinds
    me, group = meta[0], meta[1]

    def clear(i, c):
        slot_of[i] = -1
        rate[i] = 0.0
        return c

    lax.fori_loop(0, screening.shape[0], clear, 0)
    for q in range(2 * batch):
        rate[screening.shape[0] + q] = 0.0
    lane = lax.broadcasted_iota(jnp.int32, (1, LANES), 1) % orbs

    def rank(i, carry):
        found, lane_slot = carry
        level = levels[i]
        known = slot_of[level]
        slot = jnp.where(known < 0, found, known)
        slot_of[level] = slot
        rate[slot] = screening[level] * (-log2e)
        return found + (known < 0).astype(jnp.int32), jnp.where(lane == i, slot, lane_slot)

    n_levels, lane_slot = lax.fori_loop(0, orbs, rank, (jnp.int32(0), jnp.zeros((1, LANES), jnp.int32)))
    n_batches = (n_levels + batch - 1) // batch

    for k in range(3):
        there = lax.bitwise_xor(me, jnp.clip(me - 1 + k, 0, planes - 1))
        field = (before, phi, after)[k]

        def prepare(c, carry):
            at = k * PLANE + c
            share = lax.rem(c, groups)
            owner = lax.bitwise_xor(lax.bitwise_xor(share, c // groups), group)
            potential = pts[at, 3:4, :] + gathered[there, owner, 0, pl.ds(c // groups, 1), :]
            scaled = pts[at, 4:5, :] * potential
            v = jnp.concatenate([strided(field.at[g], c, kinds) for g in range(groups)], axis=0) * scaled
            vh, vl = split(v)
            both = jnp.concatenate([vh, vl], axis=0)
            val[at] = both
            z_low = (me - 1 + k).astype(jnp.float32) * cell_side
            low = (*cell_low(c), z_low)
            wh, wl = split(weights(cst, pts[at, 0:1, :], pts[at, 1:2, :], pts[at, 2:3, :], low, (cell_side,) * 3))
            first = dot_bf16(both, wh)
            mh, ml = split(first[:orbs] + first[orbs:] + dot_bf16(vh, wl))
            mom[at] = jnp.concatenate([mh, ml], axis=0)
            return carry

        lax.fori_loop(0, PLANE, prepare, 0, unroll=4)

    def put_plane(g, c):
        there = lax.bitwise_xor(me, g)
        parts = []
        for k in range(groups):
            source = 1 + lax.bitwise_xor(group, k)
            parts.append(sum(gathered[there, z, source, :kinds, :] for z in range(groups)))
        mh, ml = split(jnp.concatenate(parts, axis=0))
        mom[3 * PLANE + g] = jnp.concatenate([mh, ml], axis=0)
        return c

    lax.fori_loop(0, planes, put_plane, 0)

    def put_near(j, slot):
        srcv[j] = val[slot]

    def put_far(j, first, second, live, low_half):
        srcv[j] = jnp.where(low_half, mom[first], jnp.where(live, mom[second], jnp.zeros_like(mom[second])))

    def put_none(j):
        srcv[j] = jnp.zeros(srcv.shape[1:], srcv.dtype)

    def make(ref, b, unit):
        rates = [rate[b * batch + q] for q in range(batch)]
        for half in range(2):
            for r in range(LANES // 16):
                rows = slice(16 * r, 16 * r + 16)
                d = dist[2 * unit + half, rows, :]
                i = inv[2 * unit + half, rows, :]
                for q in range(batch):
                    ref[q * LANES + 16 * r : q * LANES + 16 * r + 16, half * LANES : (half + 1) * LANES] = (
                        jnp.exp2(d * rates[q]) * i
                    ).astype(jnp.bfloat16)

    def consume(ref, unit):
        v = jnp.concatenate([srcv[2 * unit], srcv[2 * unit + 1]], axis=1)
        acc[...] = acc[...] + dot_bf16(ref[...], v)

    def per_cell(t, carry):
        cell = target_cell(group, t, groups)
        n_blocks = list_sources(me, cell, counts, near, far, planes, table, pts, src, put_near, put_far, put_none, 4)
        n_loops = (n_blocks + 3) // 4
        put_targets(pts, cell, tgt)

        def measure(c, x):
            sq = square(tgt, src, c, slice(None))
            i = lax.rsqrt(sq)
            inv[c] = i
            dist[c] = sq * i
            return x

        lax.fori_loop(0, 4 * n_loops, measure, 0)
        total[...] = jnp.zeros(total.shape, jnp.float32)
        make(even, 0, 0)

        def per_batch(b, x):
            acc[...] = jnp.zeros(acc.shape, jnp.float32)

            def step(i, y):
                make(odd, b, 2 * i + 1)
                consume(even, 2 * i)
                last = i + 1 == n_loops
                make(even, jnp.where(last, b + 1, b), jnp.where(last, 0, 2 * i + 2))
                consume(odd, 2 * i + 1)
                return y

            lax.fori_loop(0, n_loops, step, 0)
            add = total[...]
            for q in range(batch):
                mine = lane_slot[:, : 2 * orbs] == b * batch + q
                add = add + jnp.where(mine, acc[q * LANES : (q + 1) * LANES, :], 0.0)
            total[...] = add
            return x

        lax.fori_loop(0, n_batches, per_batch, 0)
        flipped = jnp.concatenate([total[...], jnp.zeros((LANES, LANES - 2 * orbs), jnp.float32)], axis=1).T
        rows = (flipped[:orbs] + flipped[orbs : 2 * orbs]) * green_scale
        for k in range(groups):
            out[k, t] = rows[k * kinds : (k + 1) * kinds]
        return carry

    lax.fori_loop(0, cells, per_cell, 0)
    for k in range(groups):
        for t in range(cells):
            cell = target_cell(lax.bitwise_xor(group, k), t, groups)
            hartree[pl.ds(cell, 1), :] = gathered[0, k, 0, t : t + 1, :]


def place_kernel(meta, *refs):
    parts, out, ordered = refs[:-2], refs[-2], refs[-1]
    for k, part in enumerate(parts):
        for t in range(part.shape[0]):
            ordered[target_cell(lax.bitwise_xor(meta[1], k), t, len(parts))] = part[t]
    for c in range(PLANE):
        out[:, c, :] = ordered[c]


def smem():
    return pl.BlockSpec(memory_space=pltpu.SMEM)


def vmem():
    return pl.BlockSpec(memory_space=pltpu.VMEM)


def call(kernel, name, out_shape, smems, args, scratch=()):
    return pl.pallas_call(
        kernel,
        out_shape=out_shape,
        in_specs=[smem()] * smems + [vmem()] * (len(args) - smems),
        out_specs=jax.tree.map(lambda _: vmem(), out_shape),
        scratch_shapes=scratch,
        compiler_params=pltpu.CompilerParams(vmem_limit_bytes=52 * 1024 * 1024),
        name=name,
    )(*args)


def body(orbitals, points, quad_weight, external, screening, level_index, near_cells, far_cells):
    kinds, cells, point_count = orbitals.shape
    planes, groups = lax.axis_size("space"), lax.axis_size("orb")
    orbs = kinds * groups
    window = 3 * PLANE
    share = cells // groups
    me, group = lax.axis_index("space"), lax.axis_index("orb")
    meta = jnp.stack([me, group]).astype(jnp.int32)
    f32, bf16 = jnp.float32, jnp.bfloat16

    marks = jnp.broadcast_to(level_index.astype(f32)[:, None], (kinds, LANES))
    phi = jnp.concatenate(
        [orbitals.reshape(kinds * cells, LANES), marks, jnp.zeros((ROWS - kinds, LANES), f32)], axis=0
    )
    phi = gather_xor(phi, "orb", True)
    weight = quad_weight * (cell_side**3 / point_count)
    own = jnp.concatenate(
        [jnp.transpose(points, (1, 0, 2)), external[:, None], weight[:, None], jnp.zeros((cells, 3, LANES), f32)], axis=1
    )
    ends = planes - 1
    up = [(i, i + 1) for i in range(ends)]
    down = [(i + 1, i) for i in range(ends)]
    pts = jnp.concatenate([lax.ppermute(own, "space", up), own, lax.ppermute(own, "space", down)], axis=0)
    cst = jnp.asarray(basis_rows())
    base_table = proxy_table(planes, window)
    shift = np.zeros(base_table.shape, np.float32)
    shift[:window, 2] = cell_side
    table = jnp.asarray(base_table) + jnp.asarray(shift) * (me - 1).astype(f32)
    counts = jnp.stack(
        [jnp.sum((near_cells >= 0).astype(jnp.int32), 1), jnp.sum((far_cells >= 0).astype(jnp.int32), 1)], axis=1
    )
    levels = phi[:, kinds * cells : kinds * cells + kinds, 0].reshape(orbs).astype(jnp.int32)

    charges = call(
        charge_kernel, "charge", jax.ShapeDtypeStruct((2 * cells + ROWS, LANES), f32), 1, (meta, cst, own, phi)
    )
    charges = gather_xor(charges, "space", False)
    before, after = lax.ppermute(phi, "space", up), lax.ppermute(phi, "space", down)

    unroll = 2
    blocks = near_cells.shape[1] + (far_cells.shape[1] + planes + 1) // 2 + 6
    shares = call(
        functools.partial(hartree_kernel, unroll),
        "hartree",
        jax.ShapeDtypeStruct((1 + groups, ROWS, LANES), f32),
        4,
        (meta, counts, near_cells, far_cells, cst, table, pts, phi, charges),
        [
            pltpu.VMEM((window, 1, LANES), f32),
            pltpu.VMEM((window + planes, 1, LANES), f32),
            pltpu.VMEM((3, LANES, LANES), f32),
            pltpu.VMEM((blocks, ROWS, LANES), f32),
            pltpu.VMEM((blocks, 1, LANES), f32),
        ],
    )
    gathered = gather_xor(gather_xor(shares, "orb", True), "space", False)

    batch = 4
    sent, hartree = call(
        functools.partial(orbital_kernel, batch),
        "orbitals",
        (jax.ShapeDtypeStruct((groups, share, kinds, LANES), f32), jax.ShapeDtypeStruct((cells, LANES), f32)),
        6,
        (meta, counts, near_cells, far_cells, levels, screening, cst, table, pts, phi, before, after, gathered),
        [
            pltpu.SMEM((screening.shape[0] + 2 * batch,), f32),
            pltpu.SMEM((screening.shape[0],), jnp.int32),
            pltpu.VMEM((window, 2 * orbs, LANES), bf16),
            pltpu.VMEM((window + planes, 2 * orbs, LANES), bf16),
            pltpu.VMEM((3, LANES, LANES), f32),
            pltpu.VMEM((blocks, ROWS, LANES), f32),
            pltpu.VMEM((blocks, 2 * orbs, LANES), bf16),
            pltpu.VMEM((blocks, LANES, LANES), f32),
            pltpu.VMEM((blocks, LANES, LANES), f32),
            pltpu.VMEM((batch * LANES, 2 * LANES), bf16),
            pltpu.VMEM((batch * LANES, 2 * LANES), bf16),
            pltpu.VMEM((batch * LANES, 2 * orbs), f32),
            pltpu.VMEM((LANES, 2 * orbs), f32),
        ],
    )
    parts = [sent[0]]
    for k in range(1, groups):
        parts.append(lax.ppermute(sent[k], "orb", [(i, i ^ k) for i in range(groups)]))
    updated = call(
        place_kernel,
        "place",
        jax.ShapeDtypeStruct((kinds, cells, LANES), f32),
        1,
        (meta, *parts),
        [pltpu.VMEM((cells, kinds, LANES), f32)],
    )
    return updated, hartree


def solution(mesh):
    in_specs = (
        P("orb", "space", None),
        P(None, "space", None),
        P("space", None),
        P("space", None),
        P(),
        P("orb"),
        P("space", None),
        P("space", None),
    )
    out_specs = (P("orb", "space", None), P("space", None))
    return jax.shard_map(body, mesh=mesh, in_specs=in_specs, out_specs=out_specs, check_vma=False)
```

```python
import functools
import math

import jax
import jax.numpy as jnp
import numpy as np
from jax import lax
from jax.experimental import pallas as pl
from jax.experimental.pallas import tpu as pltpu
from jax.sharding import PartitionSpec as P

NODES = 4
LANES = 128
PLANE = 16
ROWS = 8
HALF = NODES**3

cell_side = 0.25
soften = 6.25e-06
green_scale = -0.5 / math.pi
log2e = math.log2(math.e)
highest = lax.Precision.HIGHEST

node_set = np.cos((2.0 * np.arange(NODES) + 1.0) * (math.pi / (2.0 * NODES)))
roots = [[node_set[m] for m in range(NODES) if m != a] for a in range(NODES)]
scales = [1.0 / np.prod([node_set[a] - r for r in roots[a]]) for a in range(NODES)]


def basis_rows():
    row = np.arange(ROWS)
    out = []
    for pick in (row // 4, 2 + row // 4, row % 4):
        for k in range(NODES - 1):
            out.append([roots[a][k] for a in pick])
        out.append([scales[a] for a in pick])
    return np.broadcast_to(np.array(out, np.float32)[:, :, None], (12, ROWS, LANES)).copy()


def proxy_table(planes, window):
    offset = 0.5 * (node_set + 1.0)
    p = np.arange(LANES) % HALF
    offs = np.stack([offset[p // 16], offset[p // 4 % 4], offset[p % 4]])
    cells = np.arange(window)
    lows = np.stack([cells % 4, cells // 4 % 4, cells // 16]) * cell_side
    near = lows[:, :, None] + offs[:, None, :] * cell_side
    levels = np.arange(planes)
    lows = np.stack([0 * levels, 0 * levels, levels]) * cell_side
    far = lows[:, :, None] + offs[:, None, :] * np.array([1.0, 1.0, cell_side])[:, None, None]
    table = np.zeros((window + planes, ROWS, LANES), np.float32)
    table[:, :3] = np.moveaxis(np.concatenate([near, far], 1), 0, 1)
    return table


def poly(u, r0, r1, r2, scale):
    return ((u - r0) * (u - r1)) * ((u - r2) * scale)


def weights(cst, x, y, z, lows, sides):
    ux, uy, uz = (
        jnp.broadcast_to(2.0 * (c - lo) / e - 1.0, (ROWS, LANES)) for c, lo, e in zip((x, y, z), lows, sides)
    )
    pz = poly(uz, cst[8], cst[9], cst[10], cst[11])
    pyz = [poly(uy, cst[4 * k], cst[4 * k + 1], cst[4 * k + 2], cst[4 * k + 3]) * pz for k in range(2)]
    parts = []
    for a in range(NODES):
        px = poly(ux, *(float(r) for r in roots[a]), float(scales[a]))
        parts += [px * pyz[0], px * pyz[1]]
    return jnp.concatenate(parts, axis=0)


def twice(w):
    return jnp.concatenate([w, w], axis=0)


def cell_low(cell):
    return [(cell % 4).astype(jnp.float32) * cell_side, (cell // 4 % 4).astype(jnp.float32) * cell_side]


def dot_nt(a, b):
    return lax.dot_general(a, b, (((1,), (1,)), ((), ())), precision=highest, preferred_element_type=jnp.float32)


def gather_xor(block, axis, pairs):
    count = lax.axis_size(axis)
    out = block[None]
    while out.shape[0] < count:
        have = out.shape[0]
        steps = range(1, 4 if (have > 1 or pairs) and have * 4 <= count else 2)
        parts = [lax.ppermute(out, axis, [(i, i ^ (have * j)) for i in range(count)]) for j in steps]
        out = jnp.concatenate([out] + parts, axis=0)
    return out


def target_cell(me, t, groups):
    return t * groups + lax.bitwise_xor(jnp.int32(t) if isinstance(t, int) else t, me)


def strided(phi, c, kinds):
    return phi[pl.ds(c, kinds, stride=PLANE), :]


def split(v):
    high = v.astype(jnp.bfloat16)
    return high, (v - high.astype(jnp.float32)).astype(jnp.bfloat16)


def dot_bf16(a, b):
    return lax.dot_general(a, b, (((1,), (1,)), ((), ())), preferred_element_type=jnp.float32)


def dot_split(v, w):
    vh, vl = split(v)
    wh, wl = split(w)
    rows = v.shape[0]
    both = dot_bf16(jnp.concatenate([vh, vl], axis=0), wh)
    return both[:rows] + both[rows:] + dot_bf16(vh, wl)


def charge_kernel(meta, cst, own, phi, out):
    z_low = meta[0].astype(jnp.float32) * cell_side
    groups = phi.shape[0]
    kinds = (phi.shape[1] - ROWS) // PLANE
    density = jnp.zeros((PLANE, LANES), jnp.float32)
    for g in range(groups):
        for j in range(kinds):
            v = phi[g, j * PLANE : (j + 1) * PLANE, :]
            density = density + v * v
    out[:PLANE, :] = density
    acc = jnp.zeros((HALF, LANES), jnp.float32)
    ones = jnp.ones((ROWS, LANES), jnp.float32)
    for c in range(PLANE):
        charge = own[c, 4:5, :] * (2.0 * out[c : c + 1, :])
        out[c : c + 1, :] = charge
        x, y, z = own[c, 0:1, :], own[c, 1:2, :], own[c, 2:3, :]
        low = (cell_side * (c % 4), cell_side * (c // 4), z_low)
        acc = acc + weights(cst, x, y, z, (0.0, 0.0, z_low), (1.0, 1.0, cell_side)) * charge
        moments = dot_nt(ones, twice(weights(cst, x, y, z, low, (cell_side,) * 3) * charge))
        out[PLANE + c : PLANE + c + 1, :] = moments[0:1, :]
    out[2 * PLANE :, :] = dot_nt(ones, twice(acc))


def live_planes(me, planes):
    below = jnp.maximum(me - 1, 0)
    return below, below + jnp.maximum(planes - 2 - me, 0)


def list_sources(me, cell, counts, near, far, planes, table, pts, src, put_near, put_far, put_none, multiple):
    window = 3 * PLANE
    base = (me - 1) * PLANE
    below, n_planes = live_planes(me, planes)
    low_half = lax.broadcasted_iota(jnp.int32, (1, LANES), 1) < HALF
    n_near, n_far = counts[cell, 0], counts[cell, 1]
    n_items = n_far + n_planes
    n_pairs = (n_items + 1) // 2

    def near_step(j, c):
        slot = near[cell, j] - base
        src[j] = pts[slot]
        put_near(j, slot)
        return c

    lax.fori_loop(0, n_near, near_step, 0)

    def item(j):
        j = jnp.minimum(j, n_items - 1)
        p = j - n_far
        level = jnp.where(p < below, p, p + (me + 2 - below))
        slot = far[cell, jnp.minimum(j, far.shape[1] - 1)] - base
        return jnp.where(j < n_far, slot, window + level)

    def far_step(j, c):
        first, second = item(2 * j), item(2 * j + 1)
        src[n_near + j] = jnp.where(low_half, table[first], table[second])
        put_far(n_near + j, first, second, 2 * j + 1 < n_items, low_half)
        return c

    lax.fori_loop(0, n_pairs, far_step, 0)
    n_blocks = n_near + n_pairs
    for u in range(multiple - 1):
        src[n_blocks + u] = jnp.zeros(src.shape[1:], jnp.float32)
        put_none(n_blocks + u)
    return n_blocks


def put_targets(pts, cell, tgt):
    for d in range(3):
        tgt[d] = jnp.broadcast_to(pts[PLANE + cell, d : d + 1, :], (LANES, LANES)).T


def square(tgt, src, slot, rows):
    dx = tgt[0, rows, :] - src[slot, 0:1, :]
    dy = tgt[1, rows, :] - src[slot, 1:2, :]
    dz = tgt[2, rows, :] - src[slot, 2:3, :]
    return (dx * dx + dy * dy) + (dz * dz + soften)


def hartree_kernel(unroll, meta, counts, near, far, cst, table, pts, phi, gathered, out, val, mom, tgt, src, srcv):
    planes = gathered.shape[0]
    groups = phi.shape[0]
    kinds = (phi.shape[1] - ROWS) // PLANE
    cells = PLANE // groups
    me, group = meta[0], meta[1]
    for k in range(3):
        there = lax.bitwise_xor(me, jnp.clip(me - 1 + k, 0, planes - 1))
        val[k * PLANE : (k + 1) * PLANE, 0, :] = gathered[there, :PLANE, :]
        mom[k * PLANE : (k + 1) * PLANE, 0, :] = gathered[there, PLANE : 2 * PLANE, :]

    def put_plane(g, c):
        mom[3 * PLANE + g] = gathered[lax.bitwise_xor(me, g), 2 * PLANE : 2 * PLANE + 1, :]
        return c

    lax.fori_loop(0, planes, put_plane, 0)

    def put_near(j, slot):
        srcv[j] = val[slot]

    def put_far(j, first, second, live, low_half):
        srcv[j] = jnp.where(low_half, mom[first], mom[second] * live.astype(jnp.float32))

    def put_none(j):
        srcv[j] = jnp.zeros((1, LANES), jnp.float32)

    z_low = me.astype(jnp.float32) * cell_side
    total = jnp.zeros((groups * kinds, LANES), jnp.float32)
    out[0] = jnp.zeros((ROWS, LANES), jnp.float32)
    for t in range(cells):
        cell = target_cell(group, t, groups)
        n_blocks = list_sources(
            me, cell, counts, near, far, planes, table, pts, src, put_near, put_far, put_none, unroll
        )
        put_targets(pts, cell, tgt)

        def step(k, acc):
            for u in range(unroll):
                slot = k * unroll + u
                acc = acc + lax.rsqrt(square(tgt, src, slot, slice(None))) * srcv[slot]
            return acc

        acc = lax.fori_loop(0, (n_blocks + unroll - 1) // unroll, step, jnp.zeros((LANES, LANES), jnp.float32))
        row = dot_nt(jnp.ones((ROWS, LANES), jnp.float32), acc)[0:1, :]
        out[0, t : t + 1, :] = row
        there = PLANE + cell
        scaled = pts[there, 4:5, :] * (pts[there, 3:4, :] + row)
        v = jnp.concatenate([strided(phi.at[k], cell, kinds) for k in range(groups)], axis=0) * scaled
        w = weights(
            cst, pts[there, 0:1, :], pts[there, 1:2, :], pts[there, 2:3, :], (0.0, 0.0, z_low), (1.0, 1.0, cell_side)
        )
        total = total + dot_split(v, twice(w))
    for k in range(groups):
        out[1 + lax.bitwise_xor(group, k), :kinds, :] = total[k * kinds : (k + 1) * kinds, :]


def orbital_kernel(
    batch, unit, steps, meta, counts, near, far, levels, screening, cst, table, pts, phi, before, after, gathered,
    out, hartree, rate, slot_of, val, mom, tgt, src, srcv, dist, inv, acc, total,
):
    planes = gathered.shape[0]
    groups, cells, kinds, _ = out.shape
    orbs = groups * kinds
    me, group = meta[0], meta[1]

    def clear(i, c):
        slot_of[i] = -1
        rate[i] = 0.0
        return c

    lax.fori_loop(0, screening.shape[0], clear, 0)
    for q in range(2 * batch):
        rate[screening.shape[0] + q] = 0.0
    lane = lax.broadcasted_iota(jnp.int32, (1, LANES), 1) % orbs

    def rank(i, carry):
        found, lane_slot = carry
        level = levels[i]
        known = slot_of[level]
        slot = jnp.where(known < 0, found, known)
        slot_of[level] = slot
        rate[slot] = screening[level] * (-log2e)
        return found + (known < 0).astype(jnp.int32), jnp.where(lane == i, slot, lane_slot)

    n_levels, lane_slot = lax.fori_loop(0, orbs, rank, (jnp.int32(0), jnp.zeros((1, LANES), jnp.int32)))
    n_batches = (n_levels + batch - 1) // batch

    first_half = lax.broadcasted_iota(jnp.int32, (1, 2 * orbs), 1) < orbs

    def flip(v):
        high = v.astype(jnp.bfloat16).astype(jnp.float32)
        square = jnp.concatenate([high, v - high, jnp.zeros((LANES - 2 * orbs, LANES), jnp.float32)], axis=0)
        return square.T[:, : 2 * orbs].astype(jnp.bfloat16)

    for k in range(3):
        there = lax.bitwise_xor(me, jnp.clip(me - 1 + k, 0, planes - 1))
        field = (before, phi, after)[k]

        def prepare(c, carry):
            at = k * PLANE + c
            share = lax.rem(c, groups)
            owner = lax.bitwise_xor(lax.bitwise_xor(share, c // groups), group)
            potential = pts[at, 3:4, :] + gathered[there, owner, 0, pl.ds(c // groups, 1), :]
            scaled = pts[at, 4:5, :] * potential
            v = jnp.concatenate([strided(field.at[g], c, kinds) for g in range(groups)], axis=0) * scaled
            val[at] = flip(v)
            vh, vl = split(v)
            z_low = (me - 1 + k).astype(jnp.float32) * cell_side
            low = (*cell_low(c), z_low)
            wh, wl = split(weights(cst, pts[at, 0:1, :], pts[at, 1:2, :], pts[at, 2:3, :], low, (cell_side,) * 3))
            all_of = dot_bf16(jnp.concatenate([wh, wl], axis=0), jnp.concatenate([vh, vh, vl, vl], axis=0))
            m = all_of[:HALF] + all_of[HALF:]
            m = m[:, : 2 * orbs] + pltpu.roll(all_of[:HALF], 4 * orbs - 2 * orbs, 1)[:, : 2 * orbs]
            high = m.astype(jnp.bfloat16).astype(jnp.float32)
            mom[at] = jnp.where(first_half, high, m - high).astype(jnp.bfloat16)
            return carry

        lax.fori_loop(0, PLANE, prepare, 0, unroll=4)

    def put_plane(g, c):
        there = lax.bitwise_xor(me, g)
        parts = []
        for k in range(groups):
            source = 1 + lax.bitwise_xor(group, k)
            parts.append(sum(gathered[there, z, source, :kinds, :] for z in range(groups)))
        mom[3 * PLANE + g] = flip(jnp.concatenate(parts, axis=0))[:HALF]
        return c

    lax.fori_loop(0, planes, put_plane, 0)

    def put_near(j, slot):
        srcv[j] = val[slot]

    def put_far(j, first, second, live, low_half):
        srcv[j, :HALF, :] = mom[first]
        srcv[j, HALF:, :] = jnp.where(live, mom[second], jnp.zeros_like(mom[second]))

    def put_none(j):
        srcv[j] = jnp.zeros(srcv.shape[1:], srcv.dtype)

    def products(b, first):
        rates = [rate[b * batch + q] for q in range(batch)]
        rows = []
        for q in range(batch):
            tiles = [(jnp.exp2(dist[first + h] * rates[q]) * inv[first + h]).astype(jnp.bfloat16) for h in range(unit)]
            rows.append(jnp.concatenate(tiles, axis=1))
        v = jnp.concatenate([srcv[first + h] for h in range(unit)], axis=0)
        return jnp.dot(jnp.concatenate(rows, axis=0), v, preferred_element_type=jnp.float32)

    def per_cell(t, carry):
        cell = target_cell(group, t, groups)
        n_blocks = list_sources(me, cell, counts, near, far, planes, table, pts, src, put_near, put_far, put_none, unit)
        n_loops = (n_blocks + unit - 1) // unit
        put_targets(pts, cell, tgt)

        def measure(c, x):
            sq = square(tgt, src, c, slice(None))
            i = lax.rsqrt(sq)
            inv[c] = i
            dist[c] = sq * i
            return x

        lax.fori_loop(0, unit * n_loops, measure, 0)
        total[...] = jnp.zeros(total.shape, jnp.float32)

        def clear(b, x):
            acc[b] = jnp.zeros(acc.shape[1:], jnp.float32)
            return x

        lax.fori_loop(0, n_batches, clear, 0)

        def step(i, at):
            b, u = at
            for _ in range(steps):
                acc[b] = acc[b] + products(b, unit * u)
                wrap = u + 1 == n_loops
                b, u = jnp.where(wrap, b + 1, b), jnp.where(wrap, 0, u + 1)
            return b, u

        lax.fori_loop(0, (n_batches * n_loops + steps - 1) // steps, step, (jnp.int32(0), jnp.int32(0)))

        def choose(b, x):
            add = total[...]
            for q in range(batch):
                mine = lane_slot[:, : 2 * orbs] == b * batch + q
                add = add + jnp.where(mine, acc[b, q * LANES : (q + 1) * LANES, :], 0.0)
            total[...] = add
            return x

        lax.fori_loop(0, n_batches, choose, 0)
        flipped = jnp.concatenate([total[...], jnp.zeros((LANES, LANES - 2 * orbs), jnp.float32)], axis=1).T
        rows = (flipped[:orbs] + flipped[orbs : 2 * orbs]) * green_scale
        for k in range(groups):
            out[k, t] = rows[k * kinds : (k + 1) * kinds]
        return carry

    lax.fori_loop(0, cells, per_cell, 0)
    for k in range(groups):
        for t in range(cells):
            cell = target_cell(lax.bitwise_xor(group, k), t, groups)
            hartree[pl.ds(cell, 1), :] = gathered[0, k, 0, t : t + 1, :]


def place_kernel(meta, *refs):
    parts, out, ordered = refs[:-2], refs[-2], refs[-1]
    for k, part in enumerate(parts):
        for t in range(part.shape[0]):
            ordered[target_cell(lax.bitwise_xor(meta[1], k), t, len(parts))] = part[t]
    for c in range(PLANE):
        out[:, c, :] = ordered[c]


def smem():
    return pl.BlockSpec(memory_space=pltpu.SMEM)


def vmem():
    return pl.BlockSpec(memory_space=pltpu.VMEM)


def call(kernel, name, out_shape, smems, args, scratch=()):
    return pl.pallas_call(
        kernel,
        out_shape=out_shape,
        in_specs=[smem()] * smems + [vmem()] * (len(args) - smems),
        out_specs=jax.tree.map(lambda _: vmem(), out_shape),
        scratch_shapes=scratch,
        compiler_params=pltpu.CompilerParams(vmem_limit_bytes=52 * 1024 * 1024),
        name=name,
    )(*args)


def body(orbitals, points, quad_weight, external, screening, level_index, near_cells, far_cells):
    kinds, cells, point_count = orbitals.shape
    planes, groups = lax.axis_size("space"), lax.axis_size("orb")
    orbs = kinds * groups
    window = 3 * PLANE
    share = cells // groups
    me, group = lax.axis_index("space"), lax.axis_index("orb")
    meta = jnp.stack([me, group]).astype(jnp.int32)
    f32, bf16 = jnp.float32, jnp.bfloat16

    marks = jnp.broadcast_to(level_index.astype(f32)[:, None], (kinds, LANES))
    phi = jnp.concatenate(
        [orbitals.reshape(kinds * cells, LANES), marks, jnp.zeros((ROWS - kinds, LANES), f32)], axis=0
    )
    phi = gather_xor(phi, "orb", True)
    weight = quad_weight * (cell_side**3 / point_count)
    own = jnp.concatenate(
        [jnp.transpose(points, (1, 0, 2)), external[:, None], weight[:, None], jnp.zeros((cells, 3, LANES), f32)], axis=1
    )
    ends = planes - 1
    up = [(i, i + 1) for i in range(ends)]
    down = [(i + 1, i) for i in range(ends)]
    pts = jnp.concatenate([lax.ppermute(own, "space", up), own, lax.ppermute(own, "space", down)], axis=0)
    cst = jnp.asarray(basis_rows())
    base_table = proxy_table(planes, window)
    shift = np.zeros(base_table.shape, np.float32)
    shift[:window, 2] = cell_side
    table = jnp.asarray(base_table) + jnp.asarray(shift) * (me - 1).astype(f32)
    counts = jnp.stack(
        [jnp.sum((near_cells >= 0).astype(jnp.int32), 1), jnp.sum((far_cells >= 0).astype(jnp.int32), 1)], axis=1
    )
    levels = phi[:, kinds * cells : kinds * cells + kinds, 0].reshape(orbs).astype(jnp.int32)

    charges = call(
        charge_kernel, "charge", jax.ShapeDtypeStruct((2 * cells + ROWS, LANES), f32), 1, (meta, cst, own, phi)
    )
    charges = gather_xor(charges, "space", False)
    before, after = lax.ppermute(phi, "space", up), lax.ppermute(phi, "space", down)

    unroll = 2
    blocks = near_cells.shape[1] + (far_cells.shape[1] + planes + 1) // 2 + 8
    shares = call(
        functools.partial(hartree_kernel, unroll),
        "hartree",
        jax.ShapeDtypeStruct((1 + groups, ROWS, LANES), f32),
        4,
        (meta, counts, near_cells, far_cells, cst, table, pts, phi, charges),
        [
            pltpu.VMEM((window, 1, LANES), f32),
            pltpu.VMEM((window + planes, 1, LANES), f32),
            pltpu.VMEM((3, LANES, LANES), f32),
            pltpu.VMEM((blocks, ROWS, LANES), f32),
            pltpu.VMEM((blocks, 1, LANES), f32),
        ],
    )
    gathered = gather_xor(gather_xor(shares, "orb", True), "space", False)

    batch, unit, steps = 4, 6, 3
    levels_at_most = -(-screening.shape[0] // batch) + 1
    sent, hartree = call(
        functools.partial(orbital_kernel, batch, unit, steps),
        "orbitals",
        (jax.ShapeDtypeStruct((groups, share, kinds, LANES), f32), jax.ShapeDtypeStruct((cells, LANES), f32)),
        6,
        (meta, counts, near_cells, far_cells, levels, screening, cst, table, pts, phi, before, after, gathered),
        [
            pltpu.SMEM((screening.shape[0] + 2 * batch,), f32),
            pltpu.SMEM((screening.shape[0],), jnp.int32),
            pltpu.VMEM((window, LANES, 2 * orbs), bf16),
            pltpu.VMEM((window + planes, HALF, 2 * orbs), bf16),
            pltpu.VMEM((3, LANES, LANES), f32),
            pltpu.VMEM((blocks, ROWS, LANES), f32),
            pltpu.VMEM((blocks, LANES, 2 * orbs), bf16),
            pltpu.VMEM((blocks, LANES, LANES), f32),
            pltpu.VMEM((blocks, LANES, LANES), f32),
            pltpu.VMEM((levels_at_most, batch * LANES, 2 * orbs), f32),
            pltpu.VMEM((LANES, 2 * orbs), f32),
        ],
    )
    parts = [sent[0]]
    for k in range(1, groups):
        parts.append(lax.ppermute(sent[k], "orb", [(i, i ^ k) for i in range(groups)]))
    updated = call(
        place_kernel,
        "place",
        jax.ShapeDtypeStruct((kinds, cells, LANES), f32),
        1,
        (meta, *parts),
        [pltpu.VMEM((cells, kinds, LANES), f32)],
    )
    return updated, hartree


def solution(mesh):
    in_specs = (
        P("orb", "space", None),
        P(None, "space", None),
        P("space", None),
        P("space", None),
        P(),
        P("orb"),
        P("space", None),
        P("space", None),
    )
    out_specs = (P("orb", "space", None), P("space", None))
    return jax.shard_map(body, mesh=mesh, in_specs=in_specs, out_specs=out_specs, check_vma=False)
```

```python
import functools
import math

import jax
import jax.numpy as jnp
import numpy as np
from jax import lax
from jax.experimental import pallas as pl
from jax.experimental.pallas import tpu as pltpu
from jax.sharding import PartitionSpec as P

NODES = 4
LANES = 128
PLANE = 16
ROWS = 8
HALF = NODES**3

cell_side = 0.25
soften = 6.25e-06
green_scale = -0.5 / math.pi
log2e = math.log2(math.e)
highest = lax.Precision.HIGHEST

node_set = np.cos((2.0 * np.arange(NODES) + 1.0) * (math.pi / (2.0 * NODES)))
roots = [[node_set[m] for m in range(NODES) if m != a] for a in range(NODES)]
scales = [1.0 / np.prod([node_set[a] - r for r in roots[a]]) for a in range(NODES)]


def basis_rows():
    row = np.arange(ROWS)
    out = []
    for pick in (row // 4, 2 + row // 4, row % 4):
        for k in range(NODES - 1):
            out.append([roots[a][k] for a in pick])
        out.append([scales[a] for a in pick])
    return np.broadcast_to(np.array(out, np.float32)[:, :, None], (12, ROWS, LANES)).copy()


def proxy_table(planes, window):
    offset = 0.5 * (node_set + 1.0)
    p = np.arange(LANES) % HALF
    offs = np.stack([offset[p // 16], offset[p // 4 % 4], offset[p % 4]])
    cells = np.arange(window)
    lows = np.stack([cells % 4, cells // 4 % 4, cells // 16]) * cell_side
    near = lows[:, :, None] + offs[:, None, :] * cell_side
    levels = np.arange(planes)
    lows = np.stack([0 * levels, 0 * levels, levels]) * cell_side
    far = lows[:, :, None] + offs[:, None, :] * np.array([1.0, 1.0, cell_side])[:, None, None]
    table = np.zeros((window + planes, ROWS, LANES), np.float32)
    table[:, :3] = np.moveaxis(np.concatenate([near, far], 1), 0, 1)
    return table


def poly(u, r0, r1, r2, scale):
    return ((u - r0) * (u - r1)) * ((u - r2) * scale)


def weights(cst, x, y, z, lows, sides):
    ux, uy, uz = (
        jnp.broadcast_to(2.0 * (c - lo) / e - 1.0, (ROWS, LANES)) for c, lo, e in zip((x, y, z), lows, sides)
    )
    pz = poly(uz, cst[8], cst[9], cst[10], cst[11])
    pyz = [poly(uy, cst[4 * k], cst[4 * k + 1], cst[4 * k + 2], cst[4 * k + 3]) * pz for k in range(2)]
    parts = []
    for a in range(NODES):
        px = poly(ux, *(float(r) for r in roots[a]), float(scales[a]))
        parts += [px * pyz[0], px * pyz[1]]
    return jnp.concatenate(parts, axis=0)


def twice(w):
    return jnp.concatenate([w, w], axis=0)


def cell_low(cell):
    return [(cell % 4).astype(jnp.float32) * cell_side, (cell // 4 % 4).astype(jnp.float32) * cell_side]


def dot_nt(a, b):
    return lax.dot_general(a, b, (((1,), (1,)), ((), ())), precision=highest, preferred_element_type=jnp.float32)


def gather_parts(block, axis, pairs):
    count = lax.axis_size(axis)
    parts = [block[None]]
    while sum(p.shape[0] for p in parts) < count:
        held = parts[0] if len(parts) == 1 else jnp.concatenate(parts, axis=0)
        have = held.shape[0]
        steps = range(1, 4 if (have > 1 or pairs) and have * 4 <= count else 2)
        parts = [held] + [lax.ppermute(held, axis, [(i, i ^ (have * j)) for i in range(count)]) for j in steps]
    return parts


def gather_list(block, axis):
    parts = gather_parts(block, axis, True)
    return [p[k] for p in parts for k in range(p.shape[0])]


def lay_out(parts, whole):
    at = 0
    for part in parts:
        for k in range(part.shape[0]):
            whole[at + k] = part[k]
        at += part.shape[0]


def target_cell(me, t, groups):
    return t * groups + lax.bitwise_xor(jnp.int32(t) if isinstance(t, int) else t, me)


def split(v):
    high = v.astype(jnp.bfloat16)
    return high, (v - high.astype(jnp.float32)).astype(jnp.bfloat16)


def dot_bf16(a, b):
    return lax.dot_general(a, b, (((1,), (1,)), ((), ())), preferred_element_type=jnp.float32)


def dot_split(v, w):
    vh, vl = split(v)
    wh, wl = split(w)
    rows = v.shape[0]
    both = dot_bf16(jnp.concatenate([vh, vl], axis=0), wh)
    return both[:rows] + both[rows:] + dot_bf16(vh, wl)


def charge_kernel(meta, cst, own, *refs):
    z_low = meta[0].astype(jnp.float32) * cell_side
    fields, out = refs[:-1], refs[-1]
    density = jnp.zeros((PLANE, LANES), jnp.float32)
    for phi in fields:
        for j in range(phi.shape[0]):
            v = phi[j]
            density = density + v * v
    out[:PLANE, :] = density
    acc = jnp.zeros((HALF, LANES), jnp.float32)
    ones = jnp.ones((ROWS, LANES), jnp.float32)
    for c in range(PLANE):
        charge = own[c, 4:5, :] * (2.0 * out[c : c + 1, :])
        out[c : c + 1, :] = charge
        x, y, z = own[c, 0:1, :], own[c, 1:2, :], own[c, 2:3, :]
        low = (cell_side * (c % 4), cell_side * (c // 4), z_low)
        acc = acc + weights(cst, x, y, z, (0.0, 0.0, z_low), (1.0, 1.0, cell_side)) * charge
        moments = dot_nt(ones, twice(weights(cst, x, y, z, low, (cell_side,) * 3) * charge))
        out[PLANE + c : PLANE + c + 1, :] = moments[0:1, :]
    out[2 * PLANE :, :] = dot_nt(ones, twice(acc))


def live_planes(me, planes):
    below = jnp.maximum(me - 1, 0)
    return below, below + jnp.maximum(planes - 2 - me, 0)


def list_sources(me, cell, counts, near, far, planes, table, pts, src, put_near, put_far, put_none, multiple):
    window = 3 * PLANE
    base = (me - 1) * PLANE
    below, n_planes = live_planes(me, planes)
    low_half = lax.broadcasted_iota(jnp.int32, (1, LANES), 1) < HALF
    n_near, n_far = counts[cell, 0], counts[cell, 1]
    n_items = n_far + n_planes
    n_pairs = (n_items + 1) // 2

    def near_step(j, c):
        slot = near[cell, j] - base
        src[j] = pts[slot]
        put_near(j, slot)
        return c

    lax.fori_loop(0, n_near, near_step, 0)

    def item(j):
        j = jnp.minimum(j, n_items - 1)
        p = j - n_far
        level = jnp.where(p < below, p, p + (me + 2 - below))
        slot = far[cell, jnp.minimum(j, far.shape[1] - 1)] - base
        return jnp.where(j < n_far, slot, window + level)

    def far_step(j, c):
        first, second = item(2 * j), item(2 * j + 1)
        src[n_near + j] = jnp.where(low_half, table[first], table[second])
        put_far(n_near + j, first, second, 2 * j + 1 < n_items, low_half)
        return c

    lax.fori_loop(0, n_pairs, far_step, 0)
    n_blocks = n_near + n_pairs
    for u in range(multiple - 1):
        src[n_blocks + u] = jnp.zeros(src.shape[1:], jnp.float32)
        put_none(n_blocks + u)
    return n_blocks


def put_targets(pts, cell, tgt):
    for d in range(3):
        tgt[d] = jnp.broadcast_to(pts[PLANE + cell, d : d + 1, :], (LANES, LANES)).T


def square(tgt, src, slot, rows):
    dx = tgt[0, rows, :] - src[slot, 0:1, :]
    dy = tgt[1, rows, :] - src[slot, 1:2, :]
    dz = tgt[2, rows, :] - src[slot, 2:3, :]
    return (dx * dx + dy * dy) + (dz * dz + soften)


def put_points(messages, pts):
    for k, message in enumerate(messages):
        top = message.shape[0] - PLANE * ROWS
        for c in range(PLANE):
            pts[k * PLANE + c] = message[top + c * ROWS : top + (c + 1) * ROWS, :]


def cell_fields(message, c, groups, kinds):
    rows = kinds * PLANE
    return jnp.concatenate(
        [message[pl.ds(g * rows + c, kinds, stride=PLANE), :] for g in range(groups)], axis=0
    )


def hartree_kernel(unroll, groups, kinds, meta, counts, near, far, cst, table, marks, before, mine, after, *refs):
    parts, (out, every, pts, val, mom, tgt, src, srcv) = refs[:-8], refs[-8:]
    lay_out(parts, every)
    put_points((before, mine, after), pts)
    planes = every.shape[0]
    cells = PLANE // groups
    me, group = meta[0], meta[1]
    for k in range(3):
        there = lax.bitwise_xor(me, jnp.clip(me - 1 + k, 0, planes - 1))
        val[k * PLANE : (k + 1) * PLANE, 0, :] = every[there, :PLANE, :]
        mom[k * PLANE : (k + 1) * PLANE, 0, :] = every[there, PLANE : 2 * PLANE, :]

    def put_plane(g, c):
        mom[3 * PLANE + g] = every[lax.bitwise_xor(me, g), 2 * PLANE : 2 * PLANE + 1, :]
        return c

    lax.fori_loop(0, planes, put_plane, 0)

    def put_near(j, slot):
        srcv[j] = val[slot]

    def put_far(j, first, second, live, low_half):
        srcv[j] = jnp.where(low_half, mom[first], mom[second] * live.astype(jnp.float32))

    def put_none(j):
        srcv[j] = jnp.zeros((1, LANES), jnp.float32)

    z_low = me.astype(jnp.float32) * cell_side
    total = jnp.zeros((groups * kinds, LANES), jnp.float32)
    out[0] = jnp.broadcast_to(marks[...], (ROWS, LANES))
    for t in range(cells):
        cell = target_cell(group, t, groups)
        n_blocks = list_sources(
            me, cell, counts, near, far, planes, table, pts, src, put_near, put_far, put_none, unroll
        )
        put_targets(pts, cell, tgt)

        def step(k, acc):
            for u in range(unroll):
                slot = k * unroll + u
                acc = acc + lax.rsqrt(square(tgt, src, slot, slice(None))) * srcv[slot]
            return acc

        acc = lax.fori_loop(0, (n_blocks + unroll - 1) // unroll, step, jnp.zeros((LANES, LANES), jnp.float32))
        row = dot_nt(jnp.ones((ROWS, LANES), jnp.float32), acc)[0:1, :]
        out[0, t : t + 1, :] = row
        there = PLANE + cell
        scaled = pts[there, 4:5, :] * (pts[there, 3:4, :] + row)
        v = cell_fields(mine, cell, groups, kinds) * scaled
        w = weights(
            cst, pts[there, 0:1, :], pts[there, 1:2, :], pts[there, 2:3, :], (0.0, 0.0, z_low), (1.0, 1.0, cell_side)
        )
        total = total + dot_split(v, twice(w))
    for k in range(groups):
        out[1 + lax.bitwise_xor(group, k), :kinds, :] = total[k * kinds : (k + 1) * kinds, :]


def combine_kernel(kinds, meta, *refs):
    shares, (hartree, out, total) = refs[:-3], refs[-3:]
    groups = len(shares)
    for k, share in enumerate(shares):
        for t in range(PLANE // groups):
            cell = target_cell(lax.bitwise_xor(meta[1], k), t, groups)
            out[pl.ds(cell, 1), :] = share[0, t : t + 1, :]
    hartree[...] = out[:PLANE, :]
    for g in range(groups):
        added = shares[0][1 + g, :kinds, :]
        for share in shares[1:]:
            added = added + share[1 + g, :kinds, :]
        total[g * kinds : (g + 1) * kinds, :] = added
    rows = groups * kinds // 2
    low_half = lax.broadcasted_iota(jnp.int32, (1, LANES), 1) < HALF
    out[PLANE:, :] = jnp.where(low_half, total[:rows, :], total[rows:, :])


def orbital_kernel(
    batch, unit, steps, meta, counts, near, far, levels, screening, cst, table, before, mine, after, *refs
):
    parts, refs = refs[:-14], refs[-14:]
    out, rate, slot_of, every, pts, val, mom, tgt, src, srcv, dist, inv, acc, total = refs
    lay_out(parts, every)
    put_points((before, mine, after), pts)
    planes = every.shape[0]
    groups, cells, kinds, _ = out.shape
    orbs = groups * kinds
    me, group = meta[0], meta[1]

    def clear(i, c):
        slot_of[i] = -1
        rate[i] = 0.0
        return c

    lax.fori_loop(0, screening.shape[0], clear, 0)
    for q in range(2 * batch):
        rate[screening.shape[0] + q] = 0.0
    lane = lax.broadcasted_iota(jnp.int32, (1, LANES), 1) % orbs

    def rank(i, carry):
        found, lane_slot = carry
        level = levels[i]
        known = slot_of[level]
        slot = jnp.where(known < 0, found, known)
        slot_of[level] = slot
        rate[slot] = screening[level] * (-log2e)
        return found + (known < 0).astype(jnp.int32), jnp.where(lane == i, slot, lane_slot)

    n_levels, lane_slot = lax.fori_loop(0, orbs, rank, (jnp.int32(0), jnp.zeros((1, LANES), jnp.int32)))
    n_batches = (n_levels + batch - 1) // batch

    first_half = lax.broadcasted_iota(jnp.int32, (1, 2 * orbs), 1) < orbs

    def flip(v):
        high = v.astype(jnp.bfloat16).astype(jnp.float32)
        square = jnp.concatenate([high, v - high, jnp.zeros((LANES - 2 * orbs, LANES), jnp.float32)], axis=0)
        return square.T[:, : 2 * orbs].astype(jnp.bfloat16)

    for k in range(3):
        there = lax.bitwise_xor(me, jnp.clip(me - 1 + k, 0, planes - 1))
        message = (before, mine, after)[k]

        def prepare(c, carry):
            at = k * PLANE + c
            scaled = pts[at, 4:5, :] * (pts[at, 3:4, :] + every[there, pl.ds(c, 1), :])
            v = cell_fields(message, c, groups, kinds) * scaled
            val[at] = flip(v)
            vh, vl = split(v)
            z_low = (me - 1 + k).astype(jnp.float32) * cell_side
            low = (*cell_low(c), z_low)
            wh, wl = split(weights(cst, pts[at, 0:1, :], pts[at, 1:2, :], pts[at, 2:3, :], low, (cell_side,) * 3))
            all_of = dot_bf16(jnp.concatenate([wh, wl], axis=0), jnp.concatenate([vh, vh, vl, vl], axis=0))
            m = all_of[:HALF] + all_of[HALF:]
            m = m[:, : 2 * orbs] + pltpu.roll(all_of[:HALF], 4 * orbs - 2 * orbs, 1)[:, : 2 * orbs]
            high = m.astype(jnp.bfloat16).astype(jnp.float32)
            mom[at] = jnp.where(first_half, high, m - high).astype(jnp.bfloat16)
            return carry

        lax.fori_loop(0, PLANE, prepare, 0, unroll=4)

    def put_plane(g, c):
        there = lax.bitwise_xor(me, g)
        rows = []
        for k in range(groups):
            row = lax.bitwise_xor(group, k) * kinds
            v = every[there, pl.ds(PLANE + lax.rem(row, orbs // 2), kinds), :]
            rows.append(jnp.where(row < orbs // 2, v, pltpu.roll(v, HALF, 1)))
        mom[3 * PLANE + g] = flip(jnp.concatenate(rows, axis=0))[:HALF]
        return c

    lax.fori_loop(0, planes, put_plane, 0)

    def put_near(j, slot):
        srcv[j] = val[slot]

    def put_far(j, first, second, live, low_half):
        srcv[j, :HALF, :] = mom[first]
        srcv[j, HALF:, :] = jnp.where(live, mom[second], jnp.zeros_like(mom[second]))

    def put_none(j):
        srcv[j] = jnp.zeros(srcv.shape[1:], srcv.dtype)

    def products(b, first):
        rates = [rate[b * batch + q] for q in range(batch)]
        rows = []
        for q in range(batch):
            tiles = [(jnp.exp2(dist[first + h] * rates[q]) * inv[first + h]).astype(jnp.bfloat16) for h in range(unit)]
            rows.append(jnp.concatenate(tiles, axis=1))
        v = jnp.concatenate([srcv[first + h] for h in range(unit)], axis=0)
        return jnp.dot(jnp.concatenate(rows, axis=0), v, preferred_element_type=jnp.float32)

    def per_cell(t, carry):
        cell = target_cell(group, t, groups)
        n_blocks = list_sources(me, cell, counts, near, far, planes, table, pts, src, put_near, put_far, put_none, unit)
        n_loops = (n_blocks + unit - 1) // unit
        put_targets(pts, cell, tgt)

        def measure(c, x):
            sq = square(tgt, src, c, slice(None))
            i = lax.rsqrt(sq)
            inv[c] = i
            dist[c] = sq * i
            return x

        lax.fori_loop(0, unit * n_loops, measure, 0)
        total[...] = jnp.zeros(total.shape, jnp.float32)

        def clear(b, x):
            acc[b] = jnp.zeros(acc.shape[1:], jnp.float32)
            return x

        lax.fori_loop(0, n_batches, clear, 0)

        def step(i, at):
            b, u = at
            for _ in range(steps):
                acc[b] = acc[b] + products(b, unit * u)
                wrap = u + 1 == n_loops
                b, u = jnp.where(wrap, b + 1, b), jnp.where(wrap, 0, u + 1)
            return b, u

        lax.fori_loop(0, (n_batches * n_loops + steps - 1) // steps, step, (jnp.int32(0), jnp.int32(0)))

        def choose(b, x):
            add = total[...]
            for q in range(batch):
                mine = lane_slot[:, : 2 * orbs] == b * batch + q
                add = add + jnp.where(mine, acc[b, q * LANES : (q + 1) * LANES, :], 0.0)
            total[...] = add
            return x

        lax.fori_loop(0, n_batches, choose, 0)
        flipped = jnp.concatenate([total[...], jnp.zeros((LANES, LANES - 2 * orbs), jnp.float32)], axis=1).T
        rows = (flipped[:orbs] + flipped[orbs : 2 * orbs]) * green_scale
        for k in range(groups):
            out[k, t] = rows[k * kinds : (k + 1) * kinds]
        return carry

    lax.fori_loop(0, cells, per_cell, 0)


def place_kernel(meta, *refs):
    parts, out, ordered = refs[:-2], refs[-2], refs[-1]
    for k, part in enumerate(parts):
        for t in range(part.shape[0]):
            ordered[target_cell(lax.bitwise_xor(meta[1], k), t, len(parts))] = part[t]
    for c in range(PLANE):
        out[:, c, :] = ordered[c]


def smem():
    return pl.BlockSpec(memory_space=pltpu.SMEM)


def vmem():
    return pl.BlockSpec(memory_space=pltpu.VMEM)


def call(kernel, name, out_shape, smems, args, scratch=()):
    return pl.pallas_call(
        kernel,
        out_shape=out_shape,
        in_specs=[smem()] * smems + [vmem()] * (len(args) - smems),
        out_specs=jax.tree.map(lambda _: vmem(), out_shape),
        scratch_shapes=scratch,
        compiler_params=pltpu.CompilerParams(vmem_limit_bytes=52 * 1024 * 1024),
        name=name,
    )(*args)


def body(orbitals, points, quad_weight, external, screening, level_index, near_cells, far_cells):
    kinds, cells, point_count = orbitals.shape
    planes, groups = lax.axis_size("space"), lax.axis_size("orb")
    orbs = kinds * groups
    window = 3 * PLANE
    share = cells // groups
    me, group = lax.axis_index("space"), lax.axis_index("orb")
    meta = jnp.stack([me, group]).astype(jnp.int32)
    f32, bf16 = jnp.float32, jnp.bfloat16

    fields = gather_list(orbitals, "orb")
    weight = quad_weight * (cell_side**3 / point_count)
    own = jnp.concatenate(
        [jnp.transpose(points, (1, 0, 2)), external[:, None], weight[:, None], jnp.zeros((cells, 3, LANES), f32)], axis=1
    )
    marks = jnp.pad(level_index.astype(f32), (0, LANES - kinds))[None]
    ends = planes - 1
    up = [(i, i + 1) for i in range(ends)]
    down = [(i + 1, i) for i in range(ends)]
    message = jnp.concatenate([f.reshape(kinds * cells, LANES) for f in fields] + [own.reshape(cells * ROWS, LANES)], axis=0)
    windows = (lax.ppermute(message, "space", up), message, lax.ppermute(message, "space", down))
    cst = jnp.asarray(basis_rows())
    base_table = proxy_table(planes, window)
    shift = np.zeros(base_table.shape, np.float32)
    shift[:window, 2] = cell_side
    table = jnp.asarray(base_table) + jnp.asarray(shift) * (me - 1).astype(f32)
    counts = jnp.stack(
        [jnp.sum((near_cells >= 0).astype(jnp.int32), 1), jnp.sum((far_cells >= 0).astype(jnp.int32), 1)], axis=1
    )
    charges = call(
        charge_kernel, "charge", jax.ShapeDtypeStruct((2 * cells + ROWS, LANES), f32), 1, (meta, cst, own, *fields)
    )
    charges = gather_parts(charges, "space", False)

    unroll = 2
    blocks = near_cells.shape[1] + (far_cells.shape[1] + planes + 1) // 2 + 8
    shares = call(
        functools.partial(hartree_kernel, unroll, groups, kinds),
        "hartree",
        jax.ShapeDtypeStruct((1 + groups, ROWS, LANES), f32),
        4,
        (meta, counts, near_cells, far_cells, cst, table, marks, *windows, *charges),
        [
            pltpu.VMEM((planes, 2 * cells + ROWS, LANES), f32),
            pltpu.VMEM((window, ROWS, LANES), f32),
            pltpu.VMEM((window, 1, LANES), f32),
            pltpu.VMEM((window + planes, 1, LANES), f32),
            pltpu.VMEM((3, LANES, LANES), f32),
            pltpu.VMEM((blocks, ROWS, LANES), f32),
            pltpu.VMEM((blocks, 1, LANES), f32),
        ],
    )
    shares = gather_list(shares, "orb")
    levels = jnp.concatenate([share[0, ROWS - 1, :kinds] for share in shares]).astype(jnp.int32)
    hartree, combined = call(
        functools.partial(combine_kernel, kinds),
        "combine",
        (jax.ShapeDtypeStruct((cells, LANES), f32), jax.ShapeDtypeStruct((cells + orbs // 2, LANES), f32)),
        1,
        (meta, *shares),
        [pltpu.VMEM((orbs, LANES), f32)],
    )
    gathered = gather_parts(combined, "space", False)

    batch, unit, steps = 4, 4, 9
    levels_at_most = -(-screening.shape[0] // batch) + 1
    sent = call(
        functools.partial(orbital_kernel, batch, unit, steps),
        "orbitals",
        jax.ShapeDtypeStruct((groups, share, kinds, LANES), f32),
        6,
        (meta, counts, near_cells, far_cells, levels, screening, cst, table, *windows, *gathered),
        [
            pltpu.SMEM((screening.shape[0] + 2 * batch,), f32),
            pltpu.SMEM((screening.shape[0],), jnp.int32),
            pltpu.VMEM((planes, cells + orbs // 2, LANES), f32),
            pltpu.VMEM((window, ROWS, LANES), f32),
            pltpu.VMEM((window, LANES, 2 * orbs), bf16),
            pltpu.VMEM((window + planes, HALF, 2 * orbs), bf16),
            pltpu.VMEM((3, LANES, LANES), f32),
            pltpu.VMEM((blocks, ROWS, LANES), f32),
            pltpu.VMEM((blocks, LANES, 2 * orbs), bf16),
            pltpu.VMEM((blocks, LANES, LANES), f32),
            pltpu.VMEM((blocks, LANES, LANES), f32),
            pltpu.VMEM((levels_at_most, batch * LANES, 2 * orbs), f32),
            pltpu.VMEM((LANES, 2 * orbs), f32),
        ],
    )
    parts = [sent[0]]
    for k in range(1, groups):
        parts.append(lax.ppermute(sent[k], "orb", [(i, i ^ k) for i in range(groups)]))
    updated = call(
        place_kernel,
        "place",
        jax.ShapeDtypeStruct((kinds, cells, LANES), f32),
        1,
        (meta, *parts),
        [pltpu.VMEM((cells, kinds, LANES), f32)],
    )
    return updated, hartree


def solution(mesh):
    in_specs = (
        P("orb", "space", None),
        P(None, "space", None),
        P("space", None),
        P("space", None),
        P(),
        P("orb"),
        P("space", None),
        P("space", None),
    )
    out_specs = (P("orb", "space", None), P("space", None))
    return jax.shard_map(body, mesh=mesh, in_specs=in_specs, out_specs=out_specs, check_vma=False)
```

```python
import functools
import math

import jax
import jax.numpy as jnp
import numpy as np
from jax import lax
from jax.experimental import pallas as pl
from jax.experimental.pallas import tpu as pltpu
from jax.sharding import PartitionSpec as P

NODES = 4
LANES = 128
PLANE = 16
ROWS = 8
HALF = NODES**3

cell_side = 0.25
soften = 6.25e-06
green_scale = -0.5 / math.pi
log2e = math.log2(math.e)
highest = lax.Precision.HIGHEST

node_set = np.cos((2.0 * np.arange(NODES) + 1.0) * (math.pi / (2.0 * NODES)))
roots = [[node_set[m] for m in range(NODES) if m != a] for a in range(NODES)]
scales = [1.0 / np.prod([node_set[a] - r for r in roots[a]]) for a in range(NODES)]


def basis_rows():
    row = np.arange(ROWS)
    out = []
    for pick in (row // 4, 2 + row // 4, row % 4):
        for k in range(NODES - 1):
            out.append([roots[a][k] for a in pick])
        out.append([scales[a] for a in pick])
    return np.broadcast_to(np.array(out, np.float32)[:, :, None], (12, ROWS, LANES)).copy()


def proxy_table(planes, window):
    offset = 0.5 * (node_set + 1.0)
    p = np.arange(LANES) % HALF
    offs = np.stack([offset[p // 16], offset[p // 4 % 4], offset[p % 4]])
    cells = np.arange(window)
    lows = np.stack([cells % 4, cells // 4 % 4, cells // 16]) * cell_side
    near = lows[:, :, None] + offs[:, None, :] * cell_side
    levels = np.arange(planes)
    lows = np.stack([0 * levels, 0 * levels, levels]) * cell_side
    far = lows[:, :, None] + offs[:, None, :] * np.array([1.0, 1.0, cell_side])[:, None, None]
    table = np.zeros((window + planes, ROWS, LANES), np.float32)
    table[:, :3] = np.moveaxis(np.concatenate([near, far], 1), 0, 1)
    return table


def poly(u, r0, r1, r2, scale):
    return ((u - r0) * (u - r1)) * ((u - r2) * scale)


def weights(cst, x, y, z, lows, sides):
    ux, uy, uz = (
        jnp.broadcast_to(2.0 * (c - lo) / e - 1.0, (ROWS, LANES)) for c, lo, e in zip((x, y, z), lows, sides)
    )
    pz = poly(uz, cst[8], cst[9], cst[10], cst[11])
    pyz = [poly(uy, cst[4 * k], cst[4 * k + 1], cst[4 * k + 2], cst[4 * k + 3]) * pz for k in range(2)]
    parts = []
    for a in range(NODES):
        px = poly(ux, *(float(r) for r in roots[a]), float(scales[a]))
        parts += [px * pyz[0], px * pyz[1]]
    return jnp.concatenate(parts, axis=0)


def twice(w):
    return jnp.concatenate([w, w], axis=0)


def cell_low(cell):
    return [(cell % 4).astype(jnp.float32) * cell_side, (cell // 4 % 4).astype(jnp.float32) * cell_side]


def dot_nt(a, b):
    return lax.dot_general(a, b, (((1,), (1,)), ((), ())), precision=highest, preferred_element_type=jnp.float32)


def gather_parts(block, axis, pairs):
    count = lax.axis_size(axis)
    parts = [block[None]]
    while sum(p.shape[0] for p in parts) < count:
        held = parts[0] if len(parts) == 1 else jnp.concatenate(parts, axis=0)
        have = held.shape[0]
        steps = range(1, 4 if (have > 1 or pairs) and have * 4 <= count else 2)
        parts = [held] + [lax.ppermute(held, axis, [(i, i ^ (have * j)) for i in range(count)]) for j in steps]
    return parts


def gather_list(block, axis):
    parts = gather_parts(block, axis, True)
    return [p[k] for p in parts for k in range(p.shape[0])]


def lay_out(parts, whole):
    at = 0
    for part in parts:
        for k in range(part.shape[0]):
            whole[at + k] = part[k]
        at += part.shape[0]


def target_cell(me, t, groups):
    return t * groups + lax.bitwise_xor(jnp.int32(t) if isinstance(t, int) else t, me)


def split(v):
    high = v.astype(jnp.bfloat16)
    return high, (v - high.astype(jnp.float32)).astype(jnp.bfloat16)


def dot_bf16(a, b):
    return lax.dot_general(a, b, (((1,), (1,)), ((), ())), preferred_element_type=jnp.float32)


def dot_split(v, w):
    vh, vl = split(v)
    wh, wl = split(w)
    rows = v.shape[0]
    both = dot_bf16(jnp.concatenate([vh, vl], axis=0), wh)
    return both[:rows] + both[rows:] + dot_bf16(vh, wl)


def charge_kernel(meta, cst, own, *refs):
    z_low = meta[0].astype(jnp.float32) * cell_side
    fields, out = refs[:-1], refs[-1]
    density = jnp.zeros((PLANE, LANES), jnp.float32)
    for phi in fields:
        for j in range(phi.shape[0]):
            v = phi[j]
            density = density + v * v
    out[:PLANE, :] = density
    acc = jnp.zeros((HALF, LANES), jnp.float32)
    ones = jnp.ones((ROWS, LANES), jnp.float32)
    for c in range(PLANE):
        charge = own[c, 4:5, :] * (2.0 * out[c : c + 1, :])
        out[c : c + 1, :] = charge
        x, y, z = own[c, 0:1, :], own[c, 1:2, :], own[c, 2:3, :]
        low = (cell_side * (c % 4), cell_side * (c // 4), z_low)
        acc = acc + weights(cst, x, y, z, (0.0, 0.0, z_low), (1.0, 1.0, cell_side)) * charge
        moments = dot_nt(ones, twice(weights(cst, x, y, z, low, (cell_side,) * 3) * charge))
        out[PLANE + c : PLANE + c + 1, :] = moments[0:1, :]
    out[2 * PLANE :, :] = dot_nt(ones, twice(acc))


def live_planes(me, planes):
    below = jnp.maximum(me - 1, 0)
    return below, below + jnp.maximum(planes - 2 - me, 0)


def list_blocks(own, start, me, cell, counts, near, far, planes, put_near, put_far, put_none):
    window = 3 * PLANE
    base = (me - 1) * PLANE
    near_low, near_own, near_all, far_low, far_own, far_all = (counts[cell, k] for k in range(6))
    if own:
        n_near, n_far, n_planes = near_own, far_own, 0
    else:
        below, n_planes = live_planes(me, planes)
        n_near, n_far = near_all - near_own, far_all - far_own
    n_items = n_far + n_planes
    n_pairs = (n_items + 1) // 2

    def place(j, low, mid):
        return j + low if own else jnp.where(j < low, j, j + mid)

    def near_step(j, c):
        put_near(start + j, near[cell, place(j, near_low, near_own)] - base)
        return c

    lax.fori_loop(0, n_near, near_step, 0)

    def item(j):
        j = jnp.minimum(j, n_items - 1)
        slot = far[cell, jnp.clip(place(j, far_low, far_own), 0, far.shape[1] - 1)] - base
        if own:
            return slot
        p = j - n_far
        level = jnp.where(p < below, p, p + (me + 2 - below))
        return jnp.where(j < n_far, slot, window + level)

    def far_step(j, c):
        put_far(start + n_near + j, item(2 * j), item(2 * j + 1), 2 * j + 1 < n_items)
        return c

    lax.fori_loop(0, n_pairs, far_step, 0)
    last = start + n_near + n_pairs
    put_none(last)
    return start + (n_near + n_pairs + 1) // 2 * 2


def in_low_half():
    return lax.broadcasted_iota(jnp.int32, (1, LANES), 1) < HALF


def put_targets(pts, cell, tgt):
    for d in range(3):
        tgt[d] = jnp.broadcast_to(pts[PLANE + cell, d : d + 1, :], (LANES, LANES)).T


def square(tgt, src, slot, rows):
    dx = tgt[0, rows, :] - src[slot, 0:1, :]
    dy = tgt[1, rows, :] - src[slot, 1:2, :]
    dz = tgt[2, rows, :] - src[slot, 2:3, :]
    return (dx * dx + dy * dy) + (dz * dz + soften)


def put_points(messages, pts):
    for k, message in enumerate(messages):
        top = message.shape[0] - PLANE * ROWS
        for c in range(PLANE):
            pts[k * PLANE + c] = message[top + c * ROWS : top + (c + 1) * ROWS, :]


def cell_fields(message, c, groups, kinds):
    rows = kinds * PLANE
    return jnp.concatenate(
        [message[pl.ds(g * rows + c, kinds, stride=PLANE), :] for g in range(groups)], axis=0
    )


def pairs_kernel(groups, planes, meta, counts, near, far, table, before, mine, after, inv, dist, pts, tgt, src):
    put_points((before, mine, after), pts)
    me, group = meta[0], meta[1]
    low_half = in_low_half()

    def put_near(j, slot):
        src[j] = pts[slot]

    def put_far(j, first, second, live):
        src[j] = jnp.where(low_half, table[first], table[second])

    def put_none(j):
        src[j] = jnp.zeros(src.shape[1:], jnp.float32)

    def per_cell(t, carry):
        cell = target_cell(group, t, groups)
        end = jnp.int32(0)
        for own in (True, False):
            end = list_blocks(own, end, me, cell, counts, near, far, planes, put_near, put_far, put_none)
        put_targets(pts, cell, tgt)

        def measure(i, x):
            for u in range(2):
                sq = square(tgt, src, 2 * i + u, slice(None))
                r = lax.rsqrt(sq)
                inv[t, 2 * i + u] = r
                dist[t, 2 * i + u] = sq * r
            return x

        lax.fori_loop(0, end // 2, measure, 0)
        return carry

    lax.fori_loop(0, PLANE // groups, per_cell, 0)


def hartree_kernel(groups, kinds, meta, counts, near, far, cst, marks, mine, inv, *refs):
    parts, (out, every, val, mom, srcv) = refs[:-5], refs[-5:]
    lay_out(parts, every)
    planes = every.shape[0]
    cells = PLANE // groups
    me, group = meta[0], meta[1]
    for k in range(3):
        there = lax.bitwise_xor(me, jnp.clip(me - 1 + k, 0, planes - 1))
        val[k * PLANE : (k + 1) * PLANE, 0, :] = every[there, :PLANE, :]
        mom[k * PLANE : (k + 1) * PLANE, 0, :] = every[there, PLANE : 2 * PLANE, :]

    def put_plane(g, c):
        mom[3 * PLANE + g] = every[lax.bitwise_xor(me, g), 2 * PLANE : 2 * PLANE + 1, :]
        return c

    lax.fori_loop(0, planes, put_plane, 0)
    low_half = in_low_half()

    def put_near(j, slot):
        srcv[j] = val[slot]

    def put_far(j, first, second, live):
        srcv[j] = jnp.where(low_half, mom[first], mom[second] * live.astype(jnp.float32))

    def put_none(j):
        srcv[j] = jnp.zeros((1, LANES), jnp.float32)

    z_low = me.astype(jnp.float32) * cell_side
    top = mine.shape[0] - PLANE * ROWS
    total = jnp.zeros((groups * kinds, LANES), jnp.float32)
    out[0] = jnp.broadcast_to(marks[...], (ROWS, LANES))
    for t in range(cells):
        cell = target_cell(group, t, groups)
        end = jnp.int32(0)
        for own in (True, False):
            end = list_blocks(own, end, me, cell, counts, near, far, planes, put_near, put_far, put_none)

        def step(i, acc):
            return acc + (inv[t, 2 * i] * srcv[2 * i] + inv[t, 2 * i + 1] * srcv[2 * i + 1])

        acc = lax.fori_loop(0, end // 2, step, jnp.zeros((LANES, LANES), jnp.float32))
        row = dot_nt(jnp.ones((ROWS, LANES), jnp.float32), acc)[0:1, :]
        out[0, t : t + 1, :] = row
        point = mine[pl.ds(pl.multiple_of(top + cell * ROWS, ROWS), ROWS), :]
        scaled = point[4:5] * (point[3:4] + row)
        v = cell_fields(mine, cell, groups, kinds) * scaled
        w = weights(cst, point[0:1], point[1:2], point[2:3], (0.0, 0.0, z_low), (1.0, 1.0, cell_side))
        total = total + dot_split(v, twice(w))
    for k in range(groups):
        out[1 + lax.bitwise_xor(group, k), :kinds, :] = total[k * kinds : (k + 1) * kinds, :]


def combine_kernel(kinds, meta, *refs):
    shares, (hartree, out, total) = refs[:-3], refs[-3:]
    groups = len(shares)
    for k, share in enumerate(shares):
        for t in range(PLANE // groups):
            cell = target_cell(lax.bitwise_xor(meta[1], k), t, groups)
            out[pl.ds(cell, 1), :] = share[0, t : t + 1, :]
    hartree[...] = out[:PLANE, :]
    for g in range(groups):
        added = shares[0][1 + g, :kinds, :]
        for share in shares[1:]:
            added = added + share[1 + g, :kinds, :]
        total[g * kinds : (g + 1) * kinds, :] = added
    rows = groups * kinds // 2
    low_half = lax.broadcasted_iota(jnp.int32, (1, LANES), 1) < HALF
    out[PLANE:, :] = jnp.where(low_half, total[:rows, :], total[rows:, :])


def orbital_kernel(own, planes, batch, steps, meta, counts, near, far, levels, screening, cst, inv, dist, *refs):
    if own:
        mine, hartree, out, rate, slot_of, units, val, mom, srcv, acc = refs
    else:
        before, after, partial, *parts = refs[:-9]
        out, rate, slot_of, units, val, mom, srcv, acc, every = refs[-9:]
        lay_out(parts, every)
    groups, cells, kinds, _ = out.shape
    orbs = groups * kinds
    me, group = meta[0], meta[1]

    def clear(i, c):
        slot_of[i] = -1
        rate[i] = 0.0
        return c

    lax.fori_loop(0, screening.shape[0], clear, 0)
    for q in range(2 * batch):
        rate[screening.shape[0] + q] = 0.0
    lane = lax.broadcasted_iota(jnp.int32, (1, LANES), 1) % orbs

    def rank(i, carry):
        found, lane_slot = carry
        level = levels[i]
        known = slot_of[level]
        slot = jnp.where(known < 0, found, known)
        slot_of[level] = slot
        rate[slot] = screening[level] * (-log2e)
        return found + (known < 0).astype(jnp.int32), jnp.where(lane == i, slot, lane_slot)

    n_levels, lane_slot = lax.fori_loop(0, orbs, rank, (jnp.int32(0), jnp.zeros((1, LANES), jnp.int32)))
    n_batches = (n_levels + batch - 1) // batch
    first_half = lax.broadcasted_iota(jnp.int32, (1, 2 * orbs), 1) < orbs

    def flip(v):
        high = v.astype(jnp.bfloat16).astype(jnp.float32)
        square = jnp.concatenate([high, v - high, jnp.zeros((LANES - 2 * orbs, LANES), jnp.float32)], axis=0)
        return square.T[:, : 2 * orbs].astype(jnp.bfloat16)

    for k in (1,) if own else (0, 2):
        message = mine if own else (before if k == 0 else after)
        there = lax.bitwise_xor(me, jnp.clip(me - 1 + k, 0, planes - 1))
        top = message.shape[0] - PLANE * ROWS

        def prepare(c, carry):
            at = k * PLANE + c
            point = message[pl.ds(pl.multiple_of(top + c * ROWS, ROWS), ROWS), :]
            potential = point[3:4] + (hartree[pl.ds(c, 1), :] if own else every[there, pl.ds(c, 1), :])
            v = cell_fields(message, c, groups, kinds) * (point[4:5] * potential)
            val[at] = flip(v)
            vh, vl = split(v)
            z_low = (me - 1 + k).astype(jnp.float32) * cell_side
            low = (*cell_low(c), z_low)
            wh, wl = split(weights(cst, point[0:1], point[1:2], point[2:3], low, (cell_side,) * 3))
            all_of = dot_bf16(jnp.concatenate([wh, wl], axis=0), jnp.concatenate([vh, vh, vl, vl], axis=0))
            m = all_of[:HALF] + all_of[HALF:]
            m = m[:, : 2 * orbs] + pltpu.roll(all_of[:HALF], 2 * orbs, 1)[:, : 2 * orbs]
            high = m.astype(jnp.bfloat16).astype(jnp.float32)
            mom[at] = jnp.where(first_half, high, m - high).astype(jnp.bfloat16)
            return carry

        lax.fori_loop(0, PLANE, prepare, 0, unroll=4)

    def put_plane(g, c):
        there = lax.bitwise_xor(me, g)
        rows = []
        for k in range(groups):
            row = lax.bitwise_xor(group, k) * kinds
            v = every[there, pl.ds(PLANE + lax.rem(row, orbs // 2), kinds), :]
            rows.append(jnp.where(row < orbs // 2, v, pltpu.roll(v, HALF, 1)))
        mom[3 * PLANE + g] = flip(jnp.concatenate(rows, axis=0))[:HALF]
        return c

    if not own:
        lax.fori_loop(0, planes, put_plane, 0)

    def list_cell(t, carry):
        def put_near(j, slot):
            srcv[t, j] = val[slot]

        def put_far(j, first, second, live):
            srcv[t, j, :HALF, :] = mom[first]
            srcv[t, j, HALF:, :] = jnp.where(live, mom[second], jnp.zeros_like(mom[second]))

        def put_none(j):
            srcv[t, j] = jnp.zeros(srcv.shape[2:], srcv.dtype)

        cell = target_cell(group, t, groups)
        begin = jnp.int32(0)
        if not own:
            begin = counts[cell, 1] + (counts[cell, 4] + 1) // 2
            begin = (begin + 1) // 2 * 2
        end = list_blocks(own, begin, me, cell, counts, near, far, planes, put_near, put_far, put_none)
        units[0, t] = begin // 2
        units[1, t] = end // 2

        def clear_acc(b, x):
            acc[t, b] = jnp.zeros(acc.shape[2:], jnp.float32)
            return x

        lax.fori_loop(0, n_batches, clear_acc, 0)
        return carry

    lax.fori_loop(0, cells, list_cell, 0)
    work = sum(units[1, t] - units[0, t] for t in range(cells)) * n_batches

    def step(i, at):
        t, b, u = at
        for _ in range(steps):
            rows = []
            for q in range(batch):
                r = rate[b * batch + q]
                tiles = [(jnp.exp2(dist[t, 2 * u + h] * r) * inv[t, 2 * u + h]).astype(jnp.bfloat16) for h in range(2)]
                rows.append(jnp.concatenate(tiles, axis=1))
            v = jnp.concatenate([srcv[t, 2 * u], srcv[t, 2 * u + 1]], axis=0)
            acc[t, b] = acc[t, b] + jnp.dot(jnp.concatenate(rows, axis=0), v, preferred_element_type=jnp.float32)
            wrap = u + 1 >= units[1, t]
            b = jnp.where(wrap, b + 1, b)
            over = b >= n_batches
            done = over & (t + 1 >= cells)
            t = jnp.where(over & (t + 1 < cells), t + 1, t)
            b = jnp.where(done, n_batches, jnp.where(over, 0, b))
            u = jnp.where(wrap, units[0, t], u + 1)
        return t, b, u

    lax.fori_loop(0, (work + steps - 1) // steps, step, (jnp.int32(0), jnp.int32(0), units[0, 0]))

    def finish(t, carry):
        def choose(b, add):
            for q in range(batch):
                mine = lane_slot[:, : 2 * orbs] == b * batch + q
                add = add + jnp.where(mine, acc[t, b, q * LANES : (q + 1) * LANES, :], 0.0)
            return add

        total = lax.fori_loop(0, n_batches, choose, jnp.zeros((LANES, 2 * orbs), jnp.float32))
        flipped = jnp.concatenate([total, jnp.zeros((LANES, LANES - 2 * orbs), jnp.float32)], axis=1).T
        rows = (flipped[:orbs] + flipped[orbs : 2 * orbs]) * green_scale
        for k in range(groups):
            mine = rows[k * kinds : (k + 1) * kinds]
            out[k, t] = mine if own else mine + partial[k, t]
        return carry

    lax.fori_loop(0, cells, finish, 0)


def place_kernel(meta, *refs):
    parts, out, ordered = refs[:-2], refs[-2], refs[-1]
    for k, part in enumerate(parts):
        for t in range(part.shape[0]):
            ordered[target_cell(lax.bitwise_xor(meta[1], k), t, len(parts))] = part[t]
    for c in range(PLANE):
        out[:, c, :] = ordered[c]


def smem():
    return pl.BlockSpec(memory_space=pltpu.SMEM)


def vmem():
    return pl.BlockSpec(memory_space=pltpu.VMEM)


def call(kernel, name, out_shape, smems, args, scratch=()):
    return pl.pallas_call(
        kernel,
        out_shape=out_shape,
        in_specs=[smem()] * smems + [vmem()] * (len(args) - smems),
        out_specs=jax.tree.map(lambda _: vmem(), out_shape),
        scratch_shapes=scratch,
        compiler_params=pltpu.CompilerParams(vmem_limit_bytes=28 * 1024 * 1024),
        name=name,
    )(*args)


def body(orbitals, points, quad_weight, external, screening, level_index, near_cells, far_cells):
    kinds, cells, point_count = orbitals.shape
    planes, groups = lax.axis_size("space"), lax.axis_size("orb")
    orbs = kinds * groups
    window = 3 * PLANE
    share = cells // groups
    me, group = lax.axis_index("space"), lax.axis_index("orb")
    meta = jnp.stack([me, group]).astype(jnp.int32)
    f32, bf16 = jnp.float32, jnp.bfloat16

    fields = gather_list(orbitals, "orb")
    weight = quad_weight * (cell_side**3 / point_count)
    own = jnp.concatenate(
        [jnp.transpose(points, (1, 0, 2)), external[:, None], weight[:, None], jnp.zeros((cells, 3, LANES), f32)], axis=1
    )
    marks = jnp.pad(level_index.astype(f32), (0, LANES - kinds))[None]
    ends = planes - 1
    up = [(i, i + 1) for i in range(ends)]
    down = [(i + 1, i) for i in range(ends)]
    cst = jnp.asarray(basis_rows())
    base_table = proxy_table(planes, window)
    shift = np.zeros(base_table.shape, np.float32)
    shift[:window, 2] = cell_side
    table = jnp.asarray(base_table) + jnp.asarray(shift) * (me - 1).astype(f32)
    counts = []
    for cells_of in (near_cells, far_cells):
        slot = cells_of - me * cells
        listed = cells_of >= 0
        inside = (slot >= 0) & (slot < cells)
        for chosen in (listed & (slot < 0), listed & inside, listed):
            counts.append(jnp.sum(chosen.astype(jnp.int32), axis=1))
    counts = jnp.stack(counts, axis=1)

    charges = call(
        charge_kernel, "charge", jax.ShapeDtypeStruct((2 * cells + ROWS, LANES), f32), 1, (meta, cst, own, *fields)
    )
    message = jnp.concatenate([f.reshape(kinds * cells, LANES) for f in fields] + [own.reshape(cells * ROWS, LANES)], axis=0)
    charges, message = lax.optimization_barrier((charges, message))
    charges = gather_parts(charges, "space", False)
    before, mine, after = lax.ppermute(message, "space", up), message, lax.ppermute(message, "space", down)

    most = near_cells.shape[1]
    blocks = most + (window - most + planes + 1) // 2 + 4
    pairs = pltpu.VMEM((share, blocks, LANES, LANES), f32)
    inv, dist = call(
        functools.partial(pairs_kernel, groups, planes),
        "pairs",
        (pairs, pairs),
        4,
        (meta, counts, near_cells, far_cells, table, before, mine, after),
        [
            pltpu.VMEM((window, ROWS, LANES), f32),
            pltpu.VMEM((3, LANES, LANES), f32),
            pltpu.VMEM((blocks, ROWS, LANES), f32),
        ],
    )
    shares = call(
        functools.partial(hartree_kernel, groups, kinds),
        "hartree",
        jax.ShapeDtypeStruct((1 + groups, ROWS, LANES), f32),
        4,
        (meta, counts, near_cells, far_cells, cst, marks, mine, inv, *charges),
        [
            pltpu.VMEM((planes, 2 * cells + ROWS, LANES), f32),
            pltpu.VMEM((window, 1, LANES), f32),
            pltpu.VMEM((window + planes, 1, LANES), f32),
            pltpu.VMEM((blocks, 1, LANES), f32),
        ],
    )
    shares = gather_list(shares, "orb")
    levels = jnp.concatenate([share[0, ROWS - 1, :kinds] for share in shares]).astype(jnp.int32)
    hartree, combined = call(
        functools.partial(combine_kernel, kinds),
        "combine",
        (jax.ShapeDtypeStruct((cells, LANES), f32), jax.ShapeDtypeStruct((cells + orbs // 2, LANES), f32)),
        1,
        (meta, *shares),
        [pltpu.VMEM((orbs, LANES), f32)],
    )
    gathered = gather_parts(combined, "space", False)

    batch, steps = 4, 16
    levels_at_most = -(-screening.shape[0] // batch) + 1

    def orbital_part(own_plane, *args):
        scratch = [
            pltpu.SMEM((screening.shape[0] + 2 * batch,), f32),
            pltpu.SMEM((screening.shape[0],), jnp.int32),
            pltpu.SMEM((2, share), jnp.int32),
            pltpu.VMEM((window, LANES, 2 * orbs), bf16),
            pltpu.VMEM((window + planes, HALF, 2 * orbs), bf16),
            pltpu.VMEM((share, blocks, LANES, 2 * orbs), bf16),
            pltpu.VMEM((share, levels_at_most, batch * LANES, 2 * orbs), f32),
        ]
        if not own_plane:
            scratch.append(pltpu.VMEM((planes, cells + orbs // 2, LANES), f32))
        return call(
            functools.partial(orbital_kernel, own_plane, planes, batch, steps),
            "own_orbitals" if own_plane else "orbitals",
            jax.ShapeDtypeStruct((groups, share, kinds, LANES), f32),
            6,
            (meta, counts, near_cells, far_cells, levels, screening, cst, inv, dist, *args),
            scratch,
        )

    partial = orbital_part(True, mine, hartree)
    sent = orbital_part(False, before, after, partial, *gathered)
    parts = [sent[0]]
    for k in range(1, groups):
        parts.append(lax.ppermute(sent[k], "orb", [(i, i ^ k) for i in range(groups)]))
    updated = call(
        place_kernel,
        "place",
        jax.ShapeDtypeStruct((kinds, cells, LANES), f32),
        1,
        (meta, *parts),
        [pltpu.VMEM((cells, kinds, LANES), f32)],
    )
    return updated, hartree


def solution(mesh):
    in_specs = (
        P("orb", "space", None),
        P(None, "space", None),
        P("space", None),
        P("space", None),
        P(),
        P("orb"),
        P("space", None),
        P("space", None),
    )
    out_specs = (P("orb", "space", None), P("space", None))
    return jax.shard_map(body, mesh=mesh, in_specs=in_specs, out_specs=out_specs, check_vma=False)
```

```python
import functools
import math

import jax
import jax.numpy as jnp
import numpy as np
from jax import lax
from jax.experimental import pallas as pl
from jax.experimental.pallas import tpu as pltpu
from jax.sharding import PartitionSpec as P

NODES = 4
LANES = 128
PLANE = 16
ROWS = 8
HALF = NODES**3

cell_side = 0.25
soften = 6.25e-06
green_scale = -0.5 / math.pi
log2e = math.log2(math.e)
highest = lax.Precision.HIGHEST

node_set = np.cos((2.0 * np.arange(NODES) + 1.0) * (math.pi / (2.0 * NODES)))
roots = [[node_set[m] for m in range(NODES) if m != a] for a in range(NODES)]
scales = [1.0 / np.prod([node_set[a] - r for r in roots[a]]) for a in range(NODES)]


def basis_rows():
    row = np.arange(ROWS)
    out = []
    for pick in (row // 4, 2 + row // 4, row % 4):
        for k in range(NODES - 1):
            out.append([roots[a][k] for a in pick])
        out.append([scales[a] for a in pick])
    return np.broadcast_to(np.array(out, np.float32)[:, :, None], (12, ROWS, LANES)).copy()


def proxy_table(planes, window):
    offset = 0.5 * (node_set + 1.0)
    p = np.arange(LANES) % HALF
    offs = np.stack([offset[p // 16], offset[p // 4 % 4], offset[p % 4]])
    cells = np.arange(window)
    lows = np.stack([cells % 4, cells // 4 % 4, cells // 16]) * cell_side
    near = lows[:, :, None] + offs[:, None, :] * cell_side
    levels = np.arange(planes)
    lows = np.stack([0 * levels, 0 * levels, levels]) * cell_side
    far = lows[:, :, None] + offs[:, None, :] * np.array([1.0, 1.0, cell_side])[:, None, None]
    table = np.zeros((window + planes, ROWS, LANES), np.float32)
    table[:, :3] = np.moveaxis(np.concatenate([near, far], 1), 0, 1)
    return table


def poly(u, r0, r1, r2, scale):
    return ((u - r0) * (u - r1)) * ((u - r2) * scale)


def weights(cst, x, y, z, lows, sides):
    ux, uy, uz = (
        jnp.broadcast_to(2.0 * (c - lo) / e - 1.0, (ROWS, LANES)) for c, lo, e in zip((x, y, z), lows, sides)
    )
    pz = poly(uz, cst[8], cst[9], cst[10], cst[11])
    pyz = [poly(uy, cst[4 * k], cst[4 * k + 1], cst[4 * k + 2], cst[4 * k + 3]) * pz for k in range(2)]
    parts = []
    for a in range(NODES):
        px = poly(ux, *(float(r) for r in roots[a]), float(scales[a]))
        parts += [px * pyz[0], px * pyz[1]]
    return jnp.concatenate(parts, axis=0)


def twice(w):
    return jnp.concatenate([w, w], axis=0)


def cell_low(cell):
    return [(cell % 4).astype(jnp.float32) * cell_side, (cell // 4 % 4).astype(jnp.float32) * cell_side]


def dot_nt(a, b):
    return lax.dot_general(a, b, (((1,), (1,)), ((), ())), precision=highest, preferred_element_type=jnp.float32)


def gather_parts(block, axis, pairs, later=()):
    count = lax.axis_size(axis)
    parts = [block[None]]
    while sum(p.shape[0] for p in parts) < count:
        held = parts[0] if len(parts) == 1 else jnp.concatenate(parts, axis=0)
        have = held.shape[0]
        steps = range(1, 4 if (have > 1 or pairs) and have * 4 <= count else 2)
        parts = [held] + [lax.ppermute(held, axis, [(i, i ^ (have * j)) for i in range(count)]) for j in steps]
        if later and have == 1:
            parts[1], later = lax.optimization_barrier((parts[1], later))
    return parts, later


def gather_list(block, axis):
    parts, _ = gather_parts(block, axis, True)
    return [p[k] for p in parts for k in range(p.shape[0])]


def lay_out(parts, whole):
    at = 0
    for part in parts:
        for k in range(part.shape[0]):
            whole[at + k] = part[k]
        at += part.shape[0]


def target_cell(me, t, groups):
    return t * groups + lax.bitwise_xor(jnp.int32(t) if isinstance(t, int) else t, me)


def split(v):
    high = v.astype(jnp.bfloat16)
    return high, (v - high.astype(jnp.float32)).astype(jnp.bfloat16)


def dot_bf16(a, b):
    return lax.dot_general(a, b, (((1,), (1,)), ((), ())), preferred_element_type=jnp.float32)


def dot_split(v, w):
    vh, vl = split(v)
    wh, wl = split(w)
    rows = v.shape[0]
    both = dot_bf16(jnp.concatenate([vh, vl], axis=0), wh)
    return both[:rows] + both[rows:] + dot_bf16(vh, wl)


def charge_kernel(meta, cst, own, *refs):
    z_low = meta[0].astype(jnp.float32) * cell_side
    fields, out = refs[:-1], refs[-1]
    density = jnp.zeros((PLANE, LANES), jnp.float32)
    for phi in fields:
        for j in range(phi.shape[0]):
            v = phi[j]
            density = density + v * v
    out[:PLANE, :] = density
    acc = jnp.zeros((HALF, LANES), jnp.float32)
    ones = jnp.ones((ROWS, LANES), jnp.float32)
    for c in range(PLANE):
        charge = own[c, 4:5, :] * (2.0 * out[c : c + 1, :])
        out[c : c + 1, :] = charge
        x, y, z = own[c, 0:1, :], own[c, 1:2, :], own[c, 2:3, :]
        low = (cell_side * (c % 4), cell_side * (c // 4), z_low)
        acc = acc + weights(cst, x, y, z, (0.0, 0.0, z_low), (1.0, 1.0, cell_side)) * charge
        moments = dot_nt(ones, twice(weights(cst, x, y, z, low, (cell_side,) * 3) * charge))
        out[PLANE + c : PLANE + c + 1, :] = moments[0:1, :]
    out[2 * PLANE :, :] = dot_nt(ones, twice(acc))


def live_planes(me, planes):
    below = jnp.maximum(me - 1, 0)
    return below, below + jnp.maximum(planes - 2 - me, 0)


def list_blocks(me, cell, counts, near, far, planes, put_near, put_far, put_none, multiple):
    window = 3 * PLANE
    base = (me - 1) * PLANE
    below, n_planes = live_planes(me, planes)
    n_near, n_far = counts[cell, 0], counts[cell, 1]
    n_items = n_far + n_planes
    n_pairs = (n_items + 1) // 2

    def near_step(j, c):
        put_near(j, near[cell, j] - base)
        return c

    lax.fori_loop(0, n_near, near_step, 0)

    def item(j):
        j = jnp.minimum(j, n_items - 1)
        p = j - n_far
        level = jnp.where(p < below, p, p + (me + 2 - below))
        slot = far[cell, jnp.minimum(j, far.shape[1] - 1)] - base
        return jnp.where(j < n_far, slot, window + level)

    def far_step(j, c):
        put_far(n_near + j, item(2 * j), item(2 * j + 1), 2 * j + 1 < n_items)
        return c

    lax.fori_loop(0, n_pairs, far_step, 0)
    for u in range(multiple - 1):
        put_none(n_near + n_pairs + u)
    return n_near + n_pairs


def in_low_half():
    return lax.broadcasted_iota(jnp.int32, (1, LANES), 1) < HALF


def put_targets(pts, cell, tgt):
    for d in range(3):
        tgt[d] = jnp.broadcast_to(pts[PLANE + cell, d : d + 1, :], (LANES, LANES)).T


def square(tgt, src, slot, rows):
    dx = tgt[0, rows, :] - src[slot, 0:1, :]
    dy = tgt[1, rows, :] - src[slot, 1:2, :]
    dz = tgt[2, rows, :] - src[slot, 2:3, :]
    return (dx * dx + dy * dy) + (dz * dz + soften)


def cell_fields(message, c, groups, kinds):
    rows = kinds * PLANE
    return jnp.concatenate([message[pl.ds(g * rows + c, kinds, stride=PLANE), :] for g in range(groups)], axis=0)


def pairs_kernel(groups, planes, unit, meta, counts, near, far, table, before, mine, after, out, pts, tgt, src):
    for k, points in enumerate((before, mine, after)):
        pts[k * PLANE : (k + 1) * PLANE] = points[...]
    me, group = meta[0], meta[1]
    low_half = in_low_half()

    def put_near(j, slot):
        src[j] = pts[slot]

    def put_far(j, first, second, live):
        src[j] = jnp.where(low_half, table[first], table[second])

    def put_none(j):
        src[j] = jnp.zeros(src.shape[1:], jnp.float32)

    def per_cell(t, carry):
        cell = target_cell(group, t, groups)
        n_blocks = list_blocks(me, cell, counts, near, far, planes, put_near, put_far, put_none, unit)
        put_targets(pts, cell, tgt)

        def measure(i, x):
            for u in range(unit):
                out[t, unit * i + u] = square(tgt, src, unit * i + u, slice(None))
            return x

        lax.fori_loop(0, (n_blocks + unit - 1) // unit, measure, 0)
        return carry

    lax.fori_loop(0, PLANE // groups, per_cell, 0)


def hartree_kernel(groups, kinds, meta, counts, near, far, cst, marks, own, mine, squares, *refs):
    parts, (out, every, val, mom, srcv) = refs[:-5], refs[-5:]
    lay_out(parts, every)
    planes = every.shape[0]
    cells = PLANE // groups
    me, group = meta[0], meta[1]
    for k in range(3):
        there = lax.bitwise_xor(me, jnp.clip(me - 1 + k, 0, planes - 1))
        val[k * PLANE : (k + 1) * PLANE, 0, :] = every[there, :PLANE, :]
        mom[k * PLANE : (k + 1) * PLANE, 0, :] = every[there, PLANE : 2 * PLANE, :]

    def put_plane(g, c):
        mom[3 * PLANE + g] = every[lax.bitwise_xor(me, g), 2 * PLANE : 2 * PLANE + 1, :]
        return c

    lax.fori_loop(0, planes, put_plane, 0)
    low_half = in_low_half()

    def put_near(j, slot):
        srcv[j] = val[slot]

    def put_far(j, first, second, live):
        srcv[j] = jnp.where(low_half, mom[first], mom[second] * live.astype(jnp.float32))

    def put_none(j):
        srcv[j] = jnp.zeros((1, LANES), jnp.float32)

    z_low = me.astype(jnp.float32) * cell_side
    total = jnp.zeros((groups * kinds, LANES), jnp.float32)
    out[0] = jnp.broadcast_to(marks[...], (ROWS, LANES))
    for t in range(cells):
        cell = target_cell(group, t, groups)
        n_blocks = list_blocks(me, cell, counts, near, far, planes, put_near, put_far, put_none, 2)

        def step(i, acc):
            parts = [lax.rsqrt(squares[t, 2 * i + u]) * srcv[2 * i + u] for u in range(2)]
            return acc + (parts[0] + parts[1])

        acc = lax.fori_loop(0, (n_blocks + 1) // 2, step, jnp.zeros((LANES, LANES), jnp.float32))
        row = dot_nt(jnp.ones((ROWS, LANES), jnp.float32), acc)[0:1, :]
        out[0, t : t + 1, :] = row
        point = own[cell]
        scaled = point[4:5] * (point[3:4] + row)
        v = cell_fields(mine, cell, groups, kinds) * scaled
        w = weights(cst, point[0:1], point[1:2], point[2:3], (0.0, 0.0, z_low), (1.0, 1.0, cell_side))
        total = total + dot_split(v, twice(w))
    for k in range(groups):
        out[1 + lax.bitwise_xor(group, k), :kinds, :] = total[k * kinds : (k + 1) * kinds, :]


def combine_kernel(kinds, meta, *refs):
    shares, (hartree, out, total) = refs[:-3], refs[-3:]
    groups = len(shares)
    for k, share in enumerate(shares):
        for t in range(PLANE // groups):
            cell = target_cell(lax.bitwise_xor(meta[1], k), t, groups)
            out[pl.ds(cell, 1), :] = share[0, t : t + 1, :]
    hartree[...] = out[:PLANE, :]
    for g in range(groups):
        added = shares[0][1 + g, :kinds, :]
        for share in shares[1:]:
            added = added + share[1 + g, :kinds, :]
        total[g * kinds : (g + 1) * kinds, :] = added
    rows = groups * kinds // 2
    low_half = lax.broadcasted_iota(jnp.int32, (1, LANES), 1) < HALF
    out[PLANE:, :] = jnp.where(low_half, total[:rows, :], total[rows:, :])


def orbital_kernel(
    planes, batch, unit, steps, meta, counts, near, far, levels, screening, cst,
    points_before, own, points_after, before, mine, after, squares, *refs,
):
    parts, (out, rate, slot_of, every, val, mom, srcv, dist, inv, acc) = refs[:-10], refs[-10:]
    lay_out(parts, every)
    groups, cells, kinds, _ = out.shape
    orbs = groups * kinds
    me, group = meta[0], meta[1]

    def clear(i, c):
        slot_of[i] = -1
        rate[i] = 0.0
        return c

    lax.fori_loop(0, screening.shape[0], clear, 0)
    for q in range(2 * batch):
        rate[screening.shape[0] + q] = 0.0
    lane = lax.broadcasted_iota(jnp.int32, (1, LANES), 1) % orbs

    def rank(i, carry):
        found, lane_slot = carry
        level = levels[i]
        known = slot_of[level]
        slot = jnp.where(known < 0, found, known)
        slot_of[level] = slot
        rate[slot] = screening[level] * (-log2e)
        return found + (known < 0).astype(jnp.int32), jnp.where(lane == i, slot, lane_slot)

    n_levels, lane_slot = lax.fori_loop(0, orbs, rank, (jnp.int32(0), jnp.zeros((1, LANES), jnp.int32)))
    n_batches = (n_levels + batch - 1) // batch
    first_half = lax.broadcasted_iota(jnp.int32, (1, 2 * orbs), 1) < orbs

    def flip(v):
        high = v.astype(jnp.bfloat16).astype(jnp.float32)
        square = jnp.concatenate([high, v - high, jnp.zeros((LANES - 2 * orbs, LANES), jnp.float32)], axis=0)
        return square.T[:, : 2 * orbs].astype(jnp.bfloat16)

    for k in range(3):
        points, message = (points_before, own, points_after)[k], (before, mine, after)[k]
        there = lax.bitwise_xor(me, jnp.clip(me - 1 + k, 0, planes - 1))

        def prepare(c, carry):
            at = k * PLANE + c
            point = points[c]
            potential = point[3:4] + every[there, pl.ds(c, 1), :]
            v = cell_fields(message, c, groups, kinds) * (point[4:5] * potential)
            val[at] = flip(v)
            vh, vl = split(v)
            z_low = (me - 1 + k).astype(jnp.float32) * cell_side
            low = (*cell_low(c), z_low)
            wh, wl = split(weights(cst, point[0:1], point[1:2], point[2:3], low, (cell_side,) * 3))
            all_of = dot_bf16(jnp.concatenate([wh, wl], axis=0), jnp.concatenate([vh, vh, vl, vl], axis=0))
            m = all_of[:HALF] + all_of[HALF:]
            m = m[:, : 2 * orbs] + pltpu.roll(all_of[:HALF], 2 * orbs, 1)[:, : 2 * orbs]
            high = m.astype(jnp.bfloat16).astype(jnp.float32)
            mom[at] = jnp.where(first_half, high, m - high).astype(jnp.bfloat16)
            return carry

        lax.fori_loop(0, PLANE, prepare, 0, unroll=4)

    def put_plane(g, c):
        there = lax.bitwise_xor(me, g)
        rows = []
        for k in range(groups):
            row = lax.bitwise_xor(group, k) * kinds
            v = every[there, pl.ds(PLANE + lax.rem(row, orbs // 2), kinds), :]
            rows.append(jnp.where(row < orbs // 2, v, pltpu.roll(v, HALF, 1)))
        mom[3 * PLANE + g] = flip(jnp.concatenate(rows, axis=0))[:HALF]
        return c

    lax.fori_loop(0, planes, put_plane, 0)

    def put_near(j, slot):
        srcv[j] = val[slot]

    def put_far(j, first, second, live):
        srcv[j, :HALF, :] = mom[first]
        srcv[j, HALF:, :] = jnp.where(live, mom[second], jnp.zeros_like(mom[second]))

    def put_none(j):
        srcv[j] = jnp.zeros(srcv.shape[1:], srcv.dtype)

    def products(b, first):
        rates = [rate[b * batch + q] for q in range(batch)]
        rows = []
        for q in range(batch):
            tiles = [(jnp.exp2(dist[first + h] * rates[q]) * inv[first + h]).astype(jnp.bfloat16) for h in range(unit)]
            rows.append(jnp.concatenate(tiles, axis=1))
        v = jnp.concatenate([srcv[first + h] for h in range(unit)], axis=0)
        return jnp.dot(jnp.concatenate(rows, axis=0), v, preferred_element_type=jnp.float32)

    def per_cell(t, carry):
        cell = target_cell(group, t, groups)
        n_blocks = list_blocks(me, cell, counts, near, far, planes, put_near, put_far, put_none, unit)
        n_units = (n_blocks + unit - 1) // unit

        def measure(i, x):
            for u in range(unit):
                sq = squares[t, unit * i + u]
                r = lax.rsqrt(sq)
                inv[unit * i + u] = r
                dist[unit * i + u] = sq * r
            return x

        lax.fori_loop(0, n_units, measure, 0)

        def clear_acc(b, x):
            acc[b] = jnp.zeros(acc.shape[1:], jnp.float32)
            return x

        lax.fori_loop(0, n_batches, clear_acc, 0)

        def step(i, at):
            b, u = at
            for _ in range(steps):
                acc[b] = acc[b] + products(b, unit * u)
                wrap = u + 1 == n_units
                b, u = jnp.where(wrap, b + 1, b), jnp.where(wrap, 0, u + 1)
            return b, u

        lax.fori_loop(0, (n_batches * n_units + steps - 1) // steps, step, (jnp.int32(0), jnp.int32(0)))

        def choose(b, add):
            for q in range(batch):
                mine = lane_slot[:, : 2 * orbs] == b * batch + q
                add = add + jnp.where(mine, acc[b, q * LANES : (q + 1) * LANES, :], 0.0)
            return add

        total = lax.fori_loop(0, n_batches, choose, jnp.zeros((LANES, 2 * orbs), jnp.float32))
        flipped = jnp.concatenate([total, jnp.zeros((LANES, LANES - 2 * orbs), jnp.float32)], axis=1).T
        rows = (flipped[:orbs] + flipped[orbs : 2 * orbs]) * green_scale
        for k in range(groups):
            out[k, t] = rows[k * kinds : (k + 1) * kinds]
        return carry

    lax.fori_loop(0, cells, per_cell, 0)


def place_kernel(meta, *refs):
    parts, out, ordered = refs[:-2], refs[-2], refs[-1]
    for k, part in enumerate(parts):
        for t in range(part.shape[0]):
            ordered[target_cell(lax.bitwise_xor(meta[1], k), t, len(parts))] = part[t]
    for c in range(PLANE):
        out[:, c, :] = ordered[c]


def smem():
    return pl.BlockSpec(memory_space=pltpu.SMEM)


def vmem():
    return pl.BlockSpec(memory_space=pltpu.VMEM)


def call(kernel, name, out_shape, smems, args, scratch=(), mib=8):
    return pl.pallas_call(
        kernel,
        out_shape=out_shape,
        in_specs=[smem()] * smems + [vmem()] * (len(args) - smems),
        out_specs=jax.tree.map(lambda _: vmem(), out_shape),
        scratch_shapes=scratch,
        compiler_params=pltpu.CompilerParams(vmem_limit_bytes=mib * 1024 * 1024),
        name=name,
    )(*args)


def body(orbitals, points, quad_weight, external, screening, level_index, near_cells, far_cells):
    kinds, cells, point_count = orbitals.shape
    planes, groups = lax.axis_size("space"), lax.axis_size("orb")
    orbs = kinds * groups
    window = 3 * PLANE
    share = cells // groups
    me, group = lax.axis_index("space"), lax.axis_index("orb")
    meta = jnp.stack([me, group]).astype(jnp.int32)
    f32, bf16 = jnp.float32, jnp.bfloat16

    fields = gather_list(orbitals, "orb")
    weight = quad_weight * (cell_side**3 / point_count)
    own = jnp.concatenate(
        [jnp.transpose(points, (1, 0, 2)), external[:, None], weight[:, None], jnp.zeros((cells, 3, LANES), f32)], axis=1
    )
    marks = jnp.pad(level_index.astype(f32), (0, LANES - kinds))[None]
    ends = planes - 1
    up = [(i, i + 1) for i in range(ends)]
    down = [(i + 1, i) for i in range(ends)]
    cst = jnp.asarray(basis_rows())
    base_table = proxy_table(planes, window)
    shift = np.zeros(base_table.shape, np.float32)
    shift[:window, 2] = cell_side
    table = jnp.asarray(base_table) + jnp.asarray(shift) * (me - 1).astype(f32)
    counts = jnp.stack(
        [jnp.sum((near_cells >= 0).astype(jnp.int32), 1), jnp.sum((far_cells >= 0).astype(jnp.int32), 1)], axis=1
    )
    points_before, points_after = lax.ppermute(own, "space", up), lax.ppermute(own, "space", down)

    charges = call(
        charge_kernel, "charge", jax.ShapeDtypeStruct((2 * cells + ROWS, LANES), f32), 1, (meta, cst, own, *fields)
    )
    charges, (points_before, points_after) = gather_parts(charges, "space", False, (points_before, points_after))

    batch, unit, steps = 4, 4, 9
    most = near_cells.shape[1]
    blocks = most + (window - most + planes + 1) // 2 + 2 * unit
    squares = call(
        functools.partial(pairs_kernel, groups, planes, unit),
        "pairs",
        jax.ShapeDtypeStruct((share, blocks, LANES, LANES), f32),
        4,
        (meta, counts, near_cells, far_cells, table, points_before, own, points_after),
        [
            pltpu.VMEM((window, ROWS, LANES), f32),
            pltpu.VMEM((3, LANES, LANES), f32),
            pltpu.VMEM((blocks, ROWS, LANES), f32),
        ],
    )
    mine = jnp.concatenate([f.reshape(kinds * cells, LANES) for f in fields], axis=0)
    mine, squares = lax.optimization_barrier((mine, squares))
    before, after = lax.ppermute(mine, "space", up), lax.ppermute(mine, "space", down)
    shares = call(
        functools.partial(hartree_kernel, groups, kinds),
        "hartree",
        jax.ShapeDtypeStruct((1 + groups, ROWS, LANES), f32),
        4,
        (meta, counts, near_cells, far_cells, cst, marks, own, mine, squares, *charges),
        [
            pltpu.VMEM((planes, 2 * cells + ROWS, LANES), f32),
            pltpu.VMEM((window, 1, LANES), f32),
            pltpu.VMEM((window + planes, 1, LANES), f32),
            pltpu.VMEM((blocks, 1, LANES), f32),
        ],
    )
    shares = gather_list(shares, "orb")
    levels = jnp.concatenate([share[0, ROWS - 1, :kinds] for share in shares]).astype(jnp.int32)
    hartree, combined = call(
        functools.partial(combine_kernel, kinds),
        "combine",
        (jax.ShapeDtypeStruct((cells, LANES), f32), jax.ShapeDtypeStruct((cells + orbs // 2, LANES), f32)),
        1,
        (meta, *shares),
        [pltpu.VMEM((orbs, LANES), f32)],
    )
    gathered, _ = gather_parts(combined, "space", False)

    levels_at_most = -(-screening.shape[0] // batch) + 1
    sent = call(
        functools.partial(orbital_kernel, planes, batch, unit, steps),
        "orbitals",
        jax.ShapeDtypeStruct((groups, share, kinds, LANES), f32),
        6,
        (meta, counts, near_cells, far_cells, levels, screening, cst)
        + (points_before, own, points_after, before, mine, after, squares, *gathered),
        [
            pltpu.SMEM((screening.shape[0] + 2 * batch,), f32),
            pltpu.SMEM((screening.shape[0],), jnp.int32),
            pltpu.VMEM((planes, cells + orbs // 2, LANES), f32),
            pltpu.VMEM((window, LANES, 2 * orbs), bf16),
            pltpu.VMEM((window + planes, HALF, 2 * orbs), bf16),
            pltpu.VMEM((blocks, LANES, 2 * orbs), bf16),
            pltpu.VMEM((blocks, LANES, LANES), f32),
            pltpu.VMEM((blocks, LANES, LANES), f32),
            pltpu.VMEM((levels_at_most, batch * LANES, 2 * orbs), f32),
        ],
        24,
    )
    parts = [sent[0]]
    for k in range(1, groups):
        parts.append(lax.ppermute(sent[k], "orb", [(i, i ^ k) for i in range(groups)]))
    updated = call(
        place_kernel,
        "place",
        jax.ShapeDtypeStruct((kinds, cells, LANES), f32),
        1,
        (meta, *parts),
        [pltpu.VMEM((cells, kinds, LANES), f32)],
    )
    return updated, hartree


def solution(mesh):
    in_specs = (
        P("orb", "space", None),
        P(None, "space", None),
        P("space", None),
        P("space", None),
        P(),
        P("orb"),
        P("space", None),
        P("space", None),
    )
    out_specs = (P("orb", "space", None), P("space", None))
    return jax.shard_map(body, mesh=mesh, in_specs=in_specs, out_specs=out_specs, check_vma=False)
```

```python
import functools
import math

import jax
import jax.numpy as jnp
import numpy as np
from jax import lax
from jax.experimental import pallas as pl
from jax.experimental.pallas import tpu as pltpu
from jax.sharding import PartitionSpec as P

NODES = 4
LANES = 128
PLANE = 16
ROWS = 8
HALF = NODES**3

cell_side = 0.25
soften = 6.25e-06
green_scale = -0.5 / math.pi
log2e = math.log2(math.e)
highest = lax.Precision.HIGHEST

node_set = np.cos((2.0 * np.arange(NODES) + 1.0) * (math.pi / (2.0 * NODES)))
roots = [[node_set[m] for m in range(NODES) if m != a] for a in range(NODES)]
scales = [1.0 / np.prod([node_set[a] - r for r in roots[a]]) for a in range(NODES)]


def basis_rows():
    row = np.arange(ROWS)
    out = []
    for pick in (row // 4, 2 + row // 4, row % 4):
        for k in range(NODES - 1):
            out.append([roots[a][k] for a in pick])
        out.append([scales[a] for a in pick])
    return np.broadcast_to(np.array(out, np.float32)[:, :, None], (12, ROWS, LANES)).copy()


def proxy_table(planes, window):
    offset = 0.5 * (node_set + 1.0)
    p = np.arange(LANES) % HALF
    offs = np.stack([offset[p // 16], offset[p // 4 % 4], offset[p % 4]])
    cells = np.arange(window)
    lows = np.stack([cells % 4, cells // 4 % 4, cells // 16]) * cell_side
    near = lows[:, :, None] + offs[:, None, :] * cell_side
    levels = np.arange(planes)
    lows = np.stack([0 * levels, 0 * levels, levels]) * cell_side
    far = lows[:, :, None] + offs[:, None, :] * np.array([1.0, 1.0, cell_side])[:, None, None]
    table = np.zeros((window + planes, ROWS, LANES), np.float32)
    table[:, :3] = np.moveaxis(np.concatenate([near, far], 1), 0, 1)
    return table


def poly(u, r0, r1, r2, scale):
    return ((u - r0) * (u - r1)) * ((u - r2) * scale)


def weights(cst, x, y, z, lows, sides):
    ux, uy, uz = (
        jnp.broadcast_to(2.0 * (c - lo) / e - 1.0, (ROWS, LANES)) for c, lo, e in zip((x, y, z), lows, sides)
    )
    pz = poly(uz, cst[8], cst[9], cst[10], cst[11])
    pyz = [poly(uy, cst[4 * k], cst[4 * k + 1], cst[4 * k + 2], cst[4 * k + 3]) * pz for k in range(2)]
    parts = []
    for a in range(NODES):
        px = poly(ux, *(float(r) for r in roots[a]), float(scales[a]))
        parts += [px * pyz[0], px * pyz[1]]
    return jnp.concatenate(parts, axis=0)


def twice(w):
    return jnp.concatenate([w, w], axis=0)


def cell_low(cell):
    return [(cell % 4).astype(jnp.float32) * cell_side, (cell // 4 % 4).astype(jnp.float32) * cell_side]


def dot_nt(a, b):
    return lax.dot_general(a, b, (((1,), (1,)), ((), ())), precision=highest, preferred_element_type=jnp.float32)


def gather_parts(block, axis, pairs, later=None):
    count = lax.axis_size(axis)
    parts = [block[None]]
    while sum(p.shape[0] for p in parts) < count:
        held = parts[0] if len(parts) == 1 else jnp.concatenate(parts, axis=0)
        have = held.shape[0]
        steps = range(1, 4 if (have > 1 or pairs) and have * 4 <= count else 2)
        parts = [held] + [lax.ppermute(held, axis, [(i, i ^ (have * j)) for i in range(count)]) for j in steps]
        if later is not None and have == 1:
            parts[1], later = lax.optimization_barrier((parts[1], later))
    return parts, later


def gather_list(block, axis):
    parts, _ = gather_parts(block, axis, True)
    return [p[k] for p in parts for k in range(p.shape[0])]


def lay_out(parts, whole):
    at = 0
    for part in parts:
        for k in range(part.shape[0]):
            whole[at + k] = part[k]
        at += part.shape[0]


def target_cell(me, t, groups):
    return t * groups + lax.bitwise_xor(jnp.int32(t) if isinstance(t, int) else t, me)


def split(v):
    high = v.astype(jnp.bfloat16)
    return high, (v - high.astype(jnp.float32)).astype(jnp.bfloat16)


def dot_bf16(a, b):
    return lax.dot_general(a, b, (((1,), (1,)), ((), ())), preferred_element_type=jnp.float32)


def dot_split(v, w):
    vh, vl = split(v)
    wh, wl = split(w)
    rows = v.shape[0]
    both = dot_bf16(jnp.concatenate([vh, vl], axis=0), wh)
    return both[:rows] + both[rows:] + dot_bf16(vh, wl)


def charge_kernel(meta, cst, own, *refs):
    z_low = meta[0].astype(jnp.float32) * cell_side
    fields, out = refs[:-1], refs[-1]
    density = jnp.zeros((PLANE, LANES), jnp.float32)
    for phi in fields:
        for j in range(phi.shape[0]):
            v = phi[j]
            density = density + v * v
    out[:PLANE, :] = density
    acc = jnp.zeros((HALF, LANES), jnp.float32)
    ones = jnp.ones((ROWS, LANES), jnp.float32)
    for c in range(PLANE):
        charge = own[c, 4:5, :] * (2.0 * out[c : c + 1, :])
        out[c : c + 1, :] = charge
        x, y, z = own[c, 0:1, :], own[c, 1:2, :], own[c, 2:3, :]
        low = (cell_side * (c % 4), cell_side * (c // 4), z_low)
        acc = acc + weights(cst, x, y, z, (0.0, 0.0, z_low), (1.0, 1.0, cell_side)) * charge
        moments = dot_nt(ones, twice(weights(cst, x, y, z, low, (cell_side,) * 3) * charge))
        out[PLANE + c : PLANE + c + 1, :] = moments[0:1, :]
    out[2 * PLANE :, :] = dot_nt(ones, twice(acc))


def live_planes(me, planes):
    below = jnp.maximum(me - 1, 0)
    return below, below + jnp.maximum(planes - 2 - me, 0)


def list_blocks(me, cell, counts, near, far, planes, put_near, put_far, put_none, multiple):
    window = 3 * PLANE
    base = (me - 1) * PLANE
    below, n_planes = live_planes(me, planes)
    n_near, n_far = counts[cell, 0], counts[cell, 1]
    n_items = n_far + n_planes
    n_pairs = (n_items + 1) // 2

    def near_step(j, c):
        put_near(j, near[cell, j] - base)
        return c

    lax.fori_loop(0, n_near, near_step, 0)

    def item(j):
        j = jnp.minimum(j, n_items - 1)
        p = j - n_far
        level = jnp.where(p < below, p, p + (me + 2 - below))
        slot = far[cell, jnp.minimum(j, far.shape[1] - 1)] - base
        return jnp.where(j < n_far, slot, window + level)

    def far_step(j, c):
        put_far(n_near + j, item(2 * j), item(2 * j + 1), 2 * j + 1 < n_items)
        return c

    lax.fori_loop(0, n_pairs, far_step, 0)
    for u in range(multiple - 1):
        put_none(n_near + n_pairs + u)
    return n_near + n_pairs


def in_low_half():
    return lax.broadcasted_iota(jnp.int32, (1, LANES), 1) < HALF


def put_targets(pts, cell, tgt):
    for d in range(3):
        tgt[d] = jnp.broadcast_to(pts[PLANE + cell, d : d + 1, :], (LANES, LANES)).T


def each_square(tgt, src, first, count, use):
    sources = [[src[first + u, d : d + 1, :] for d in range(3)] for u in range(count)]
    for r in range(LANES // ROWS):
        at = [tgt[d, r * ROWS : (r + 1) * ROWS, :] for d in range(3)]
        for u in range(count):
            dx, dy, dz = (a - b for a, b in zip(at, sources[u]))
            use(r, u, (dx * dx + dy * dy) + (dz * dz + soften))


def lay_points(windows, pts):
    for k, points in enumerate(windows):
        pts[k * PLANE : (k + 1) * PLANE] = points[...]


def cell_fields(message, c, groups, kinds):
    rows = kinds * PLANE
    return jnp.concatenate([message[pl.ds(g * rows + c, kinds, stride=PLANE), :] for g in range(groups)], axis=0)


def hartree_kernel(
    groups, kinds, unroll, meta, counts, near, far, cst, table, marks, points_before, own, points_after, mine, *refs
):
    parts, (out, every, pts, tgt, src, val, mom, srcv) = refs[:-8], refs[-8:]
    lay_out(parts, every)
    lay_points((points_before, own, points_after), pts)
    planes = every.shape[0]
    cells = PLANE // groups
    me, group = meta[0], meta[1]
    for k in range(3):
        there = lax.bitwise_xor(me, jnp.clip(me - 1 + k, 0, planes - 1))
        val[k * PLANE : (k + 1) * PLANE, 0, :] = every[there, :PLANE, :]
        mom[k * PLANE : (k + 1) * PLANE, 0, :] = every[there, PLANE : 2 * PLANE, :]

    def put_plane(g, c):
        mom[3 * PLANE + g] = every[lax.bitwise_xor(me, g), 2 * PLANE : 2 * PLANE + 1, :]
        return c

    lax.fori_loop(0, planes, put_plane, 0)
    low_half = in_low_half()

    def put_near(j, slot):
        src[j] = pts[slot]
        srcv[j] = val[slot]

    def put_far(j, first, second, live):
        src[j] = jnp.where(low_half, table[first], table[second])
        srcv[j] = jnp.where(low_half, mom[first], mom[second] * live.astype(jnp.float32))

    def put_none(j):
        src[j] = jnp.zeros(src.shape[1:], jnp.float32)
        srcv[j] = jnp.zeros((1, LANES), jnp.float32)

    z_low = me.astype(jnp.float32) * cell_side
    total = jnp.zeros((groups * kinds, LANES), jnp.float32)
    out[0] = jnp.broadcast_to(marks[...], (ROWS, LANES))
    for t in range(cells):
        cell = target_cell(group, t, groups)
        n_blocks = list_blocks(me, cell, counts, near, far, planes, put_near, put_far, put_none, unroll)
        put_targets(pts, cell, tgt)

        def step(i, accs):
            accs = list(accs)
            charges = [srcv[unroll * i + u] for u in range(unroll)]

            def use(r, u, sq):
                accs[r] = accs[r] + lax.rsqrt(sq) * charges[u]

            each_square(tgt, src, unroll * i, unroll, use)
            return tuple(accs)

        zero = jnp.zeros((ROWS, LANES), jnp.float32)
        accs = lax.fori_loop(0, (n_blocks + unroll - 1) // unroll, step, (zero,) * (LANES // ROWS))
        acc = jnp.concatenate(accs, axis=0)
        row = dot_nt(jnp.ones((ROWS, LANES), jnp.float32), acc)[0:1, :]
        out[0, t : t + 1, :] = row
        point = own[cell]
        scaled = point[4:5] * (point[3:4] + row)
        v = cell_fields(mine, cell, groups, kinds) * scaled
        w = weights(cst, point[0:1], point[1:2], point[2:3], (0.0, 0.0, z_low), (1.0, 1.0, cell_side))
        total = total + dot_split(v, twice(w))
    for k in range(groups):
        out[1 + lax.bitwise_xor(group, k), :kinds, :] = total[k * kinds : (k + 1) * kinds, :]


def combine_kernel(kinds, meta, *refs):
    shares, (hartree, out, total) = refs[:-3], refs[-3:]
    groups = len(shares)
    for k, share in enumerate(shares):
        for t in range(PLANE // groups):
            cell = target_cell(lax.bitwise_xor(meta[1], k), t, groups)
            out[pl.ds(cell, 1), :] = share[0, t : t + 1, :]
    hartree[...] = out[:PLANE, :]
    for g in range(groups):
        added = shares[0][1 + g, :kinds, :]
        for share in shares[1:]:
            added = added + share[1 + g, :kinds, :]
        total[g * kinds : (g + 1) * kinds, :] = added
    rows = groups * kinds // 2
    low_half = lax.broadcasted_iota(jnp.int32, (1, LANES), 1) < HALF
    out[PLANE:, :] = jnp.where(low_half, total[:rows, :], total[rows:, :])


def orbital_kernel(
    planes, batch, unit, steps, meta, counts, near, far, levels, screening, cst, table,
    points_before, own, points_after, before, mine, after, *refs,
):
    parts, (out, rate, slot_of, every, pts, tgt, src, val, mom, srcv, dist, inv, acc) = refs[:-13], refs[-13:]
    lay_out(parts, every)
    lay_points((points_before, own, points_after), pts)
    low_half = in_low_half()
    groups, cells, kinds, _ = out.shape
    orbs = groups * kinds
    me, group = meta[0], meta[1]

    def clear(i, c):
        slot_of[i] = -1
        rate[i] = 0.0
        return c

    lax.fori_loop(0, screening.shape[0], clear, 0)
    for q in range(2 * batch):
        rate[screening.shape[0] + q] = 0.0
    lane = lax.broadcasted_iota(jnp.int32, (1, LANES), 1) % orbs

    def rank(i, carry):
        found, lane_slot = carry
        level = levels[i]
        known = slot_of[level]
        slot = jnp.where(known < 0, found, known)
        slot_of[level] = slot
        rate[slot] = screening[level] * (-log2e)
        return found + (known < 0).astype(jnp.int32), jnp.where(lane == i, slot, lane_slot)

    n_levels, lane_slot = lax.fori_loop(0, orbs, rank, (jnp.int32(0), jnp.zeros((1, LANES), jnp.int32)))
    n_batches = (n_levels + batch - 1) // batch
    first_half = lax.broadcasted_iota(jnp.int32, (1, 2 * orbs), 1) < orbs

    def flip(v):
        high = v.astype(jnp.bfloat16).astype(jnp.float32)
        square = jnp.concatenate([high, v - high, jnp.zeros((LANES - 2 * orbs, LANES), jnp.float32)], axis=0)
        return square.T[:, : 2 * orbs].astype(jnp.bfloat16)

    for k in range(3):
        message = (before, mine, after)[k]
        there = lax.bitwise_xor(me, jnp.clip(me - 1 + k, 0, planes - 1))

        def prepare(c, carry):
            at = k * PLANE + c
            point = pts[at]
            potential = point[3:4] + every[there, pl.ds(c, 1), :]
            v = cell_fields(message, c, groups, kinds) * (point[4:5] * potential)
            val[at] = flip(v)
            vh, vl = split(v)
            z_low = (me - 1 + k).astype(jnp.float32) * cell_side
            low = (*cell_low(c), z_low)
            wh, wl = split(weights(cst, point[0:1], point[1:2], point[2:3], low, (cell_side,) * 3))
            all_of = dot_bf16(jnp.concatenate([wh, wl], axis=0), jnp.concatenate([vh, vh, vl, vl], axis=0))
            m = all_of[:HALF] + all_of[HALF:]
            m = m[:, : 2 * orbs] + pltpu.roll(all_of[:HALF], 2 * orbs, 1)[:, : 2 * orbs]
            high = m.astype(jnp.bfloat16).astype(jnp.float32)
            mom[at] = jnp.where(first_half, high, m - high).astype(jnp.bfloat16)
            return carry

        lax.fori_loop(0, PLANE, prepare, 0, unroll=4)

    def put_plane(g, c):
        there = lax.bitwise_xor(me, g)
        rows = []
        for k in range(groups):
            row = lax.bitwise_xor(group, k) * kinds
            v = every[there, pl.ds(PLANE + lax.rem(row, orbs // 2), kinds), :]
            rows.append(jnp.where(row < orbs // 2, v, pltpu.roll(v, HALF, 1)))
        mom[3 * PLANE + g] = flip(jnp.concatenate(rows, axis=0))[:HALF]
        return c

    lax.fori_loop(0, planes, put_plane, 0)

    def put_near(j, slot):
        src[j] = pts[slot]
        srcv[j] = val[slot]

    def put_far(j, first, second, live):
        src[j] = jnp.where(low_half, table[first], table[second])
        srcv[j, :HALF, :] = mom[first]
        srcv[j, HALF:, :] = jnp.where(live, mom[second], jnp.zeros_like(mom[second]))

    def put_none(j):
        src[j] = jnp.zeros(src.shape[1:], jnp.float32)
        srcv[j] = jnp.zeros(srcv.shape[1:], srcv.dtype)

    def products(b, first):
        rates = [rate[b * batch + q] for q in range(batch)]
        rows = []
        for q in range(batch):
            tiles = [(jnp.exp2(dist[first + h] * rates[q]) * inv[first + h]).astype(jnp.bfloat16) for h in range(unit)]
            rows.append(jnp.concatenate(tiles, axis=1))
        v = jnp.concatenate([srcv[first + h] for h in range(unit)], axis=0)
        return jnp.dot(jnp.concatenate(rows, axis=0), v, preferred_element_type=jnp.float32)

    def per_cell(t, carry):
        cell = target_cell(group, t, groups)
        n_blocks = list_blocks(me, cell, counts, near, far, planes, put_near, put_far, put_none, unit)
        n_units = (n_blocks + unit - 1) // unit

        put_targets(pts, cell, tgt)

        def measure(i, x):
            def use(r, u, sq):
                one_over = lax.rsqrt(sq)
                inv[unit * i + u, r * ROWS : (r + 1) * ROWS, :] = one_over
                dist[unit * i + u, r * ROWS : (r + 1) * ROWS, :] = sq * one_over

            each_square(tgt, src, unit * i, unit, use)
            return x

        lax.fori_loop(0, n_units, measure, 0)

        def clear_acc(b, x):
            acc[b] = jnp.zeros(acc.shape[1:], jnp.float32)
            return x

        lax.fori_loop(0, n_batches, clear_acc, 0)

        def step(i, at):
            b, u = at
            for _ in range(steps):
                acc[b] = acc[b] + products(b, unit * u)
                wrap = u + 1 == n_units
                b, u = jnp.where(wrap, b + 1, b), jnp.where(wrap, 0, u + 1)
            return b, u

        lax.fori_loop(0, (n_batches * n_units + steps - 1) // steps, step, (jnp.int32(0), jnp.int32(0)))

        def choose(b, add):
            for q in range(batch):
                mine = lane_slot[:, : 2 * orbs] == b * batch + q
                add = add + jnp.where(mine, acc[b, q * LANES : (q + 1) * LANES, :], 0.0)
            return add

        total = lax.fori_loop(0, n_batches, choose, jnp.zeros((LANES, 2 * orbs), jnp.float32))
        flipped = jnp.concatenate([total, jnp.zeros((LANES, LANES - 2 * orbs), jnp.float32)], axis=1).T
        rows = (flipped[:orbs] + flipped[orbs : 2 * orbs]) * green_scale
        for k in range(groups):
            out[k, t] = rows[k * kinds : (k + 1) * kinds]
        return carry

    lax.fori_loop(0, cells, per_cell, 0)


def place_kernel(meta, *refs):
    parts, out, ordered = refs[:-2], refs[-2], refs[-1]
    for k, part in enumerate(parts):
        for t in range(part.shape[0]):
            ordered[target_cell(lax.bitwise_xor(meta[1], k), t, len(parts))] = part[t]
    for c in range(PLANE):
        out[:, c, :] = ordered[c]


def smem():
    return pl.BlockSpec(memory_space=pltpu.SMEM)


def vmem():
    return pl.BlockSpec(memory_space=pltpu.VMEM)


def call(kernel, name, out_shape, smems, args, scratch=(), mib=8):
    return pl.pallas_call(
        kernel,
        out_shape=out_shape,
        in_specs=[smem()] * smems + [vmem()] * (len(args) - smems),
        out_specs=jax.tree.map(lambda _: vmem(), out_shape),
        scratch_shapes=scratch,
        compiler_params=pltpu.CompilerParams(vmem_limit_bytes=mib * 1024 * 1024),
        name=name,
    )(*args)


def body(orbitals, points, quad_weight, external, screening, level_index, near_cells, far_cells):
    kinds, cells, point_count = orbitals.shape
    planes, groups = lax.axis_size("space"), lax.axis_size("orb")
    orbs = kinds * groups
    window = 3 * PLANE
    share = cells // groups
    me, group = lax.axis_index("space"), lax.axis_index("orb")
    meta = jnp.stack([me, group]).astype(jnp.int32)
    f32, bf16 = jnp.float32, jnp.bfloat16

    fields = gather_list(orbitals, "orb")
    weight = quad_weight * (cell_side**3 / point_count)
    own = jnp.concatenate(
        [jnp.transpose(points, (1, 0, 2)), external[:, None], weight[:, None], jnp.zeros((cells, 3, LANES), f32)], axis=1
    )
    marks = jnp.pad(level_index.astype(f32), (0, LANES - kinds))[None]
    ends = planes - 1
    up = [(i, i + 1) for i in range(ends)]
    down = [(i + 1, i) for i in range(ends)]
    cst = jnp.asarray(basis_rows())
    base_table = proxy_table(planes, window)
    shift = np.zeros(base_table.shape, np.float32)
    shift[:window, 2] = cell_side
    table = jnp.asarray(base_table) + jnp.asarray(shift) * (me - 1).astype(f32)
    counts = jnp.stack(
        [jnp.sum((near_cells >= 0).astype(jnp.int32), 1), jnp.sum((far_cells >= 0).astype(jnp.int32), 1)], axis=1
    )
    charges = call(
        charge_kernel, "charge", jax.ShapeDtypeStruct((2 * cells + ROWS, LANES), f32), 1, (meta, cst, own, *fields)
    )
    mine = jnp.concatenate([f.reshape(kinds * cells, LANES) for f in fields], axis=0)
    charges, (own, mine) = gather_parts(charges, "space", False, (own, mine))
    points_before, points_after = lax.ppermute(own, "space", up), lax.ppermute(own, "space", down)
    before, after = lax.ppermute(mine, "space", up), lax.ppermute(mine, "space", down)

    batch, unit, steps = 4, 4, 9
    most = near_cells.shape[1]
    blocks = most + (window - most + planes + 1) // 2 + 2 * unit
    geometry = [
        pltpu.VMEM((window, ROWS, LANES), f32),
        pltpu.VMEM((3, LANES, LANES), f32),
        pltpu.VMEM((blocks, ROWS, LANES), f32),
    ]
    shares = call(
        functools.partial(hartree_kernel, groups, kinds, unit),
        "hartree",
        jax.ShapeDtypeStruct((1 + groups, ROWS, LANES), f32),
        4,
        (meta, counts, near_cells, far_cells, cst, table, marks, points_before, own, points_after, mine, *charges),
        [pltpu.VMEM((planes, 2 * cells + ROWS, LANES), f32)]
        + geometry
        + [
            pltpu.VMEM((window, 1, LANES), f32),
            pltpu.VMEM((window + planes, 1, LANES), f32),
            pltpu.VMEM((blocks, 1, LANES), f32),
        ],
        12,
    )
    shares = gather_list(shares, "orb")
    levels = jnp.concatenate([share[0, ROWS - 1, :kinds] for share in shares]).astype(jnp.int32)
    hartree, combined = call(
        functools.partial(combine_kernel, kinds),
        "combine",
        (jax.ShapeDtypeStruct((cells, LANES), f32), jax.ShapeDtypeStruct((cells + orbs // 2, LANES), f32)),
        1,
        (meta, *shares),
        [pltpu.VMEM((orbs, LANES), f32)],
    )
    gathered, _ = gather_parts(combined, "space", False)

    levels_at_most = -(-screening.shape[0] // batch) + 1
    sent = call(
        functools.partial(orbital_kernel, planes, batch, unit, steps),
        "orbitals",
        jax.ShapeDtypeStruct((groups, share, kinds, LANES), f32),
        6,
        (meta, counts, near_cells, far_cells, levels, screening, cst, table)
        + (points_before, own, points_after, before, mine, after, *gathered),
        [
            pltpu.SMEM((screening.shape[0] + 2 * batch,), f32),
            pltpu.SMEM((screening.shape[0],), jnp.int32),
            pltpu.VMEM((planes, cells + orbs // 2, LANES), f32),
            *geometry,
            pltpu.VMEM((window, LANES, 2 * orbs), bf16),
            pltpu.VMEM((window + planes, HALF, 2 * orbs), bf16),
            pltpu.VMEM((blocks, LANES, 2 * orbs), bf16),
            pltpu.VMEM((blocks, LANES, LANES), f32),
            pltpu.VMEM((blocks, LANES, LANES), f32),
            pltpu.VMEM((levels_at_most, batch * LANES, 2 * orbs), f32),
        ],
        24,
    )
    parts = [sent[0]]
    for k in range(1, groups):
        parts.append(lax.ppermute(sent[k], "orb", [(i, i ^ k) for i in range(groups)]))
    updated = call(
        place_kernel,
        "place",
        jax.ShapeDtypeStruct((kinds, cells, LANES), f32),
        1,
        (meta, *parts),
        [pltpu.VMEM((cells, kinds, LANES), f32)],
    )
    return updated, hartree


def solution(mesh):
    in_specs = (
        P("orb", "space", None),
        P(None, "space", None),
        P("space", None),
        P("space", None),
        P(),
        P("orb"),
        P("space", None),
        P("space", None),
    )
    out_specs = (P("orb", "space", None), P("space", None))
    return jax.shard_map(body, mesh=mesh, in_specs=in_specs, out_specs=out_specs, check_vma=False)
```

```python
import functools
import math

import jax
import jax.numpy as jnp
import numpy as np
from jax import lax
from jax.experimental import pallas as pl
from jax.experimental.pallas import tpu as pltpu
from jax.sharding import PartitionSpec as P

NODES = 4
LANES = 128
PLANE = 16
ROWS = 8
HALF = NODES**3

cell_side = 0.25
soften = 6.25e-06
green_scale = -0.5 / math.pi
log2e = math.log2(math.e)
highest = lax.Precision.HIGHEST

node_set = np.cos((2.0 * np.arange(NODES) + 1.0) * (math.pi / (2.0 * NODES)))
roots = [[node_set[m] for m in range(NODES) if m != a] for a in range(NODES)]
scales = [1.0 / np.prod([node_set[a] - r for r in roots[a]]) for a in range(NODES)]


def basis_rows():
    row = np.arange(ROWS)
    out = []
    for pick in (row // 4, 2 + row // 4, row % 4):
        for k in range(NODES - 1):
            out.append([roots[a][k] for a in pick])
        out.append([scales[a] for a in pick])
    return np.broadcast_to(np.array(out, np.float32)[:, :, None], (12, ROWS, LANES)).copy()


def proxy_table(planes, window):
    offset = 0.5 * (node_set + 1.0)
    p = np.arange(LANES) % HALF
    offs = np.stack([offset[p // 16], offset[p // 4 % 4], offset[p % 4]])
    cells = np.arange(window)
    lows = np.stack([cells % 4, cells // 4 % 4, cells // 16]) * cell_side
    near = lows[:, :, None] + offs[:, None, :] * cell_side
    levels = np.arange(planes)
    lows = np.stack([0 * levels, 0 * levels, levels]) * cell_side
    far = lows[:, :, None] + offs[:, None, :] * np.array([1.0, 1.0, cell_side])[:, None, None]
    table = np.zeros((window + planes, ROWS, LANES), np.float32)
    table[:, :3] = np.moveaxis(np.concatenate([near, far], 1), 0, 1)
    return table


def poly(u, r0, r1, r2, scale):
    return ((u - r0) * (u - r1)) * ((u - r2) * scale)


def weights(cst, x, y, z, lows, sides):
    ux, uy, uz = (
        jnp.broadcast_to(2.0 * (c - lo) / e - 1.0, (ROWS, LANES)) for c, lo, e in zip((x, y, z), lows, sides)
    )
    pz = poly(uz, cst[8], cst[9], cst[10], cst[11])
    pyz = [poly(uy, cst[4 * k], cst[4 * k + 1], cst[4 * k + 2], cst[4 * k + 3]) * pz for k in range(2)]
    parts = []
    for a in range(NODES):
        px = poly(ux, *(float(r) for r in roots[a]), float(scales[a]))
        parts += [px * pyz[0], px * pyz[1]]
    return jnp.concatenate(parts, axis=0)


def twice(w):
    return jnp.concatenate([w, w], axis=0)


def cell_low(cell):
    return [(cell % 4).astype(jnp.float32) * cell_side, (cell // 4 % 4).astype(jnp.float32) * cell_side]


def dot_nt(a, b):
    return lax.dot_general(a, b, (((1,), (1,)), ((), ())), precision=highest, preferred_element_type=jnp.float32)


def gather_parts(block, axis, pairs):
    count = lax.axis_size(axis)
    parts = [block[None]]
    while sum(p.shape[0] for p in parts) < count:
        held = parts[0] if len(parts) == 1 else jnp.concatenate(parts, axis=0)
        have = held.shape[0]
        steps = range(1, 4 if (have > 1 or pairs) and have * 4 <= count else 2)
        parts = [held] + [lax.ppermute(held, axis, [(i, i ^ (have * j)) for i in range(count)]) for j in steps]
    return parts


def gather_list(block, axis):
    parts = gather_parts(block, axis, True)
    return [p[k] for p in parts for k in range(p.shape[0])]


def lay_out(parts, whole):
    at = 0
    for part in parts:
        for k in range(part.shape[0]):
            whole[at + k] = part[k]
        at += part.shape[0]


def target_cell(me, t, groups):
    return t * groups + lax.bitwise_xor(jnp.int32(t) if isinstance(t, int) else t, me)


def split(v):
    high = v.astype(jnp.bfloat16)
    return high, (v - high.astype(jnp.float32)).astype(jnp.bfloat16)


def dot_bf16(a, b):
    return lax.dot_general(a, b, (((1,), (1,)), ((), ())), preferred_element_type=jnp.float32)


def dot_split(v, w):
    vh, vl = split(v)
    wh, wl = split(w)
    rows = v.shape[0]
    both = dot_bf16(jnp.concatenate([vh, vl], axis=0), wh)
    return both[:rows] + both[rows:] + dot_bf16(vh, wl)


def lane_sums(v):
    high, low = split(v)
    ones = jnp.ones((ROWS, 2 * v.shape[1]), jnp.bfloat16)
    return dot_bf16(ones, jnp.concatenate([high, low], axis=1))[0:1, :]


def charge_kernel(meta, cst, own, *refs):
    z_low = meta[0].astype(jnp.float32) * cell_side
    fields, (out, density) = refs[:-2], refs[-2:]
    total = jnp.zeros((PLANE, LANES), jnp.float32)
    for phi in fields:
        for j in range(phi.shape[0]):
            v = phi[j]
            total = total + v * v
    density[...] = 2.0 * total
    acc = jnp.zeros((HALF, LANES), jnp.float32)
    for c in range(PLANE):
        point = own[c]
        charge = point[4:5] * density[c : c + 1, :]
        low = (cell_side * (c % 4), cell_side * (c // 4), z_low)
        acc = acc + weights(cst, point[0:1], point[1:2], point[2:3], (0.0, 0.0, z_low), (1.0, 1.0, cell_side)) * charge
        moments = lane_sums(weights(cst, point[0:1], point[1:2], point[2:3], low, (cell_side,) * 3) * charge)
        out[c, :5, :] = point[:5]
        out[c, 5:6, :] = charge
        out[c, 6:7, :] = jnp.concatenate([moments, moments], axis=1)
    moments = lane_sums(acc)
    for c in range(PLANE):
        out[c, 7:8, :] = jnp.concatenate([moments, moments], axis=1)


def live_planes(me, planes):
    below = jnp.maximum(me - 1, 0)
    return below, below + jnp.maximum(planes - 2 - me, 0)


def list_blocks(me, cell, counts, near, far, planes, put_near, put_far, put_none, multiple):
    window = 3 * PLANE
    base = (me - 1) * PLANE
    below, n_planes = live_planes(me, planes)
    n_near, n_far = counts[cell, 0], counts[cell, 1]
    n_items = n_far + n_planes
    n_pairs = (n_items + 1) // 2

    def near_step(j, c):
        put_near(j, near[cell, j] - base)
        return c

    lax.fori_loop(0, n_near, near_step, 0)

    def item(j):
        j = jnp.minimum(j, n_items - 1)
        p = j - n_far
        level = jnp.where(p < below, p, p + (me + 2 - below))
        slot = far[cell, jnp.minimum(j, far.shape[1] - 1)] - base
        return jnp.where(j < n_far, slot, window + level)

    def far_step(j, c):
        put_far(n_near + j, item(2 * j), item(2 * j + 1), 2 * j + 1 < n_items)
        return c

    lax.fori_loop(0, n_pairs, far_step, 0)
    for u in range(multiple - 1):
        put_none(n_near + n_pairs + u)
    return n_near + n_pairs


def in_low_half():
    return lax.broadcasted_iota(jnp.int32, (1, LANES), 1) < HALF


def put_targets(pts, cell, tgt):
    for d in range(3):
        tgt[d] = jnp.broadcast_to(pts[PLANE + cell, d : d + 1, :], (LANES, LANES)).T


def each_square(tgt, src, first, count, use):
    sources = [[src[first + u, d : d + 1, :] for d in range(3)] for u in range(count)]
    for r in range(LANES // ROWS):
        at = [tgt[d, r * ROWS : (r + 1) * ROWS, :] for d in range(3)]
        for u in range(count):
            dx, dy, dz = (a - b for a, b in zip(at, sources[u]))
            use(r, u, (dx * dx + dy * dy) + (dz * dz + soften))


def cell_fields(message, c, groups, kinds):
    rows = kinds * PLANE
    return jnp.concatenate([message[pl.ds(g * rows + c, kinds, stride=PLANE), :] for g in range(groups)], axis=0)


def hartree_kernel(groups, kinds, unroll, meta, counts, near, far, cst, table, marks, mine, *refs):
    parts, (out, pts, src, every, items, tgt) = refs[:-6], refs[-6:]
    lay_out(parts, every)
    planes = every.shape[0]
    cells = PLANE // groups
    me, group = meta[0], meta[1]
    window = 3 * PLANE
    for k in range(3):
        there = lax.bitwise_xor(me, jnp.clip(me - 1 + k, 0, planes - 1))
        for c in range(PLANE):
            pts[k * PLANE + c] = every[there, c]
    row = lax.broadcasted_iota(jnp.int32, (ROWS, 1), 0)

    def put_cell(c, carry):
        items[c] = jnp.where(row == 5, pts[c, 6:7, :], table[c])
        return carry

    lax.fori_loop(0, window, put_cell, 0, unroll=8)

    def put_plane(g, c):
        items[window + g] = jnp.where(row == 5, every[lax.bitwise_xor(me, g), 0, 7:8, :], table[window + g])
        return c

    lax.fori_loop(0, planes, put_plane, 0)
    items[window + planes] = jnp.zeros((ROWS, LANES), jnp.float32)
    low_half = in_low_half()
    z_low = me.astype(jnp.float32) * cell_side
    total = jnp.zeros((groups * kinds, LANES), jnp.float32)
    out[0] = jnp.broadcast_to(marks[...], (ROWS, LANES))
    for t in range(cells):
        cell = target_cell(group, t, groups)

        def put_near(j, slot):
            src[t, j] = pts[slot]

        def put_far(j, first, second, live):
            src[t, j] = jnp.where(low_half, items[first], items[jnp.where(live, second, window + planes)])

        def put_none(j):
            src[t, j] = jnp.zeros((ROWS, LANES), jnp.float32)

        n_blocks = list_blocks(me, cell, counts, near, far, planes, put_near, put_far, put_none, unroll)
        put_targets(pts, cell, tgt)

        def step(i, accs):
            accs = list(accs)
            charges = [src[t, unroll * i + u, 5:6, :] for u in range(unroll)]

            def use(r, u, sq):
                accs[r] = accs[r] + lax.rsqrt(sq) * charges[u]

            each_square(tgt, src.at[t], unroll * i, unroll, use)
            return tuple(accs)

        zero = jnp.zeros((ROWS, LANES), jnp.float32)
        accs = lax.fori_loop(0, (n_blocks + unroll - 1) // unroll, step, (zero,) * (LANES // ROWS))
        potential = dot_nt(jnp.ones((ROWS, LANES), jnp.float32), jnp.concatenate(accs, axis=0))[0:1, :]
        out[0, t : t + 1, :] = potential
        point = pts[PLANE + cell]
        scaled = point[4:5] * (point[3:4] + potential)
        v = cell_fields(mine, cell, groups, kinds) * scaled
        w = weights(cst, point[0:1], point[1:2], point[2:3], (0.0, 0.0, z_low), (1.0, 1.0, cell_side))
        total = total + dot_split(v, twice(w))
    for k in range(groups):
        out[1 + lax.bitwise_xor(group, k), :kinds, :] = total[k * kinds : (k + 1) * kinds, :]


def pairs_kernel(groups, planes, unroll, meta, counts, pts, src, dist, inv, tgt):
    group = meta[1]
    _, n_planes = live_planes(meta[0], planes)

    def per_cell(t, carry):
        cell = target_cell(group, t, groups)
        put_targets(pts, cell, tgt)
        n_blocks = counts[cell, 0] + (counts[cell, 1] + n_planes + 1) // 2

        def measure(i, x):
            def use(r, u, sq):
                one_over = lax.rsqrt(sq)
                inv[t, unroll * i + u, r * ROWS : (r + 1) * ROWS, :] = one_over
                dist[t, unroll * i + u, r * ROWS : (r + 1) * ROWS, :] = sq * one_over

            each_square(tgt, src.at[t], unroll * i, unroll, use)
            return x

        lax.fori_loop(0, (n_blocks + unroll - 1) // unroll, measure, 0)
        return carry

    lax.fori_loop(0, PLANE // groups, per_cell, 0)


def combine_kernel(kinds, meta, *refs):
    shares, (hartree, out, total) = refs[:-3], refs[-3:]
    groups = len(shares)
    for k, share in enumerate(shares):
        for t in range(PLANE // groups):
            cell = target_cell(lax.bitwise_xor(meta[1], k), t, groups)
            out[pl.ds(cell, 1), :] = share[0, t : t + 1, :]
    hartree[...] = out[:PLANE, :]
    for g in range(groups):
        added = shares[0][1 + g, :kinds, :]
        for share in shares[1:]:
            added = added + share[1 + g, :kinds, :]
        total[g * kinds : (g + 1) * kinds, :] = added
    rows = groups * kinds // 2
    low_half = lax.broadcasted_iota(jnp.int32, (1, LANES), 1) < HALF
    out[PLANE:, :] = jnp.where(low_half, total[:rows, :], total[rows:, :])


def orbital_kernel(
    planes, batch, unit, steps, meta, counts, near, far, levels, screening, cst,
    pts, before, mine, after, dist, inv, *refs,
):
    parts, (out, rate, slot_of, every, val, mom, srcv, acc) = refs[:-8], refs[-8:]
    lay_out(parts, every)
    groups, cells, kinds, _ = out.shape
    orbs = groups * kinds
    me, group = meta[0], meta[1]

    def clear(i, c):
        slot_of[i] = -1
        rate[i] = 0.0
        return c

    lax.fori_loop(0, screening.shape[0], clear, 0)
    for q in range(2 * batch):
        rate[screening.shape[0] + q] = 0.0
    lane = lax.broadcasted_iota(jnp.int32, (1, LANES), 1) % orbs

    def rank(i, carry):
        found, lane_slot = carry
        level = levels[i]
        known = slot_of[level]
        slot = jnp.where(known < 0, found, known)
        slot_of[level] = slot
        rate[slot] = screening[level] * (-log2e)
        return found + (known < 0).astype(jnp.int32), jnp.where(lane == i, slot, lane_slot)

    n_levels, lane_slot = lax.fori_loop(0, orbs, rank, (jnp.int32(0), jnp.zeros((1, LANES), jnp.int32)))
    n_batches = (n_levels + batch - 1) // batch
    first_half = lax.broadcasted_iota(jnp.int32, (1, 2 * orbs), 1) < orbs

    def flip(v):
        high = v.astype(jnp.bfloat16).astype(jnp.float32)
        square = jnp.concatenate([high, v - high, jnp.zeros((LANES - 2 * orbs, LANES), jnp.float32)], axis=0)
        return square.T[:, : 2 * orbs].astype(jnp.bfloat16)

    for k in range(3):
        message = (before, mine, after)[k]
        there = lax.bitwise_xor(me, jnp.clip(me - 1 + k, 0, planes - 1))

        def prepare(c, carry):
            at = k * PLANE + c
            point = pts[at]
            potential = point[3:4] + every[there, pl.ds(c, 1), :]
            v = cell_fields(message, c, groups, kinds) * (point[4:5] * potential)
            val[at] = flip(v)
            vh, vl = split(v)
            z_low = (me - 1 + k).astype(jnp.float32) * cell_side
            low = (*cell_low(c), z_low)
            wh, wl = split(weights(cst, point[0:1], point[1:2], point[2:3], low, (cell_side,) * 3))
            all_of = dot_bf16(jnp.concatenate([wh, wl], axis=0), jnp.concatenate([vh, vh, vl, vl], axis=0))
            m = all_of[:HALF] + all_of[HALF:]
            m = m[:, : 2 * orbs] + pltpu.roll(all_of[:HALF], 2 * orbs, 1)[:, : 2 * orbs]
            high = m.astype(jnp.bfloat16).astype(jnp.float32)
            mom[at] = jnp.where(first_half, high, m - high).astype(jnp.bfloat16)
            return carry

        lax.fori_loop(0, PLANE, prepare, 0, unroll=4)

    def put_plane(g, c):
        there = lax.bitwise_xor(me, g)
        rows = []
        for k in range(groups):
            row = lax.bitwise_xor(group, k) * kinds
            v = every[there, pl.ds(PLANE + lax.rem(row, orbs // 2), kinds), :]
            rows.append(jnp.where(row < orbs // 2, v, pltpu.roll(v, HALF, 1)))
        mom[3 * PLANE + g] = flip(jnp.concatenate(rows, axis=0))[:HALF]
        return c

    lax.fori_loop(0, planes, put_plane, 0)

    def put_near(j, slot):
        srcv[j] = val[slot]

    def put_far(j, first, second, live):
        srcv[j, :HALF, :] = mom[first]
        srcv[j, HALF:, :] = jnp.where(live, mom[second], jnp.zeros_like(mom[second]))

    def put_none(j):
        srcv[j] = jnp.zeros(srcv.shape[1:], srcv.dtype)

    def products(t, b, first):
        rates = [rate[b * batch + q] for q in range(batch)]
        rows = []
        for q in range(batch):
            tiles = [(jnp.exp2(dist[t, first + h] * rates[q]) * inv[t, first + h]).astype(jnp.bfloat16) for h in range(unit)]
            rows.append(jnp.concatenate(tiles, axis=1))
        v = jnp.concatenate([srcv[first + h] for h in range(unit)], axis=0)
        return jnp.dot(jnp.concatenate(rows, axis=0), v, preferred_element_type=jnp.float32)

    def per_cell(t, carry):
        cell = target_cell(group, t, groups)
        n_blocks = list_blocks(me, cell, counts, near, far, planes, put_near, put_far, put_none, unit)
        n_units = (n_blocks + unit - 1) // unit

        def clear_acc(b, x):
            acc[b] = jnp.zeros(acc.shape[1:], jnp.float32)
            return x

        lax.fori_loop(0, n_batches, clear_acc, 0)

        def step(i, at):
            b, u = at
            for _ in range(steps):
                acc[b] = acc[b] + products(t, b, unit * u)
                wrap = u + 1 == n_units
                b, u = jnp.where(wrap, b + 1, b), jnp.where(wrap, 0, u + 1)
            return b, u

        lax.fori_loop(0, (n_batches * n_units + steps - 1) // steps, step, (jnp.int32(0), jnp.int32(0)))

        def choose(b, add):
            for q in range(batch):
                mine = lane_slot[:, : 2 * orbs] == b * batch + q
                add = add + jnp.where(mine, acc[b, q * LANES : (q + 1) * LANES, :], 0.0)
            return add

        total = lax.fori_loop(0, n_batches, choose, jnp.zeros((LANES, 2 * orbs), jnp.float32))
        flipped = jnp.concatenate([total, jnp.zeros((LANES, LANES - 2 * orbs), jnp.float32)], axis=1).T
        rows = (flipped[:orbs] + flipped[orbs : 2 * orbs]) * green_scale
        for k in range(groups):
            out[k, t] = rows[k * kinds : (k + 1) * kinds]
        return carry

    lax.fori_loop(0, cells, per_cell, 0)


def place_kernel(meta, *refs):
    parts, out, ordered = refs[:-2], refs[-2], refs[-1]
    for k, part in enumerate(parts):
        for t in range(part.shape[0]):
            ordered[target_cell(lax.bitwise_xor(meta[1], k), t, len(parts))] = part[t]
    for c in range(PLANE):
        out[:, c, :] = ordered[c]


def smem():
    return pl.BlockSpec(memory_space=pltpu.SMEM)


def vmem():
    return pl.BlockSpec(memory_space=pltpu.VMEM)


def call(kernel, name, out_shape, smems, args, scratch=(), mib=8):
    return pl.pallas_call(
        kernel,
        out_shape=out_shape,
        in_specs=[smem()] * smems + [vmem()] * (len(args) - smems),
        out_specs=jax.tree.map(lambda _: vmem(), out_shape),
        scratch_shapes=scratch,
        compiler_params=pltpu.CompilerParams(vmem_limit_bytes=mib * 1024 * 1024),
        name=name,
    )(*args)


def body(orbitals, points, quad_weight, external, screening, level_index, near_cells, far_cells):
    kinds, cells, point_count = orbitals.shape
    planes, groups = lax.axis_size("space"), lax.axis_size("orb")
    orbs = kinds * groups
    window = 3 * PLANE
    share = cells // groups
    me, group = lax.axis_index("space"), lax.axis_index("orb")
    meta = jnp.stack([me, group]).astype(jnp.int32)
    f32, bf16 = jnp.float32, jnp.bfloat16

    fields = gather_list(orbitals, "orb")
    weight = quad_weight * (cell_side**3 / point_count)
    own = jnp.concatenate(
        [jnp.transpose(points, (1, 0, 2)), external[:, None], weight[:, None], jnp.zeros((cells, 3, LANES), f32)], axis=1
    )
    marks = jnp.pad(level_index.astype(f32), (0, LANES - kinds))[None]
    ends = planes - 1
    up = [(i, i + 1) for i in range(ends)]
    down = [(i + 1, i) for i in range(ends)]
    cst = jnp.asarray(basis_rows())
    base_table = proxy_table(planes, window)
    shift = np.zeros(base_table.shape, np.float32)
    shift[:window, 2] = cell_side
    table = jnp.asarray(base_table) + jnp.asarray(shift) * (me - 1).astype(f32)
    counts = jnp.stack(
        [jnp.sum((near_cells >= 0).astype(jnp.int32), 1), jnp.sum((far_cells >= 0).astype(jnp.int32), 1)], axis=1
    )
    charges = call(
        charge_kernel,
        "charge",
        jax.ShapeDtypeStruct((cells, ROWS, LANES), f32),
        1,
        (meta, cst, own, *fields),
        [pltpu.VMEM((cells, LANES), f32)],
    )
    charges = gather_parts(charges, "space", False)
    mine = jnp.concatenate([f.reshape(kinds * cells, LANES) for f in fields], axis=0)

    batch, unit, steps = 4, 4, 9
    most = near_cells.shape[1]
    blocks = most + (window - most + planes + 1) // 2
    blocks = -(-blocks // unit) * unit + unit
    shares, pts, src = call(
        functools.partial(hartree_kernel, groups, kinds, unit),
        "hartree",
        (
            jax.ShapeDtypeStruct((1 + groups, ROWS, LANES), f32),
            jax.ShapeDtypeStruct((window, ROWS, LANES), f32),
            jax.ShapeDtypeStruct((share, blocks, ROWS, LANES), f32),
        ),
        4,
        (meta, counts, near_cells, far_cells, cst, table, marks, mine, *charges),
        [
            pltpu.VMEM((planes, cells, ROWS, LANES), f32),
            pltpu.VMEM((window + planes + 1, ROWS, LANES), f32),
            pltpu.VMEM((3, LANES, LANES), f32),
        ],
        12,
    )
    dist, inv = call(
        functools.partial(pairs_kernel, groups, planes, unit),
        "pairs",
        (jax.ShapeDtypeStruct((share, blocks, LANES, LANES), f32),) * 2,
        2,
        (meta, counts, pts, src),
        [pltpu.VMEM((3, LANES, LANES), f32)],
        4,
    )
    mine, shares = lax.optimization_barrier((mine, shares))
    before, after = lax.ppermute(mine, "space", up), lax.ppermute(mine, "space", down)
    shares = gather_list(shares, "orb")
    levels = jnp.concatenate([share[0, ROWS - 1, :kinds] for share in shares]).astype(jnp.int32)
    hartree, combined = call(
        functools.partial(combine_kernel, kinds),
        "combine",
        (jax.ShapeDtypeStruct((cells, LANES), f32), jax.ShapeDtypeStruct((cells + orbs // 2, LANES), f32)),
        1,
        (meta, *shares),
        [pltpu.VMEM((orbs, LANES), f32)],
    )
    gathered = gather_parts(combined, "space", False)

    levels_at_most = -(-screening.shape[0] // batch) + 1
    sent = call(
        functools.partial(orbital_kernel, planes, batch, unit, steps),
        "orbitals",
        jax.ShapeDtypeStruct((groups, share, kinds, LANES), f32),
        6,
        (meta, counts, near_cells, far_cells, levels, screening, cst, pts, before, mine, after, dist, inv, *gathered),
        [
            pltpu.SMEM((screening.shape[0] + 2 * batch,), f32),
            pltpu.SMEM((screening.shape[0],), jnp.int32),
            pltpu.VMEM((planes, cells + orbs // 2, LANES), f32),
            pltpu.VMEM((window, LANES, 2 * orbs), bf16),
            pltpu.VMEM((window + planes, HALF, 2 * orbs), bf16),
            pltpu.VMEM((blocks, LANES, 2 * orbs), bf16),
            pltpu.VMEM((levels_at_most, batch * LANES, 2 * orbs), f32),
        ],
        14,
    )
    parts = [sent[0]]
    for k in range(1, groups):
        parts.append(lax.ppermute(sent[k], "orb", [(i, i ^ k) for i in range(groups)]))
    updated = call(
        place_kernel,
        "place",
        jax.ShapeDtypeStruct((kinds, cells, LANES), f32),
        1,
        (meta, *parts),
        [pltpu.VMEM((cells, kinds, LANES), f32)],
    )
    return updated, hartree


def solution(mesh):
    in_specs = (
        P("orb", "space", None),
        P(None, "space", None),
        P("space", None),
        P("space", None),
        P(),
        P("orb"),
        P("space", None),
        P("space", None),
    )
    out_specs = (P("orb", "space", None), P("space", None))
    return jax.shard_map(body, mesh=mesh, in_specs=in_specs, out_specs=out_specs, check_vma=False)
```

```python
import functools
import math

import jax
import jax.numpy as jnp
import numpy as np
from jax import lax
from jax.experimental import pallas as pl
from jax.experimental.pallas import tpu as pltpu
from jax.sharding import PartitionSpec as P

NODES = 4
LANES = 128
PLANE = 16
ROWS = 8
HALF = NODES**3

cell_side = 0.25
soften = 6.25e-06
green_scale = -0.5 / math.pi
log2e = math.log2(math.e)
highest = lax.Precision.HIGHEST

node_set = np.cos((2.0 * np.arange(NODES) + 1.0) * (math.pi / (2.0 * NODES)))
roots = [[node_set[m] for m in range(NODES) if m != a] for a in range(NODES)]
scales = [1.0 / np.prod([node_set[a] - r for r in roots[a]]) for a in range(NODES)]


def basis_rows():
    row = lax.broadcasted_iota(jnp.int32, (ROWS, LANES), 0)
    out = []
    for pick in (row // 4, 2 + row // 4, row % 4):
        for k in range(NODES):
            values = [float(scales[a] if k == NODES - 1 else roots[a][k]) for a in range(NODES)]
            made = jnp.full((ROWS, LANES), values[0], jnp.float32)
            for a in range(1, NODES):
                made = jnp.where(pick == a, values[a], made)
            out.append(made)
    return out


def proxy_table(planes, window):
    offset = 0.5 * (node_set + 1.0)
    p = np.arange(LANES) % HALF
    offs = np.stack([offset[p // 16], offset[p // 4 % 4], offset[p % 4]])
    cells = np.arange(window)
    lows = np.stack([cells % 4, cells // 4 % 4, cells // 16]) * cell_side
    near = lows[:, :, None] + offs[:, None, :] * cell_side
    levels = np.arange(planes)
    lows = np.stack([0 * levels, 0 * levels, levels]) * cell_side
    far = lows[:, :, None] + offs[:, None, :] * np.array([1.0, 1.0, cell_side])[:, None, None]
    table = np.zeros((window + planes, ROWS, LANES), np.float32)
    table[:, :3] = np.moveaxis(np.concatenate([near, far], 1), 0, 1)
    return table


def poly(u, r0, r1, r2, scale):
    return ((u - r0) * (u - r1)) * ((u - r2) * scale)


def weights(cst, x, y, z, lows, sides):
    ux, uy, uz = (
        jnp.broadcast_to(2.0 * (c - lo) / e - 1.0, (ROWS, LANES)) for c, lo, e in zip((x, y, z), lows, sides)
    )
    pz = poly(uz, cst[8], cst[9], cst[10], cst[11])
    pyz = [poly(uy, cst[4 * k], cst[4 * k + 1], cst[4 * k + 2], cst[4 * k + 3]) * pz for k in range(2)]
    parts = []
    for a in range(NODES):
        px = poly(ux, *(float(r) for r in roots[a]), float(scales[a]))
        parts += [px * pyz[0], px * pyz[1]]
    return jnp.concatenate(parts, axis=0)


def twice(w):
    return jnp.concatenate([w, w], axis=0)


def cell_low(cell):
    return [(cell % 4).astype(jnp.float32) * cell_side, (cell // 4 % 4).astype(jnp.float32) * cell_side]


def dot_nt(a, b):
    return lax.dot_general(a, b, (((1,), (1,)), ((), ())), precision=highest, preferred_element_type=jnp.float32)


def gather_parts(block, axis, pairs, later=None):
    count = lax.axis_size(axis)
    parts = [block[None]]
    while sum(p.shape[0] for p in parts) < count:
        held = parts[0] if len(parts) == 1 else jnp.concatenate(parts, axis=0)
        have = held.shape[0]
        steps = range(1, 4 if (have > 1 or pairs) and have * 4 <= count else 2)
        parts = [held] + [lax.ppermute(held, axis, [(i, i ^ (have * j)) for i in range(count)]) for j in steps]
        if later is not None and have == 1:
            parts[1], later = lax.optimization_barrier((parts[1], later))
    return parts, later


def gather_list(block, axis):
    parts, _ = gather_parts(block, axis, True)
    return [p[k] for p in parts for k in range(p.shape[0])]


def lay_out(parts, whole):
    at = 0
    for part in parts:
        for k in range(part.shape[0]):
            whole[at + k] = part[k]
        at += part.shape[0]


def target_cell(me, t, groups):
    return t * groups + lax.bitwise_xor(jnp.int32(t) if isinstance(t, int) else t, me)


def split(v):
    high = v.astype(jnp.bfloat16)
    return high, (v - high.astype(jnp.float32)).astype(jnp.bfloat16)


def dot_bf16(a, b):
    return lax.dot_general(a, b, (((1,), (1,)), ((), ())), preferred_element_type=jnp.float32)


def dot_split(v, w):
    vh, vl = split(v)
    wh, wl = split(w)
    rows = v.shape[0]
    both = dot_bf16(jnp.concatenate([vh, vl], axis=0), wh)
    return both[:rows] + both[rows:] + dot_bf16(vh, wl)


def lane_sums(v):
    high, low = split(v)
    ones = jnp.ones((ROWS, 2 * v.shape[1]), jnp.bfloat16)
    return dot_bf16(ones, jnp.concatenate([high, low], axis=1))[0:1, :]


def charge_kernel(meta, own, partial, *refs):
    z_low = meta[0].astype(jnp.float32) * cell_side
    fields, (out, density) = refs[:-2], refs[-2:]
    cst = basis_rows()
    total = partial[...]
    for phi in fields:
        for j in range(phi.shape[0]):
            v = phi[j]
            total = total + v * v
    density[...] = 2.0 * total
    acc = jnp.zeros((HALF, LANES), jnp.float32)
    for c in range(PLANE):
        point = own[c]
        charge = point[4:5] * density[c : c + 1, :]
        low = (cell_side * (c % 4), cell_side * (c // 4), z_low)
        acc = acc + weights(cst, point[0:1], point[1:2], point[2:3], (0.0, 0.0, z_low), (1.0, 1.0, cell_side)) * charge
        moments = lane_sums(weights(cst, point[0:1], point[1:2], point[2:3], low, (cell_side,) * 3) * charge)
        out[c, :5, :] = point[:5]
        out[c, 5:6, :] = charge
        out[c, 6:7, :] = jnp.concatenate([moments, moments], axis=1)
    moments = lane_sums(acc)
    for c in range(PLANE):
        out[c, 7:8, :] = jnp.concatenate([moments, moments], axis=1)


def live_planes(me, planes):
    below = jnp.maximum(me - 1, 0)
    return below, below + jnp.maximum(planes - 2 - me, 0)


def list_lengths(lists, cell, slots):
    return lists[cell, sum(slots)], lists[cell, sum(slots) + 1]


def list_blocks(me, cell, lists, slots, planes, put_near, put_far, put_none, multiple):
    window = 3 * PLANE
    base = (me - 1) * PLANE
    below, n_planes = live_planes(me, planes)
    near_slots, far_slots = slots
    n_near, n_far = list_lengths(lists, cell, slots)
    n_items = n_far + n_planes
    n_pairs = (n_items + 1) // 2

    def near_step(j, c):
        put_near(j, lists[cell, j] - base)
        return c

    lax.fori_loop(0, n_near, near_step, 0)

    def item(j):
        j = jnp.minimum(j, n_items - 1)
        p = j - n_far
        level = jnp.where(p < below, p, p + (me + 2 - below))
        slot = lists[cell, near_slots + jnp.minimum(j, far_slots - 1)] - base
        return jnp.where(j < n_far, slot, window + level)

    def far_step(j, c):
        put_far(n_near + j, item(2 * j), item(2 * j + 1), 2 * j + 1 < n_items)
        return c

    lax.fori_loop(0, n_pairs, far_step, 0)
    for u in range(multiple - 1):
        put_none(n_near + n_pairs + u)
    return n_near + n_pairs


def in_low_half():
    return lax.broadcasted_iota(jnp.int32, (1, LANES), 1) < HALF


def put_targets(pts, cell, tgt):
    for d in range(3):
        tgt[d] = jnp.broadcast_to(pts[PLANE + cell, d : d + 1, :], (LANES, LANES)).T


def each_square(tgt, src, first, count, use):
    sources = [[src[first + u, d : d + 1, :] for d in range(3)] for u in range(count)]
    for r in range(LANES // ROWS):
        at = [tgt[d, r * ROWS : (r + 1) * ROWS, :] for d in range(3)]
        for u in range(count):
            dx, dy, dz = (a - b for a, b in zip(at, sources[u]))
            use(r, u, (dx * dx + dy * dy) + (dz * dz + soften))


def cell_fields(message, c, groups, kinds):
    rows = kinds * PLANE
    return jnp.concatenate([message[pl.ds(g * rows + c, kinds, stride=PLANE), :] for g in range(groups)], axis=0)


def hartree_kernel(groups, kinds, unroll, slots, meta, lists, table, marks, mine, *refs):
    parts, (out, pts, src, every, items, tgt) = refs[:-6], refs[-6:]
    lay_out(parts, every)
    planes = every.shape[0]
    cells = PLANE // groups
    me, group = meta[0], meta[1]
    window = 3 * PLANE
    cst = basis_rows()
    for k in range(3):
        there = lax.bitwise_xor(me, jnp.clip(me - 1 + k, 0, planes - 1))
        for c in range(PLANE):
            pts[k * PLANE + c] = every[there, c]
    row = lax.broadcasted_iota(jnp.int32, (ROWS, 1), 0)

    def put_cell(c, carry):
        items[c] = jnp.where(row == 5, pts[c, 6:7, :], table[c])
        return carry

    lax.fori_loop(0, window, put_cell, 0, unroll=8)

    def put_plane(g, c):
        items[window + g] = jnp.where(row == 5, every[lax.bitwise_xor(me, g), 0, 7:8, :], table[window + g])
        return c

    lax.fori_loop(0, planes, put_plane, 0)
    items[window + planes] = jnp.zeros((ROWS, LANES), jnp.float32)
    low_half = in_low_half()
    z_low = me.astype(jnp.float32) * cell_side
    total = jnp.zeros((groups * kinds, LANES), jnp.float32)
    out[0] = jnp.broadcast_to(marks[...], (ROWS, LANES))
    for t in range(cells):
        cell = target_cell(group, t, groups)

        def put_near(j, slot):
            src[t, j] = pts[slot]

        def put_far(j, first, second, live):
            src[t, j] = jnp.where(low_half, items[first], items[jnp.where(live, second, window + planes)])

        def put_none(j):
            src[t, j] = jnp.zeros((ROWS, LANES), jnp.float32)

        n_blocks = list_blocks(me, cell, lists, slots, planes, put_near, put_far, put_none, unroll)
        put_targets(pts, cell, tgt)

        def step(i, accs):
            accs = list(accs)
            charges = [src[t, unroll * i + u, 5:6, :] for u in range(unroll)]

            def use(r, u, sq):
                accs[r] = accs[r] + lax.rsqrt(sq) * charges[u]

            each_square(tgt, src.at[t], unroll * i, unroll, use)
            return tuple(accs)

        zero = jnp.zeros((ROWS, LANES), jnp.float32)
        accs = lax.fori_loop(0, (n_blocks + unroll - 1) // unroll, step, (zero,) * (LANES // ROWS))
        potential = dot_nt(jnp.ones((ROWS, LANES), jnp.float32), jnp.concatenate(accs, axis=0))[0:1, :]
        out[0, t : t + 1, :] = potential
        point = pts[PLANE + cell]
        scaled = point[4:5] * (point[3:4] + potential)
        v = cell_fields(mine, cell, groups, kinds) * scaled
        w = weights(cst, point[0:1], point[1:2], point[2:3], (0.0, 0.0, z_low), (1.0, 1.0, cell_side))
        total = total + dot_split(v, twice(w))
    for k in range(groups):
        out[1 + lax.bitwise_xor(group, k), :kinds, :] = total[k * kinds : (k + 1) * kinds, :]


def pairs_kernel(groups, planes, unroll, slots, meta, lists, pts, src, dist, inv, tgt):
    group = meta[1]
    _, n_planes = live_planes(meta[0], planes)

    def per_cell(t, carry):
        cell = target_cell(group, t, groups)
        put_targets(pts, cell, tgt)
        n_near, n_far = list_lengths(lists, cell, slots)
        n_blocks = n_near + (n_far + n_planes + 1) // 2

        def measure(i, x):
            def use(r, u, sq):
                one_over = lax.rsqrt(sq)
                inv[t, unroll * i + u, r * ROWS : (r + 1) * ROWS, :] = one_over
                dist[t, unroll * i + u, r * ROWS : (r + 1) * ROWS, :] = sq * one_over

            each_square(tgt, src.at[t], unroll * i, unroll, use)
            return x

        lax.fori_loop(0, (n_blocks + unroll - 1) // unroll, measure, 0)
        return carry

    lax.fori_loop(0, PLANE // groups, per_cell, 0)


def combine_kernel(kinds, meta, *refs):
    shares, (hartree, out, total) = refs[:-3], refs[-3:]
    groups = len(shares)
    for k, share in enumerate(shares):
        for t in range(PLANE // groups):
            cell = target_cell(lax.bitwise_xor(meta[1], k), t, groups)
            out[pl.ds(cell, 1), :] = share[0, t : t + 1, :]
    hartree[...] = out[:PLANE, :]
    for g in range(groups):
        added = shares[0][1 + g, :kinds, :]
        for share in shares[1:]:
            added = added + share[1 + g, :kinds, :]
        total[g * kinds : (g + 1) * kinds, :] = added
    rows = groups * kinds // 2
    low_half = lax.broadcasted_iota(jnp.int32, (1, LANES), 1) < HALF
    out[PLANE:, :] = jnp.where(low_half, total[:rows, :], total[rows:, :])


def orbital_kernel(
    planes, batch, unit, steps, slots, meta, lists, levels, rates_of,
    pts, before, mine, after, dist, inv, *refs,
):
    parts, (out, rate, slot_of, every, val, mom, srcv, acc) = refs[:-8], refs[-8:]
    lay_out(parts, every)
    groups, cells, kinds, _ = out.shape
    orbs = groups * kinds
    me, group = meta[0], meta[1]

    def clear(i, c):
        slot_of[i] = -1
        rate[i] = 0.0
        return c

    lax.fori_loop(0, rates_of.shape[0], clear, 0)
    for q in range(2 * batch):
        rate[rates_of.shape[0] + q] = 0.0
    lane = lax.broadcasted_iota(jnp.int32, (1, LANES), 1) % orbs

    def rank(i, carry):
        found, lane_slot = carry
        level = levels[i]
        known = slot_of[level]
        slot = jnp.where(known < 0, found, known)
        slot_of[level] = slot
        rate[slot] = rates_of[level]
        return found + (known < 0).astype(jnp.int32), jnp.where(lane == i, slot, lane_slot)

    n_levels, lane_slot = lax.fori_loop(0, orbs, rank, (jnp.int32(0), jnp.zeros((1, LANES), jnp.int32)))
    n_batches = (n_levels + batch - 1) // batch
    first_half = lax.broadcasted_iota(jnp.int32, (1, 2 * orbs), 1) < orbs
    cst = basis_rows()

    def flip(v):
        high = v.astype(jnp.bfloat16).astype(jnp.float32)
        square = jnp.concatenate([high, v - high, jnp.zeros((LANES - 2 * orbs, LANES), jnp.float32)], axis=0)
        return square.T[:, : 2 * orbs].astype(jnp.bfloat16)

    for k in range(3):
        message = (before, mine, after)[k]
        there = lax.bitwise_xor(me, jnp.clip(me - 1 + k, 0, planes - 1))

        def prepare(c, carry):
            at = k * PLANE + c
            point = pts[at]
            potential = point[3:4] + every[there, pl.ds(c, 1), :]
            v = cell_fields(message, c, groups, kinds) * (point[4:5] * potential)
            val[at] = flip(v)
            vh, vl = split(v)
            z_low = (me - 1 + k).astype(jnp.float32) * cell_side
            low = (*cell_low(c), z_low)
            wh, wl = split(weights(cst, point[0:1], point[1:2], point[2:3], low, (cell_side,) * 3))
            all_of = dot_bf16(jnp.concatenate([wh, wl], axis=0), jnp.concatenate([vh, vh, vl, vl], axis=0))
            m = all_of[:HALF] + all_of[HALF:]
            m = m[:, : 2 * orbs] + pltpu.roll(all_of[:HALF], 2 * orbs, 1)[:, : 2 * orbs]
            high = m.astype(jnp.bfloat16).astype(jnp.float32)
            mom[at] = jnp.where(first_half, high, m - high).astype(jnp.bfloat16)
            return carry

        lax.fori_loop(0, PLANE, prepare, 0, unroll=4)

    def put_plane(g, c):
        there = lax.bitwise_xor(me, g)
        rows = []
        for k in range(groups):
            row = lax.bitwise_xor(group, k) * kinds
            v = every[there, pl.ds(PLANE + lax.rem(row, orbs // 2), kinds), :]
            rows.append(jnp.where(row < orbs // 2, v, pltpu.roll(v, HALF, 1)))
        mom[3 * PLANE + g] = flip(jnp.concatenate(rows, axis=0))[:HALF]
        return c

    lax.fori_loop(0, planes, put_plane, 0)

    def put_near(j, slot):
        srcv[j] = val[slot]

    def put_far(j, first, second, live):
        srcv[j, :HALF, :] = mom[first]
        srcv[j, HALF:, :] = jnp.where(live, mom[second], jnp.zeros_like(mom[second]))

    def put_none(j):
        srcv[j] = jnp.zeros(srcv.shape[1:], srcv.dtype)

    def products(t, b, first):
        rates = [rate[b * batch + q] for q in range(batch)]
        rows = []
        for q in range(batch):
            tiles = [(jnp.exp2(dist[t, first + h] * rates[q]) * inv[t, first + h]).astype(jnp.bfloat16) for h in range(unit)]
            rows.append(jnp.concatenate(tiles, axis=1))
        v = jnp.concatenate([srcv[first + h] for h in range(unit)], axis=0)
        return jnp.dot(jnp.concatenate(rows, axis=0), v, preferred_element_type=jnp.float32)

    def per_cell(t, carry):
        cell = target_cell(group, t, groups)
        n_blocks = list_blocks(me, cell, lists, slots, planes, put_near, put_far, put_none, unit)
        n_units = (n_blocks + unit - 1) // unit

        def clear_acc(b, x):
            acc[b] = jnp.zeros(acc.shape[1:], jnp.float32)
            return x

        lax.fori_loop(0, n_batches, clear_acc, 0)

        def step(i, at):
            b, u = at
            for _ in range(steps):
                acc[b] = acc[b] + products(t, b, unit * u)
                wrap = u + 1 == n_units
                b, u = jnp.where(wrap, b + 1, b), jnp.where(wrap, 0, u + 1)
            return b, u

        lax.fori_loop(0, (n_batches * n_units + steps - 1) // steps, step, (jnp.int32(0), jnp.int32(0)))

        def choose(b, add):
            for q in range(batch):
                mine = lane_slot[:, : 2 * orbs] == b * batch + q
                add = add + jnp.where(mine, acc[b, q * LANES : (q + 1) * LANES, :], 0.0)
            return add

        total = lax.fori_loop(0, n_batches, choose, jnp.zeros((LANES, 2 * orbs), jnp.float32))
        flipped = jnp.concatenate([total, jnp.zeros((LANES, LANES - 2 * orbs), jnp.float32)], axis=1).T
        rows = (flipped[:orbs] + flipped[orbs : 2 * orbs]) * green_scale
        for k in range(groups):
            out[k, t] = rows[k * kinds : (k + 1) * kinds]
        return carry

    lax.fori_loop(0, cells, per_cell, 0)


def place_kernel(meta, *refs):
    parts, out, ordered = refs[:-2], refs[-2], refs[-1]
    for k, part in enumerate(parts):
        for t in range(part.shape[0]):
            ordered[target_cell(lax.bitwise_xor(meta[1], k), t, len(parts))] = part[t]
    for c in range(PLANE):
        out[:, c, :] = ordered[c]


def smem():
    return pl.BlockSpec(memory_space=pltpu.SMEM)


def vmem():
    return pl.BlockSpec(memory_space=pltpu.VMEM)


def call(kernel, name, out_shape, smems, args, scratch=(), mib=8):
    return pl.pallas_call(
        kernel,
        out_shape=out_shape,
        in_specs=[smem()] * smems + [vmem()] * (len(args) - smems),
        out_specs=jax.tree.map(lambda _: vmem(), out_shape),
        scratch_shapes=scratch,
        compiler_params=pltpu.CompilerParams(vmem_limit_bytes=mib * 1024 * 1024),
        name=name,
    )(*args)


def body(orbitals, points, quad_weight, external, screening, level_index, near_cells, far_cells):
    kinds, cells, point_count = orbitals.shape
    planes, groups = lax.axis_size("space"), lax.axis_size("orb")
    orbs = kinds * groups
    window = 3 * PLANE
    share = cells // groups
    me, group = lax.axis_index("space"), lax.axis_index("orb")
    meta = jnp.stack([me, group]).astype(jnp.int32)
    f32, bf16 = jnp.float32, jnp.bfloat16

    fields = gather_list(orbitals, "orb")
    weight = quad_weight * (cell_side**3 / point_count)
    own = jnp.concatenate(
        [jnp.transpose(points, (1, 0, 2)), external[:, None], weight[:, None], jnp.zeros((cells, 3, LANES), f32)], axis=1
    )
    marks = jnp.pad(level_index.astype(f32), (0, LANES - kinds))[None]
    ends = planes - 1
    up = [(i, i + 1) for i in range(ends)]
    down = [(i + 1, i) for i in range(ends)]
    base_table = proxy_table(planes, window)
    shift = np.zeros(base_table.shape, np.float32)
    shift[:window, 2] = cell_side
    table = jnp.asarray(base_table) + jnp.asarray(shift) * (me - 1).astype(f32)
    slots = (near_cells.shape[1], far_cells.shape[1])
    lists = jnp.concatenate(
        [
            near_cells,
            far_cells,
            jnp.sum((near_cells >= 0).astype(jnp.int32), axis=1, keepdims=True),
            jnp.sum((far_cells >= 0).astype(jnp.int32), axis=1, keepdims=True),
        ],
        axis=1,
    )
    rates_of = screening * (-log2e)
    partial = jnp.sum(orbitals * orbitals, axis=0)

    charges = call(
        charge_kernel,
        "charge",
        jax.ShapeDtypeStruct((cells, ROWS, LANES), f32),
        1,
        (meta, own, partial, *fields[1:]),
        [pltpu.VMEM((cells, LANES), f32)],
    )
    mine = jnp.concatenate([f.reshape(kinds * cells, LANES) for f in fields], axis=0)
    charges, mine = gather_parts(charges, "space", False, mine)
    before, after = lax.ppermute(mine, "space", up), lax.ppermute(mine, "space", down)

    batch, unit, steps = 4, 4, 9
    most = near_cells.shape[1]
    blocks = most + (window - most + planes + 1) // 2
    blocks = -(-blocks // unit) * unit + unit
    shares, pts, src = call(
        functools.partial(hartree_kernel, groups, kinds, unit, slots),
        "hartree",
        (
            jax.ShapeDtypeStruct((1 + groups, ROWS, LANES), f32),
            jax.ShapeDtypeStruct((window, ROWS, LANES), f32),
            jax.ShapeDtypeStruct((share, blocks, ROWS, LANES), f32),
        ),
        2,
        (meta, lists, table, marks, mine, *charges),
        [
            pltpu.VMEM((planes, cells, ROWS, LANES), f32),
            pltpu.VMEM((window + planes + 1, ROWS, LANES), f32),
            pltpu.VMEM((3, LANES, LANES), f32),
        ],
        12,
    )
    dist, inv = call(
        functools.partial(pairs_kernel, groups, planes, unit, slots),
        "pairs",
        (jax.ShapeDtypeStruct((share, blocks, LANES, LANES), f32),) * 2,
        2,
        (meta, lists, pts, src),
        [pltpu.VMEM((3, LANES, LANES), f32)],
        4,
    )
    shares = gather_list(shares, "orb")
    levels = jnp.concatenate([share[0, ROWS - 1, :kinds] for share in shares]).astype(jnp.int32)
    hartree, combined = call(
        functools.partial(combine_kernel, kinds),
        "combine",
        (jax.ShapeDtypeStruct((cells, LANES), f32), jax.ShapeDtypeStruct((cells + orbs // 2, LANES), f32)),
        1,
        (meta, *shares),
        [pltpu.VMEM((orbs, LANES), f32)],
    )
    gathered, _ = gather_parts(combined, "space", False)

    levels_at_most = -(-screening.shape[0] // batch) + 1
    sent = call(
        functools.partial(orbital_kernel, planes, batch, unit, steps, slots),
        "orbitals",
        jax.ShapeDtypeStruct((groups, share, kinds, LANES), f32),
        4,
        (meta, lists, levels, rates_of, pts, before, mine, after, dist, inv, *gathered),
        [
            pltpu.SMEM((screening.shape[0] + 2 * batch,), f32),
            pltpu.SMEM((screening.shape[0],), jnp.int32),
            pltpu.VMEM((planes, cells + orbs // 2, LANES), f32),
            pltpu.VMEM((window, LANES, 2 * orbs), bf16),
            pltpu.VMEM((window + planes, HALF, 2 * orbs), bf16),
            pltpu.VMEM((blocks, LANES, 2 * orbs), bf16),
            pltpu.VMEM((levels_at_most, batch * LANES, 2 * orbs), f32),
        ],
        14,
    )
    parts = [sent[0]]
    for k in range(1, groups):
        parts.append(lax.ppermute(sent[k], "orb", [(i, i ^ k) for i in range(groups)]))
    updated = call(
        place_kernel,
        "place",
        jax.ShapeDtypeStruct((kinds, cells, LANES), f32),
        1,
        (meta, *parts),
        [pltpu.VMEM((cells, kinds, LANES), f32)],
    )
    return updated, hartree


def solution(mesh):
    in_specs = (
        P("orb", "space", None),
        P(None, "space", None),
        P("space", None),
        P("space", None),
        P(),
        P("orb"),
        P("space", None),
        P("space", None),
    )
    out_specs = (P("orb", "space", None), P("space", None))
    return jax.shard_map(body, mesh=mesh, in_specs=in_specs, out_specs=out_specs, check_vma=False)
```

```python
import functools
import math

import jax
import jax.numpy as jnp
import numpy as np
from jax import lax
from jax.experimental import pallas as pl
from jax.experimental.pallas import tpu as pltpu
from jax.sharding import PartitionSpec as P

NODES = 4
LANES = 128
PLANE = 16
ROWS = 8
HALF = NODES**3

cell_side = 0.25
soften = 6.25e-06
green_scale = -0.5 / math.pi
log2e = math.log2(math.e)
highest = lax.Precision.HIGHEST

node_set = np.cos((2.0 * np.arange(NODES) + 1.0) * (math.pi / (2.0 * NODES)))
roots = [[node_set[m] for m in range(NODES) if m != a] for a in range(NODES)]
scales = [1.0 / np.prod([node_set[a] - r for r in roots[a]]) for a in range(NODES)]


def put_basis(cst):
    row = lax.broadcasted_iota(jnp.int32, (ROWS, LANES), 0)
    for i, pick in enumerate((row // 4, 2 + row // 4, row % 4)):
        for k in range(NODES):
            values = [float(scales[a] if k == NODES - 1 else roots[a][k]) for a in range(NODES)]
            made = jnp.full((ROWS, LANES), values[0], jnp.float32)
            for a in range(1, NODES):
                made = jnp.where(pick == a, values[a], made)
            cst[NODES * i + k] = made


def node_offsets():
    lane = lax.broadcasted_iota(jnp.int32, (1, LANES), 1) % HALF
    out = []
    for pick in (lane // 16, lane // 4 % 4, lane % 4):
        made = jnp.full((1, LANES), 0.5 * (node_set[0] + 1.0), jnp.float32)
        for a in range(1, NODES):
            made = jnp.where(pick == a, float(0.5 * (node_set[a] + 1.0)), made)
        out.append(made)
    return out


def poly(u, r0, r1, r2, scale):
    return ((u - r0) * (u - r1)) * ((u - r2) * scale)


def weights(cst, x, y, z, lows, sides):
    ux, uy, uz = (
        jnp.broadcast_to(2.0 * (c - lo) / e - 1.0, (ROWS, LANES)) for c, lo, e in zip((x, y, z), lows, sides)
    )
    pz = poly(uz, cst[8], cst[9], cst[10], cst[11])
    pyz = [poly(uy, cst[4 * k], cst[4 * k + 1], cst[4 * k + 2], cst[4 * k + 3]) * pz for k in range(2)]
    parts = []
    for a in range(NODES):
        px = poly(ux, *(float(r) for r in roots[a]), float(scales[a]))
        parts += [px * pyz[0], px * pyz[1]]
    return jnp.concatenate(parts, axis=0)


def twice(w):
    return jnp.concatenate([w, w], axis=0)


def cell_low(cell):
    return [(cell % 4).astype(jnp.float32) * cell_side, (cell // 4 % 4).astype(jnp.float32) * cell_side]


def dot_nt(a, b):
    return lax.dot_general(a, b, (((1,), (1,)), ((), ())), precision=highest, preferred_element_type=jnp.float32)


def gather_parts(block, axis, pairs, later=None):
    count = lax.axis_size(axis)
    parts = [block[None]]
    while sum(p.shape[0] for p in parts) < count:
        held = parts[0] if len(parts) == 1 else jnp.concatenate(parts, axis=0)
        have = held.shape[0]
        steps = range(1, 4 if (have > 1 or pairs) and have * 4 <= count else 2)
        parts = [held] + [lax.ppermute(held, axis, [(i, i ^ (have * j)) for i in range(count)]) for j in steps]
        if later is not None and have == 1:
            parts[1], later = lax.optimization_barrier((parts[1], later))
    return parts, later


def gather_list(block, axis):
    parts, _ = gather_parts(block, axis, True)
    return [p[k] for p in parts for k in range(p.shape[0])]


def lay_out(parts, whole):
    at = 0
    for part in parts:
        for k in range(part.shape[0]):
            whole[at + k] = part[k]
        at += part.shape[0]


def target_cell(me, t, groups):
    return t * groups + lax.bitwise_xor(jnp.int32(t) if isinstance(t, int) else t, me)


def split(v):
    high = v.astype(jnp.bfloat16)
    return high, (v - high.astype(jnp.float32)).astype(jnp.bfloat16)


def dot_bf16(a, b):
    return lax.dot_general(a, b, (((1,), (1,)), ((), ())), preferred_element_type=jnp.float32)


def dot_split(v, w):
    vh, vl = split(v)
    wh, wl = split(w)
    rows = v.shape[0]
    both = dot_bf16(jnp.concatenate([vh, vl], axis=0), wh)
    return both[:rows] + both[rows:] + dot_bf16(vh, wl)


def lane_sums(v):
    high, low = split(v)
    ones = jnp.ones((ROWS, 2 * v.shape[1]), jnp.bfloat16)
    return dot_bf16(ones, jnp.concatenate([high, low], axis=1))[0:1, :]


def charge_kernel(meta, own, partial, *refs):
    z_low = meta[0].astype(jnp.float32) * cell_side
    fields, (out, density, cst) = refs[:-3], refs[-3:]
    put_basis(cst)
    total = partial[...]
    for phi in fields:
        for j in range(phi.shape[0]):
            v = phi[j]
            total = total + v * v
    density[...] = 2.0 * total
    acc = jnp.zeros((HALF, LANES), jnp.float32)
    for c in range(PLANE):
        point = own[:, c, :]
        charge = point[4:5] * density[c : c + 1, :]
        low = (cell_side * (c % 4), cell_side * (c // 4), z_low)
        acc = acc + weights(cst, point[0:1], point[1:2], point[2:3], (0.0, 0.0, z_low), (1.0, 1.0, cell_side)) * charge
        moments = lane_sums(weights(cst, point[0:1], point[1:2], point[2:3], low, (cell_side,) * 3) * charge)
        out[c, :5, :] = point[:5]
        out[c, 5:6, :] = charge
        out[c, 6:7, :] = jnp.concatenate([moments, moments], axis=1)
    moments = lane_sums(acc)
    for c in range(PLANE):
        out[c, 7:8, :] = jnp.concatenate([moments, moments], axis=1)


def live_planes(me, planes):
    below = jnp.maximum(me - 1, 0)
    return below, below + jnp.maximum(planes - 2 - me, 0)


def list_lengths(lists, cell, slots, me, planes):
    low, high = jnp.int32(0), jnp.int32(slots[0])
    for _ in range(slots[0].bit_length()):
        mid = (low + high) // 2
        live = (low < high) & (lists[cell, jnp.minimum(mid, slots[0] - 1)] >= 0)
        high = jnp.where(live | (low >= high), high, mid)
        low = jnp.where(live, mid + 1, low)
    around = 1 + (me > 0).astype(jnp.int32) + (me + 1 < planes).astype(jnp.int32)
    return low, around * PLANE - low


def list_blocks(me, cell, lists, slots, planes, put_near, put_far, put_none, multiple):
    window = 3 * PLANE
    base = (me - 1) * PLANE
    below, n_planes = live_planes(me, planes)
    near_slots, far_slots = slots
    n_near, n_far = list_lengths(lists, cell, slots, me, planes)
    n_items = n_far + n_planes
    n_pairs = (n_items + 1) // 2

    def near_step(j, c):
        put_near(j, lists[cell, j] - base)
        return c

    lax.fori_loop(0, n_near, near_step, 0)

    def item(j):
        j = jnp.minimum(j, n_items - 1)
        p = j - n_far
        level = jnp.where(p < below, p, p + (me + 2 - below))
        slot = lists[cell, near_slots + jnp.minimum(j, far_slots - 1)] - base
        return jnp.where(j < n_far, slot, window + level)

    def far_step(j, c):
        put_far(n_near + j, item(2 * j), item(2 * j + 1), 2 * j + 1 < n_items)
        return c

    lax.fori_loop(0, n_pairs, far_step, 0)
    for u in range(multiple - 1):
        put_none(n_near + n_pairs + u)
    return n_near + n_pairs


def in_low_half():
    return lax.broadcasted_iota(jnp.int32, (1, LANES), 1) < HALF


def put_targets(pts, cell, tgt):
    for d in range(3):
        tgt[d] = jnp.broadcast_to(pts[PLANE + cell, d : d + 1, :], (LANES, LANES)).T


def each_square(tgt, src, first, count, use):
    sources = [[src[first + u, d : d + 1, :] for d in range(3)] for u in range(count)]
    for r in range(LANES // ROWS):
        at = [tgt[d, r * ROWS : (r + 1) * ROWS, :] for d in range(3)]
        for u in range(count):
            dx, dy, dz = (a - b for a, b in zip(at, sources[u]))
            use(r, u, (dx * dx + dy * dy) + (dz * dz + soften))


def cell_fields(message, c, groups, kinds):
    rows = kinds * PLANE
    return jnp.concatenate([message[pl.ds(g * rows + c, kinds, stride=PLANE), :] for g in range(groups)], axis=0)


def hartree_kernel(groups, kinds, unroll, slots, meta, lists, marks, mine, *refs):
    parts, (out, pts, src, every, items, tgt, cst) = refs[:-7], refs[-7:]
    lay_out(parts, every)
    planes = every.shape[0]
    cells = PLANE // groups
    me, group = meta[0], meta[1]
    window = 3 * PLANE
    put_basis(cst)
    for k in range(3):
        there = lax.bitwise_xor(me, jnp.clip(me - 1 + k, 0, planes - 1))
        for c in range(PLANE):
            pts[k * PLANE + c] = every[there, c]
    row = lax.broadcasted_iota(jnp.int32, (ROWS, 1), 0)

    offsets = node_offsets()

    def item_of(lows, sides, moments):
        made = jnp.where(row == 5, moments, 0.0)
        for d in range(3):
            made = jnp.where(row == d, lows[d] + offsets[d] * sides[d], made)
        return made

    def put_cell(c, carry):
        lows = (*cell_low(c), (me - 1 + c // PLANE).astype(jnp.float32) * cell_side)
        items[c] = item_of(lows, (cell_side,) * 3, pts[c, 6:7, :])
        return carry

    lax.fori_loop(0, window, put_cell, 0, unroll=8)

    def put_plane(g, c):
        lows = (0.0, 0.0, g.astype(jnp.float32) * cell_side)
        items[window + g] = item_of(lows, (1.0, 1.0, cell_side), every[lax.bitwise_xor(me, g), 0, 7:8, :])
        return c

    lax.fori_loop(0, planes, put_plane, 0)
    items[window + planes] = jnp.zeros((ROWS, LANES), jnp.float32)
    low_half = in_low_half()
    z_low = me.astype(jnp.float32) * cell_side
    total = jnp.zeros((groups * kinds, LANES), jnp.float32)
    out[0] = jnp.broadcast_to(marks[...], (ROWS, LANES))
    for t in range(cells):
        cell = target_cell(group, t, groups)

        def put_near(j, slot):
            src[t, j] = pts[slot]

        def put_far(j, first, second, live):
            src[t, j] = jnp.where(low_half, items[first], items[jnp.where(live, second, window + planes)])

        def put_none(j):
            src[t, j] = jnp.zeros((ROWS, LANES), jnp.float32)

        n_blocks = list_blocks(me, cell, lists, slots, planes, put_near, put_far, put_none, unroll)
        put_targets(pts, cell, tgt)

        def step(i, accs):
            accs = list(accs)
            charges = [src[t, unroll * i + u, 5:6, :] for u in range(unroll)]

            def use(r, u, sq):
                accs[r] = accs[r] + lax.rsqrt(sq) * charges[u]

            each_square(tgt, src.at[t], unroll * i, unroll, use)
            return tuple(accs)

        zero = jnp.zeros((ROWS, LANES), jnp.float32)
        accs = lax.fori_loop(0, (n_blocks + unroll - 1) // unroll, step, (zero,) * (LANES // ROWS))
        potential = dot_nt(jnp.ones((ROWS, LANES), jnp.float32), jnp.concatenate(accs, axis=0))[0:1, :]
        out[0, t : t + 1, :] = potential
        point = pts[PLANE + cell]
        scaled = point[4:5] * (point[3:4] + potential)
        v = cell_fields(mine, cell, groups, kinds) * scaled
        w = weights(cst, point[0:1], point[1:2], point[2:3], (0.0, 0.0, z_low), (1.0, 1.0, cell_side))
        total = total + dot_split(v, twice(w))
    for k in range(groups):
        out[1 + lax.bitwise_xor(group, k), :kinds, :] = total[k * kinds : (k + 1) * kinds, :]


def pairs_kernel(groups, planes, unroll, slots, meta, lists, pts, src, dist, inv, tgt):
    group = meta[1]
    _, n_planes = live_planes(meta[0], planes)

    def per_cell(t, carry):
        cell = target_cell(group, t, groups)
        put_targets(pts, cell, tgt)
        n_near, n_far = list_lengths(lists, cell, slots, meta[0], planes)
        n_blocks = n_near + (n_far + n_planes + 1) // 2

        def measure(i, x):
            def use(r, u, sq):
                one_over = lax.rsqrt(sq)
                inv[t, unroll * i + u, r * ROWS : (r + 1) * ROWS, :] = one_over
                dist[t, unroll * i + u, r * ROWS : (r + 1) * ROWS, :] = sq * one_over

            each_square(tgt, src.at[t], unroll * i, unroll, use)
            return x

        lax.fori_loop(0, (n_blocks + unroll - 1) // unroll, measure, 0)
        return carry

    lax.fori_loop(0, PLANE // groups, per_cell, 0)


def combine_kernel(kinds, meta, *refs):
    shares, (hartree, out, total) = refs[:-3], refs[-3:]
    groups = len(shares)
    for k, share in enumerate(shares):
        for t in range(PLANE // groups):
            cell = target_cell(lax.bitwise_xor(meta[1], k), t, groups)
            out[pl.ds(cell, 1), :] = share[0, t : t + 1, :]
    hartree[...] = out[:PLANE, :]
    for g in range(groups):
        added = shares[0][1 + g, :kinds, :]
        for share in shares[1:]:
            added = added + share[1 + g, :kinds, :]
        total[g * kinds : (g + 1) * kinds, :] = added
    rows = groups * kinds // 2
    low_half = lax.broadcasted_iota(jnp.int32, (1, LANES), 1) < HALF
    out[PLANE:, :] = jnp.where(low_half, total[:rows, :], total[rows:, :])


def orbital_kernel(
    planes, batch, unit, steps, slots, meta, lists, table,
    pts, before, mine, after, dist, inv, *refs,
):
    parts, (out, rate, slot_of, every, val, mom, srcv, acc, cst) = refs[:-9], refs[-9:]
    lay_out(parts, every)
    groups, cells, kinds, _ = out.shape
    orbs = groups * kinds
    n_rates = table.shape[0] - orbs
    me, group = meta[0], meta[1]

    def clear(i, c):
        slot_of[i] = -1
        rate[i] = 0.0
        return c

    lax.fori_loop(0, n_rates, clear, 0)
    for q in range(2 * batch):
        rate[n_rates + q] = 0.0
    lane = lax.broadcasted_iota(jnp.int32, (1, LANES), 1) % orbs

    def rank(i, carry):
        found, lane_slot = carry
        level = table[i].astype(jnp.int32)
        known = slot_of[level]
        slot = jnp.where(known < 0, found, known)
        slot_of[level] = slot
        rate[slot] = table[orbs + level] * (-log2e)
        return found + (known < 0).astype(jnp.int32), jnp.where(lane == i, slot, lane_slot)

    n_levels, lane_slot = lax.fori_loop(0, orbs, rank, (jnp.int32(0), jnp.zeros((1, LANES), jnp.int32)))
    n_batches = (n_levels + batch - 1) // batch
    first_half = lax.broadcasted_iota(jnp.int32, (1, 2 * orbs), 1) < orbs
    put_basis(cst)

    def flip(v):
        high = v.astype(jnp.bfloat16).astype(jnp.float32)
        square = jnp.concatenate([high, v - high, jnp.zeros((LANES - 2 * orbs, LANES), jnp.float32)], axis=0)
        return square.T[:, : 2 * orbs].astype(jnp.bfloat16)

    for k in range(3):
        message = (before, mine, after)[k]
        there = lax.bitwise_xor(me, jnp.clip(me - 1 + k, 0, planes - 1))

        def prepare(c, carry):
            at = k * PLANE + c
            point = pts[at]
            potential = point[3:4] + every[there, pl.ds(c, 1), :]
            v = cell_fields(message, c, groups, kinds) * (point[4:5] * potential)
            val[at] = flip(v)
            vh, vl = split(v)
            z_low = (me - 1 + k).astype(jnp.float32) * cell_side
            low = (*cell_low(c), z_low)
            wh, wl = split(weights(cst, point[0:1], point[1:2], point[2:3], low, (cell_side,) * 3))
            all_of = dot_bf16(jnp.concatenate([wh, wl], axis=0), jnp.concatenate([vh, vh, vl, vl], axis=0))
            m = all_of[:HALF] + all_of[HALF:]
            m = m[:, : 2 * orbs] + pltpu.roll(all_of[:HALF], 2 * orbs, 1)[:, : 2 * orbs]
            high = m.astype(jnp.bfloat16).astype(jnp.float32)
            mom[at] = jnp.where(first_half, high, m - high).astype(jnp.bfloat16)
            return carry

        lax.fori_loop(0, PLANE, prepare, 0, unroll=4)

    def put_plane(g, c):
        there = lax.bitwise_xor(me, g)
        rows = []
        for k in range(groups):
            row = lax.bitwise_xor(group, k) * kinds
            v = every[there, pl.ds(PLANE + lax.rem(row, orbs // 2), kinds), :]
            rows.append(jnp.where(row < orbs // 2, v, pltpu.roll(v, HALF, 1)))
        mom[3 * PLANE + g] = flip(jnp.concatenate(rows, axis=0))[:HALF]
        return c

    lax.fori_loop(0, planes, put_plane, 0)

    def put_near(j, slot):
        srcv[j] = val[slot]

    def put_far(j, first, second, live):
        srcv[j, :HALF, :] = mom[first]
        srcv[j, HALF:, :] = jnp.where(live, mom[second], jnp.zeros_like(mom[second]))

    def put_none(j):
        srcv[j] = jnp.zeros(srcv.shape[1:], srcv.dtype)

    def products(t, b, first):
        rates = [rate[b * batch + q] for q in range(batch)]
        rows = []
        for q in range(batch):
            tiles = [(jnp.exp2(dist[t, first + h] * rates[q]) * inv[t, first + h]).astype(jnp.bfloat16) for h in range(unit)]
            rows.append(jnp.concatenate(tiles, axis=1))
        v = jnp.concatenate([srcv[first + h] for h in range(unit)], axis=0)
        return jnp.dot(jnp.concatenate(rows, axis=0), v, preferred_element_type=jnp.float32)

    def per_cell(t, carry):
        cell = target_cell(group, t, groups)
        n_blocks = list_blocks(me, cell, lists, slots, planes, put_near, put_far, put_none, unit)
        n_units = (n_blocks + unit - 1) // unit

        def clear_acc(b, x):
            acc[b] = jnp.zeros(acc.shape[1:], jnp.float32)
            return x

        lax.fori_loop(0, n_batches, clear_acc, 0)

        def step(i, at):
            b, u = at
            for _ in range(steps):
                acc[b] = acc[b] + products(t, b, unit * u)
                wrap = u + 1 == n_units
                b, u = jnp.where(wrap, b + 1, b), jnp.where(wrap, 0, u + 1)
            return b, u

        lax.fori_loop(0, (n_batches * n_units + steps - 1) // steps, step, (jnp.int32(0), jnp.int32(0)))

        def choose(b, add):
            for q in range(batch):
                mine = lane_slot[:, : 2 * orbs] == b * batch + q
                add = add + jnp.where(mine, acc[b, q * LANES : (q + 1) * LANES, :], 0.0)
            return add

        total = lax.fori_loop(0, n_batches, choose, jnp.zeros((LANES, 2 * orbs), jnp.float32))
        flipped = jnp.concatenate([total, jnp.zeros((LANES, LANES - 2 * orbs), jnp.float32)], axis=1).T
        rows = (flipped[:orbs] + flipped[orbs : 2 * orbs]) * green_scale
        for k in range(groups):
            out[k, t] = rows[k * kinds : (k + 1) * kinds]
        return carry

    lax.fori_loop(0, cells, per_cell, 0)


def place_kernel(meta, *refs):
    parts, out, ordered = refs[:-2], refs[-2], refs[-1]
    for k, part in enumerate(parts):
        for t in range(part.shape[0]):
            ordered[target_cell(lax.bitwise_xor(meta[1], k), t, len(parts))] = part[t]
    for c in range(PLANE):
        out[:, c, :] = ordered[c]


def smem():
    return pl.BlockSpec(memory_space=pltpu.SMEM)


def vmem():
    return pl.BlockSpec(memory_space=pltpu.VMEM)


def call(kernel, name, out_shape, smems, args, scratch=(), mib=8):
    return pl.pallas_call(
        kernel,
        out_shape=out_shape,
        in_specs=[smem()] * smems + [vmem()] * (len(args) - smems),
        out_specs=jax.tree.map(lambda _: vmem(), out_shape),
        scratch_shapes=scratch,
        compiler_params=pltpu.CompilerParams(vmem_limit_bytes=mib * 1024 * 1024),
        name=name,
    )(*args)


def body(orbitals, points, quad_weight, external, screening, level_index, near_cells, far_cells):
    kinds, cells, point_count = orbitals.shape
    planes, groups = lax.axis_size("space"), lax.axis_size("orb")
    orbs = kinds * groups
    window = 3 * PLANE
    share = cells // groups
    me, group = lax.axis_index("space"), lax.axis_index("orb")
    meta = jnp.stack([me, group]).astype(jnp.int32)
    f32, bf16 = jnp.float32, jnp.bfloat16

    fields = gather_list(orbitals, "orb")
    weight = quad_weight * (cell_side**3 / point_count)
    own = jnp.concatenate([points, external[None], weight[None], jnp.zeros((3, cells, LANES), f32)], axis=0)
    marks = jnp.pad(level_index.astype(f32), (0, LANES - kinds))[None]
    ends = planes - 1
    up = [(i, i + 1) for i in range(ends)]
    down = [(i + 1, i) for i in range(ends)]
    slots = (near_cells.shape[1], far_cells.shape[1])
    lists = jnp.concatenate([near_cells, far_cells], axis=1)
    partial = jnp.sum(orbitals * orbitals, axis=0)
    basis = pltpu.VMEM((3 * NODES, ROWS, LANES), f32)

    charges = call(
        charge_kernel,
        "charge",
        jax.ShapeDtypeStruct((cells, ROWS, LANES), f32),
        1,
        (meta, own, partial, *fields[1:]),
        [pltpu.VMEM((cells, LANES), f32), basis],
    )
    mine = jnp.concatenate([f.reshape(kinds * cells, LANES) for f in fields], axis=0)
    charges, mine = gather_parts(charges, "space", False, mine)
    before = lax.ppermute(mine, "space", up)

    batch, unit, steps = 4, 4, 9
    most = near_cells.shape[1]
    blocks = most + (window - most + planes + 1) // 2
    blocks = -(-blocks // unit) * unit + unit
    shares, pts, src = call(
        functools.partial(hartree_kernel, groups, kinds, unit, slots),
        "hartree",
        (
            jax.ShapeDtypeStruct((1 + groups, ROWS, LANES), f32),
            jax.ShapeDtypeStruct((window, ROWS, LANES), f32),
            jax.ShapeDtypeStruct((share, blocks, ROWS, LANES), f32),
        ),
        2,
        (meta, lists, marks, mine, *charges),
        [
            pltpu.VMEM((planes, cells, ROWS, LANES), f32),
            pltpu.VMEM((window + planes + 1, ROWS, LANES), f32),
            pltpu.VMEM((3, LANES, LANES), f32),
            basis,
        ],
        12,
    )
    mine, shares = lax.optimization_barrier((mine, shares))
    after = lax.ppermute(mine, "space", down)
    dist, inv = call(
        functools.partial(pairs_kernel, groups, planes, unit, slots),
        "pairs",
        (jax.ShapeDtypeStruct((share, blocks, LANES, LANES), f32),) * 2,
        2,
        (meta, lists, pts, src),
        [pltpu.VMEM((3, LANES, LANES), f32)],
        4,
    )
    shares = gather_list(shares, "orb")
    levels = jnp.concatenate([share[0, ROWS - 1, :kinds] for share in shares] + [screening])
    hartree, combined = call(
        functools.partial(combine_kernel, kinds),
        "combine",
        (jax.ShapeDtypeStruct((cells, LANES), f32), jax.ShapeDtypeStruct((cells + orbs // 2, LANES), f32)),
        1,
        (meta, *shares),
        [pltpu.VMEM((orbs, LANES), f32)],
    )
    gathered, _ = gather_parts(combined, "space", False)

    levels_at_most = -(-screening.shape[0] // batch) + 1
    sent = call(
        functools.partial(orbital_kernel, planes, batch, unit, steps, slots),
        "orbitals",
        jax.ShapeDtypeStruct((groups, share, kinds, LANES), f32),
        3,
        (meta, lists, levels, pts, before, mine, after, dist, inv, *gathered),
        [
            pltpu.SMEM((screening.shape[0] + 2 * batch,), f32),
            pltpu.SMEM((screening.shape[0],), jnp.int32),
            pltpu.VMEM((planes, cells + orbs // 2, LANES), f32),
            pltpu.VMEM((window, LANES, 2 * orbs), bf16),
            pltpu.VMEM((window + planes, HALF, 2 * orbs), bf16),
            pltpu.VMEM((blocks, LANES, 2 * orbs), bf16),
            pltpu.VMEM((levels_at_most, batch * LANES, 2 * orbs), f32),
            basis,
        ],
        14,
    )
    parts = [sent[0]]
    for k in range(1, groups):
        parts.append(lax.ppermute(sent[k], "orb", [(i, i ^ k) for i in range(groups)]))
    updated = call(
        place_kernel,
        "place",
        jax.ShapeDtypeStruct((kinds, cells, LANES), f32),
        1,
        (meta, *parts),
        [pltpu.VMEM((cells, kinds, LANES), f32)],
    )
    return updated, hartree


def solution(mesh):
    in_specs = (
        P("orb", "space", None),
        P(None, "space", None),
        P("space", None),
        P("space", None),
        P(),
        P("orb"),
        P("space", None),
        P("space", None),
    )
    out_specs = (P("orb", "space", None), P("space", None))
    return jax.shard_map(body, mesh=mesh, in_specs=in_specs, out_specs=out_specs, check_vma=False)
```

```python
import functools
import math

import jax
import jax.numpy as jnp
import numpy as np
from jax import lax
from jax.experimental import pallas as pl
from jax.experimental.pallas import tpu as pltpu
from jax.sharding import PartitionSpec as P

NODES = 4
LANES = 128
PLANE = 16
ROWS = 8
HALF = NODES**3

cell_side = 0.25
soften = 6.25e-06
green_scale = -0.5 / math.pi
log2e = math.log2(math.e)
highest = lax.Precision.HIGHEST

node_set = np.cos((2.0 * np.arange(NODES) + 1.0) * (math.pi / (2.0 * NODES)))
roots = [[node_set[m] for m in range(NODES) if m != a] for a in range(NODES)]
scales = [1.0 / np.prod([node_set[a] - r for r in roots[a]]) for a in range(NODES)]


def put_basis(cst):
    row = lax.broadcasted_iota(jnp.int32, (ROWS, LANES), 0)
    for i, pick in enumerate((row // 4, 2 + row // 4, row % 4)):
        for k in range(NODES):
            values = [float(scales[a] if k == NODES - 1 else roots[a][k]) for a in range(NODES)]
            made = jnp.full((ROWS, LANES), values[0], jnp.float32)
            for a in range(1, NODES):
                made = jnp.where(pick == a, values[a], made)
            cst[NODES * i + k] = made


def node_offsets():
    lane = lax.broadcasted_iota(jnp.int32, (1, LANES), 1) % HALF
    out = []
    for pick in (lane // 16, lane // 4 % 4, lane % 4):
        made = jnp.full((1, LANES), 0.5 * (node_set[0] + 1.0), jnp.float32)
        for a in range(1, NODES):
            made = jnp.where(pick == a, float(0.5 * (node_set[a] + 1.0)), made)
        out.append(made)
    return out


def poly(u, r0, r1, r2, scale):
    return ((u - r0) * (u - r1)) * ((u - r2) * scale)


def weights(cst, x, y, z, lows, sides):
    ux, uy, uz = (
        jnp.broadcast_to(2.0 * (c - lo) / e - 1.0, (ROWS, LANES)) for c, lo, e in zip((x, y, z), lows, sides)
    )
    pz = poly(uz, cst[8], cst[9], cst[10], cst[11])
    pyz = [poly(uy, cst[4 * k], cst[4 * k + 1], cst[4 * k + 2], cst[4 * k + 3]) * pz for k in range(2)]
    parts = []
    for a in range(NODES):
        px = poly(ux, *(float(r) for r in roots[a]), float(scales[a]))
        parts += [px * pyz[0], px * pyz[1]]
    return jnp.concatenate(parts, axis=0)


def twice(w):
    return jnp.concatenate([w, w], axis=0)


def cell_low(cell):
    return [(cell % 4).astype(jnp.float32) * cell_side, (cell // 4 % 4).astype(jnp.float32) * cell_side]


def dot_nt(a, b):
    return lax.dot_general(a, b, (((1,), (1,)), ((), ())), precision=highest, preferred_element_type=jnp.float32)


def gather_parts(block, axis, pairs, later=None):
    count = lax.axis_size(axis)
    parts = [block[None]]
    while sum(p.shape[0] for p in parts) < count:
        held = parts[0] if len(parts) == 1 else jnp.concatenate(parts, axis=0)
        have = held.shape[0]
        steps = range(1, 4 if (have > 1 or pairs) and have * 4 <= count else 2)
        parts = [held] + [lax.ppermute(held, axis, [(i, i ^ (have * j)) for i in range(count)]) for j in steps]
        if later is not None and have == 1:
            parts[1], later = lax.optimization_barrier((parts[1], later))
    return parts, later


def gather_list(block, axis):
    parts, _ = gather_parts(block, axis, True)
    return [p[k] for p in parts for k in range(p.shape[0])]


def lay_out(parts, whole):
    at = 0
    for part in parts:
        for k in range(part.shape[0]):
            whole[at + k] = part[k]
        at += part.shape[0]


def target_cell(me, t, groups):
    return t * groups + lax.bitwise_xor(jnp.int32(t) if isinstance(t, int) else t, me)


def split(v):
    high = v.astype(jnp.bfloat16)
    return high, (v - high.astype(jnp.float32)).astype(jnp.bfloat16)


def dot_bf16(a, b):
    return lax.dot_general(a, b, (((1,), (1,)), ((), ())), preferred_element_type=jnp.float32)


def dot_split(v, w):
    vh, vl = split(v)
    wh, wl = split(w)
    rows = v.shape[0]
    both = dot_bf16(jnp.concatenate([vh, vl], axis=0), wh)
    return both[:rows] + both[rows:] + dot_bf16(vh, wl)


def lane_sums(v):
    high, low = split(v)
    ones = jnp.ones((ROWS, 2 * v.shape[1]), jnp.bfloat16)
    return dot_bf16(ones, jnp.concatenate([high, low], axis=1))[0:1, :]


def charge_kernel(meta, own, partial, *refs):
    z_low = meta[0].astype(jnp.float32) * cell_side
    fields, (out, density, cst) = refs[:-3], refs[-3:]
    put_basis(cst)
    total = partial[...]
    for phi in fields:
        for j in range(phi.shape[0]):
            v = phi[j]
            total = total + v * v
    density[...] = 2.0 * total
    acc = jnp.zeros((HALF, LANES), jnp.float32)
    for c in range(PLANE):
        point = own[:, c, :]
        charge = point[4:5] * density[c : c + 1, :]
        low = (cell_side * (c % 4), cell_side * (c // 4), z_low)
        acc = acc + weights(cst, point[0:1], point[1:2], point[2:3], (0.0, 0.0, z_low), (1.0, 1.0, cell_side)) * charge
        moments = lane_sums(weights(cst, point[0:1], point[1:2], point[2:3], low, (cell_side,) * 3) * charge)
        out[c, :5, :] = point[:5]
        out[c, 5:6, :] = charge
        out[c, 6:7, :] = jnp.concatenate([moments, moments], axis=1)
    moments = lane_sums(acc)
    for c in range(PLANE):
        out[c, 7:8, :] = jnp.concatenate([moments, moments], axis=1)


def live_planes(me, planes):
    below = jnp.maximum(me - 1, 0)
    return below, below + jnp.maximum(planes - 2 - me, 0)


def list_lengths(lists, cell, slots, me, planes):
    low, high = jnp.int32(0), jnp.int32(slots[0])
    for _ in range(slots[0].bit_length()):
        mid = (low + high) // 2
        live = (low < high) & (lists[cell, jnp.minimum(mid, slots[0] - 1)] >= 0)
        high = jnp.where(live | (low >= high), high, mid)
        low = jnp.where(live, mid + 1, low)
    around = 1 + (me > 0).astype(jnp.int32) + (me + 1 < planes).astype(jnp.int32)
    return low, around * PLANE - low


def list_blocks(me, cell, lists, slots, planes, put_near, put_far, put_none, multiple):
    window = 3 * PLANE
    base = (me - 1) * PLANE
    below, n_planes = live_planes(me, planes)
    near_slots, far_slots = slots
    n_near, n_far = list_lengths(lists, cell, slots, me, planes)
    n_items = n_far + n_planes
    n_pairs = (n_items + 1) // 2

    def near_step(j, c):
        put_near(j, lists[cell, j] - base)
        return c

    lax.fori_loop(0, n_near, near_step, 0)

    def item(j):
        j = jnp.minimum(j, n_items - 1)
        p = j - n_far
        level = jnp.where(p < below, p, p + (me + 2 - below))
        slot = lists[cell, near_slots + jnp.minimum(j, far_slots - 1)] - base
        return jnp.where(j < n_far, slot, window + level)

    def far_step(j, c):
        put_far(n_near + j, item(2 * j), item(2 * j + 1), 2 * j + 1 < n_items)
        return c

    lax.fori_loop(0, n_pairs, far_step, 0)
    for u in range(multiple - 1):
        put_none(n_near + n_pairs + u)
    return n_near + n_pairs


def in_low_half():
    return lax.broadcasted_iota(jnp.int32, (1, LANES), 1) < HALF


def put_targets(pts, cell, tgt):
    for d in range(3):
        tgt[d] = jnp.broadcast_to(pts[PLANE + cell, d : d + 1, :], (LANES, LANES)).T


def each_square(tgt, src, first, count, use):
    sources = [[src[first + u, d : d + 1, :] for d in range(3)] for u in range(count)]
    for r in range(LANES // ROWS):
        at = [tgt[d, r * ROWS : (r + 1) * ROWS, :] for d in range(3)]
        for u in range(count):
            dx, dy, dz = (a - b for a, b in zip(at, sources[u]))
            use(r, u, (dx * dx + dy * dy) + (dz * dz + soften))


def cell_fields(message, c, groups, kinds):
    rows = kinds * PLANE
    return jnp.concatenate([message[pl.ds(g * rows + c, kinds, stride=PLANE), :] for g in range(groups)], axis=0)


def hartree_kernel(groups, kinds, unroll, slots, meta, lists, marks, mine, *refs):
    parts, (out, pts, src, every, items, tgt, sums, cst) = refs[:-8], refs[-8:]
    lay_out(parts, every)
    planes = every.shape[0]
    cells = PLANE // groups
    me, group = meta[0], meta[1]
    window = 3 * PLANE
    put_basis(cst)
    for k in range(3):
        there = lax.bitwise_xor(me, jnp.clip(me - 1 + k, 0, planes - 1))
        for c in range(PLANE):
            pts[k * PLANE + c] = every[there, c]
    row = lax.broadcasted_iota(jnp.int32, (ROWS, 1), 0)

    offsets = node_offsets()

    def item_of(lows, sides, moments):
        made = jnp.where(row == 5, moments, 0.0)
        for d in range(3):
            made = jnp.where(row == d, lows[d] + offsets[d] * sides[d], made)
        return made

    def put_cell(c, carry):
        lows = (*cell_low(c), (me - 1 + c // PLANE).astype(jnp.float32) * cell_side)
        items[c] = item_of(lows, (cell_side,) * 3, pts[c, 6:7, :])
        return carry

    lax.fori_loop(0, window, put_cell, 0, unroll=8)

    def put_plane(g, c):
        lows = (0.0, 0.0, g.astype(jnp.float32) * cell_side)
        items[window + g] = item_of(lows, (1.0, 1.0, cell_side), every[lax.bitwise_xor(me, g), 0, 7:8, :])
        return c

    lax.fori_loop(0, planes, put_plane, 0)
    items[window + planes] = jnp.zeros((ROWS, LANES), jnp.float32)
    low_half = in_low_half()
    z_low = me.astype(jnp.float32) * cell_side
    out[0] = jnp.broadcast_to(marks[...], (ROWS, LANES))

    def per_cell(t, carry):
        cell = target_cell(group, t, groups)

        def put_near(j, slot):
            src[t, j] = pts[slot]

        def put_far(j, first, second, live):
            src[t, j] = jnp.where(low_half, items[first], items[jnp.where(live, second, window + planes)])

        def put_none(j):
            src[t, j] = jnp.zeros((ROWS, LANES), jnp.float32)

        n_blocks = list_blocks(me, cell, lists, slots, planes, put_near, put_far, put_none, unroll)
        put_targets(pts, cell, tgt)

        def step(i, accs):
            accs = list(accs)
            charges = [src[t, unroll * i + u, 5:6, :] for u in range(unroll)]

            def use(r, u, sq):
                accs[r] = accs[r] + lax.rsqrt(sq) * charges[u]

            each_square(tgt, src.at[t], unroll * i, unroll, use)
            return tuple(accs)

        zero = jnp.zeros((ROWS, LANES), jnp.float32)
        accs = lax.fori_loop(0, (n_blocks + unroll - 1) // unroll, step, (zero,) * (LANES // ROWS))
        sums[t] = jnp.concatenate(accs, axis=0)
        return carry

    lax.fori_loop(0, cells, per_cell, 0)
    ones = jnp.ones((ROWS, LANES), jnp.float32)
    found = dot_nt(ones, sums[...].reshape(cells * LANES, LANES))
    total = jnp.zeros((groups * kinds, LANES), jnp.float32)
    for t in range(cells):
        cell = target_cell(group, t, groups)
        potential = found[0:1, t * LANES : (t + 1) * LANES]
        out[0, t : t + 1, :] = potential
        point = pts[PLANE + cell]
        scaled = point[4:5] * (point[3:4] + potential)
        v = cell_fields(mine, cell, groups, kinds) * scaled
        w = weights(cst, point[0:1], point[1:2], point[2:3], (0.0, 0.0, z_low), (1.0, 1.0, cell_side))
        total = total + dot_split(v, twice(w))
    for k in range(groups):
        out[1 + lax.bitwise_xor(group, k), :kinds, :] = total[k * kinds : (k + 1) * kinds, :]


def pairs_kernel(groups, planes, unroll, slots, meta, lists, pts, src, out, tgt):
    group = meta[1]
    _, n_planes = live_planes(meta[0], planes)

    def per_cell(t, carry):
        cell = target_cell(group, t, groups)
        put_targets(pts, cell, tgt)
        n_near, n_far = list_lengths(lists, cell, slots, meta[0], planes)
        n_blocks = n_near + (n_far + n_planes + 1) // 2

        def measure(i, x):
            def use(r, u, sq):
                out[t, unroll * i + u, r * ROWS : (r + 1) * ROWS, :] = sq

            each_square(tgt, src.at[t], unroll * i, unroll, use)
            return x

        lax.fori_loop(0, (n_blocks + unroll - 1) // unroll, measure, 0)
        return carry

    lax.fori_loop(0, PLANE // groups, per_cell, 0)


def combine_kernel(kinds, meta, *refs):
    shares, (hartree, out, total) = refs[:-3], refs[-3:]
    groups = len(shares)
    for k, share in enumerate(shares):
        for t in range(PLANE // groups):
            cell = target_cell(lax.bitwise_xor(meta[1], k), t, groups)
            out[pl.ds(cell, 1), :] = share[0, t : t + 1, :]
    hartree[...] = out[:PLANE, :]
    for g in range(groups):
        added = shares[0][1 + g, :kinds, :]
        for share in shares[1:]:
            added = added + share[1 + g, :kinds, :]
        total[g * kinds : (g + 1) * kinds, :] = added
    rows = groups * kinds // 2
    low_half = lax.broadcasted_iota(jnp.int32, (1, LANES), 1) < HALF
    out[PLANE:, :] = jnp.where(low_half, total[:rows, :], total[rows:, :])


def orbital_kernel(
    planes, batch, unit, steps, slots, meta, lists, levels, rates_of,
    pts, before, mine, after, squares, *refs,
):
    parts, (out, rate, slot_of, every, val, mom, srcv, dist, inv, acc, cst) = refs[:-11], refs[-11:]
    lay_out(parts, every)
    groups, cells, kinds, _ = out.shape
    orbs = groups * kinds
    n_rates = rates_of.shape[0]
    me, group = meta[0], meta[1]

    def clear(i, c):
        slot_of[i] = -1
        rate[i] = 0.0
        return c

    lax.fori_loop(0, n_rates, clear, 0)
    for q in range(2 * batch):
        rate[n_rates + q] = 0.0
    lane = lax.broadcasted_iota(jnp.int32, (1, LANES), 1) % orbs

    def rank(i, carry):
        found, lane_slot = carry
        level = levels[i]
        known = slot_of[level]
        slot = jnp.where(known < 0, found, known)
        slot_of[level] = slot
        rate[slot] = rates_of[level]
        return found + (known < 0).astype(jnp.int32), jnp.where(lane == i, slot, lane_slot)

    n_levels, lane_slot = lax.fori_loop(0, orbs, rank, (jnp.int32(0), jnp.zeros((1, LANES), jnp.int32)))
    n_batches = (n_levels + batch - 1) // batch
    first_half = lax.broadcasted_iota(jnp.int32, (1, 2 * orbs), 1) < orbs
    put_basis(cst)

    def flip(v):
        high = v.astype(jnp.bfloat16).astype(jnp.float32)
        square = jnp.concatenate([high, v - high, jnp.zeros((LANES - 2 * orbs, LANES), jnp.float32)], axis=0)
        return square.T[:, : 2 * orbs].astype(jnp.bfloat16)

    for k in range(3):
        message = (before, mine, after)[k]
        there = lax.bitwise_xor(me, jnp.clip(me - 1 + k, 0, planes - 1))

        def prepare(c, carry):
            at = k * PLANE + c
            point = pts[at]
            potential = point[3:4] + every[there, pl.ds(c, 1), :]
            v = cell_fields(message, c, groups, kinds) * (point[4:5] * potential)
            val[at] = flip(v)
            vh, vl = split(v)
            z_low = (me - 1 + k).astype(jnp.float32) * cell_side
            low = (*cell_low(c), z_low)
            wh, wl = split(weights(cst, point[0:1], point[1:2], point[2:3], low, (cell_side,) * 3))
            all_of = dot_bf16(jnp.concatenate([wh, wl], axis=0), jnp.concatenate([vh, vh, vl, vl], axis=0))
            m = all_of[:HALF] + all_of[HALF:]
            m = m[:, : 2 * orbs] + pltpu.roll(all_of[:HALF], 2 * orbs, 1)[:, : 2 * orbs]
            high = m.astype(jnp.bfloat16).astype(jnp.float32)
            mom[at] = jnp.where(first_half, high, m - high).astype(jnp.bfloat16)
            return carry

        lax.fori_loop(0, PLANE, prepare, 0, unroll=4)

    def put_plane(g, c):
        there = lax.bitwise_xor(me, g)
        rows = []
        for k in range(groups):
            row = lax.bitwise_xor(group, k) * kinds
            v = every[there, pl.ds(PLANE + lax.rem(row, orbs // 2), kinds), :]
            rows.append(jnp.where(row < orbs // 2, v, pltpu.roll(v, HALF, 1)))
        mom[3 * PLANE + g] = flip(jnp.concatenate(rows, axis=0))[:HALF]
        return c

    lax.fori_loop(0, planes, put_plane, 0)

    def put_near(j, slot):
        srcv[j] = val[slot]

    def put_far(j, first, second, live):
        srcv[j, :HALF, :] = mom[first]
        srcv[j, HALF:, :] = jnp.where(live, mom[second], jnp.zeros_like(mom[second]))

    def put_none(j):
        srcv[j] = jnp.zeros(srcv.shape[1:], srcv.dtype)

    def products(b, first):
        rates = [rate[b * batch + q] for q in range(batch)]
        rows = []
        for q in range(batch):
            tiles = [(jnp.exp2(dist[first + h] * rates[q]) * inv[first + h]).astype(jnp.bfloat16) for h in range(unit)]
            rows.append(jnp.concatenate(tiles, axis=1))
        v = jnp.concatenate([srcv[first + h] for h in range(unit)], axis=0)
        return jnp.dot(jnp.concatenate(rows, axis=0), v, preferred_element_type=jnp.float32)

    def per_cell(t, carry):
        cell = target_cell(group, t, groups)
        n_blocks = list_blocks(me, cell, lists, slots, planes, put_near, put_far, put_none, unit)
        n_units = (n_blocks + unit - 1) // unit

        def measure(i, x):
            for u in range(unit):
                sq = squares[t, unit * i + u]
                one_over = lax.rsqrt(sq)
                inv[unit * i + u] = one_over
                dist[unit * i + u] = sq * one_over
            return x

        lax.fori_loop(0, n_units, measure, 0)

        def clear_acc(b, x):
            acc[b] = jnp.zeros(acc.shape[1:], jnp.float32)
            return x

        lax.fori_loop(0, n_batches, clear_acc, 0)

        def step(i, at):
            b, u = at
            for _ in range(steps):
                acc[b] = acc[b] + products(b, unit * u)
                wrap = u + 1 == n_units
                b, u = jnp.where(wrap, b + 1, b), jnp.where(wrap, 0, u + 1)
            return b, u

        lax.fori_loop(0, (n_batches * n_units + steps - 1) // steps, step, (jnp.int32(0), jnp.int32(0)))

        def choose(b, add):
            for q in range(batch):
                mine = lane_slot[:, : 2 * orbs] == b * batch + q
                add = add + jnp.where(mine, acc[b, q * LANES : (q + 1) * LANES, :], 0.0)
            return add

        total = lax.fori_loop(0, n_batches, choose, jnp.zeros((LANES, 2 * orbs), jnp.float32))
        flipped = jnp.concatenate([total, jnp.zeros((LANES, LANES - 2 * orbs), jnp.float32)], axis=1).T
        rows = (flipped[:orbs] + flipped[orbs : 2 * orbs]) * green_scale
        for k in range(groups):
            out[k, t] = rows[k * kinds : (k + 1) * kinds]
        return carry

    lax.fori_loop(0, cells, per_cell, 0)


def place_kernel(meta, *refs):
    parts, out, ordered = refs[:-2], refs[-2], refs[-1]
    for k, part in enumerate(parts):
        for t in range(part.shape[0]):
            ordered[target_cell(lax.bitwise_xor(meta[1], k), t, len(parts))] = part[t]
    for c in range(PLANE):
        out[:, c, :] = ordered[c]


def smem():
    return pl.BlockSpec(memory_space=pltpu.SMEM)


def vmem():
    return pl.BlockSpec(memory_space=pltpu.VMEM)


def call(kernel, name, out_shape, smems, args, scratch=(), mib=8):
    return pl.pallas_call(
        kernel,
        out_shape=out_shape,
        in_specs=[smem()] * smems + [vmem()] * (len(args) - smems),
        out_specs=jax.tree.map(lambda _: vmem(), out_shape),
        scratch_shapes=scratch,
        compiler_params=pltpu.CompilerParams(vmem_limit_bytes=mib * 1024 * 1024),
        name=name,
    )(*args)


def body(orbitals, points, quad_weight, external, screening, level_index, near_cells, far_cells):
    kinds, cells, point_count = orbitals.shape
    planes, groups = lax.axis_size("space"), lax.axis_size("orb")
    orbs = kinds * groups
    window = 3 * PLANE
    share = cells // groups
    me, group = lax.axis_index("space"), lax.axis_index("orb")
    meta = jnp.stack([me, group]).astype(jnp.int32)
    f32, bf16 = jnp.float32, jnp.bfloat16

    fields = gather_list(orbitals, "orb")
    weight = quad_weight * (cell_side**3 / point_count)
    own = jnp.concatenate([points, external[None], weight[None], jnp.zeros((3, cells, LANES), f32)], axis=0)
    marks = jnp.pad(level_index.astype(f32), (0, LANES - kinds))[None]
    ends = planes - 1
    up = [(i, i + 1) for i in range(ends)]
    down = [(i + 1, i) for i in range(ends)]
    slots = (near_cells.shape[1], far_cells.shape[1])
    lists = jnp.concatenate([near_cells, far_cells], axis=1)
    partial = jnp.sum(orbitals * orbitals, axis=0)
    basis = pltpu.VMEM((3 * NODES, ROWS, LANES), f32)

    charges = call(
        charge_kernel,
        "charge",
        jax.ShapeDtypeStruct((cells, ROWS, LANES), f32),
        1,
        (meta, own, partial, *fields[1:]),
        [pltpu.VMEM((cells, LANES), f32), basis],
    )
    mine = jnp.concatenate([f.reshape(kinds * cells, LANES) for f in fields], axis=0)
    charges, mine = gather_parts(charges, "space", False, mine)
    before = lax.ppermute(mine, "space", up)

    batch, unit, steps = 4, 4, 9
    most = near_cells.shape[1]
    blocks = most + (window - most + planes - 2) // 2 + unit - 1
    blocks = -(-blocks // unit) * unit
    shares, pts, src = call(
        functools.partial(hartree_kernel, groups, kinds, unit, slots),
        "hartree",
        (
            jax.ShapeDtypeStruct((1 + groups, ROWS, LANES), f32),
            jax.ShapeDtypeStruct((window, ROWS, LANES), f32),
            jax.ShapeDtypeStruct((share, blocks, ROWS, LANES), f32),
        ),
        2,
        (meta, lists, marks, mine, *charges),
        [
            pltpu.VMEM((planes, cells, ROWS, LANES), f32),
            pltpu.VMEM((window + planes + 1, ROWS, LANES), f32),
            pltpu.VMEM((3, LANES, LANES), f32),
            pltpu.VMEM((share, LANES, LANES), f32),
            basis,
        ],
        12,
    )
    mine, shares = lax.optimization_barrier((mine, shares))
    after = lax.ppermute(mine, "space", down)
    squares = call(
        functools.partial(pairs_kernel, groups, planes, unit, slots),
        "pairs",
        jax.ShapeDtypeStruct((share, blocks, LANES, LANES), f32),
        2,
        (meta, lists, pts, src),
        [pltpu.VMEM((3, LANES, LANES), f32)],
        4,
    )
    shares = gather_list(shares, "orb")
    levels = jnp.concatenate([share[0, ROWS - 1, :kinds] for share in shares]).astype(jnp.int32)
    hartree, combined = call(
        functools.partial(combine_kernel, kinds),
        "combine",
        (jax.ShapeDtypeStruct((cells, LANES), f32), jax.ShapeDtypeStruct((cells + orbs // 2, LANES), f32)),
        1,
        (meta, *shares),
        [pltpu.VMEM((orbs, LANES), f32)],
    )
    gathered, _ = gather_parts(combined, "space", False)

    levels_at_most = -(-screening.shape[0] // batch) + 1
    sent = call(
        functools.partial(orbital_kernel, planes, batch, unit, steps, slots),
        "orbitals",
        jax.ShapeDtypeStruct((groups, share, kinds, LANES), f32),
        4,
        (meta, lists, levels, screening * (-log2e), pts, before, mine, after, squares, *gathered),
        [
            pltpu.SMEM((screening.shape[0] + 2 * batch,), f32),
            pltpu.SMEM((screening.shape[0],), jnp.int32),
            pltpu.VMEM((planes, cells + orbs // 2, LANES), f32),
            pltpu.VMEM((window, LANES, 2 * orbs), bf16),
            pltpu.VMEM((window + planes, HALF, 2 * orbs), bf16),
            pltpu.VMEM((blocks, LANES, 2 * orbs), bf16),
            pltpu.VMEM((blocks, LANES, LANES), f32),
            pltpu.VMEM((blocks, LANES, LANES), f32),
            pltpu.VMEM((levels_at_most, batch * LANES, 2 * orbs), f32),
            basis,
        ],
        20,
    )
    parts = [sent[0]]
    for k in range(1, groups):
        parts.append(lax.ppermute(sent[k], "orb", [(i, i ^ k) for i in range(groups)]))
    updated = call(
        place_kernel,
        "place",
        jax.ShapeDtypeStruct((kinds, cells, LANES), f32),
        1,
        (meta, *parts),
        [pltpu.VMEM((cells, kinds, LANES), f32)],
    )
    return updated, hartree


def solution(mesh):
    in_specs = (
        P("orb", "space", None),
        P(None, "space", None),
        P("space", None),
        P("space", None),
        P(),
        P("orb"),
        P("space", None),
        P("space", None),
    )
    out_specs = (P("orb", "space", None), P("space", None))
    return jax.shard_map(body, mesh=mesh, in_specs=in_specs, out_specs=out_specs, check_vma=False)
```

```python
import functools
import math

import jax
import jax.numpy as jnp
import numpy as np
from jax import lax
from jax.experimental import pallas as pl
from jax.experimental.pallas import tpu as pltpu
from jax.sharding import PartitionSpec as P

NODES = 4
LANES = 128
PLANE = 16
ROWS = 8
HALF = NODES**3

cell_side = 0.25
soften = 6.25e-06
green_scale = -0.5 / math.pi
log2e = math.log2(math.e)
highest = lax.Precision.HIGHEST

node_set = np.cos((2.0 * np.arange(NODES) + 1.0) * (math.pi / (2.0 * NODES)))
roots = [[node_set[m] for m in range(NODES) if m != a] for a in range(NODES)]
scales = [1.0 / np.prod([node_set[a] - r for r in roots[a]]) for a in range(NODES)]


def put_basis(cst):
    row = lax.broadcasted_iota(jnp.int32, (ROWS, LANES), 0)
    for i, pick in enumerate((row // 4, 2 + row // 4, row % 4)):
        for k in range(NODES):
            values = [float(scales[a] if k == NODES - 1 else roots[a][k]) for a in range(NODES)]
            made = jnp.full((ROWS, LANES), values[0], jnp.float32)
            for a in range(1, NODES):
                made = jnp.where(pick == a, values[a], made)
            cst[NODES * i + k] = made


def node_offsets():
    lane = lax.broadcasted_iota(jnp.int32, (1, LANES), 1) % HALF
    out = []
    for pick in (lane // 16, lane // 4 % 4, lane % 4):
        made = jnp.full((1, LANES), 0.5 * (node_set[0] + 1.0), jnp.float32)
        for a in range(1, NODES):
            made = jnp.where(pick == a, float(0.5 * (node_set[a] + 1.0)), made)
        out.append(made)
    return out


def poly(u, r0, r1, r2, scale):
    return ((u - r0) * (u - r1)) * ((u - r2) * scale)


def weights(cst, x, y, z, lows, sides):
    ux, uy, uz = (
        jnp.broadcast_to(2.0 * (c - lo) / e - 1.0, (ROWS, LANES)) for c, lo, e in zip((x, y, z), lows, sides)
    )
    pz = poly(uz, cst[8], cst[9], cst[10], cst[11])
    pyz = [poly(uy, cst[4 * k], cst[4 * k + 1], cst[4 * k + 2], cst[4 * k + 3]) * pz for k in range(2)]
    parts = []
    for a in range(NODES):
        px = poly(ux, *(float(r) for r in roots[a]), float(scales[a]))
        parts += [px * pyz[0], px * pyz[1]]
    return jnp.concatenate(parts, axis=0)


def twice(w):
    return jnp.concatenate([w, w], axis=0)


def cell_low(cell):
    return [(cell % 4).astype(jnp.float32) * cell_side, (cell // 4 % 4).astype(jnp.float32) * cell_side]


def dot_nt(a, b):
    return lax.dot_general(a, b, (((1,), (1,)), ((), ())), precision=highest, preferred_element_type=jnp.float32)


def gather_parts(block, axis, pairs, later=None):
    count = lax.axis_size(axis)
    parts = [block[None]]
    while sum(p.shape[0] for p in parts) < count:
        held = parts[0] if len(parts) == 1 else jnp.concatenate(parts, axis=0)
        have = held.shape[0]
        steps = range(1, 4 if (have > 1 or pairs) and have * 4 <= count else 2)
        parts = [held] + [lax.ppermute(held, axis, [(i, i ^ (have * j)) for i in range(count)]) for j in steps]
        if later is not None and have == 1:
            parts[1], later = lax.optimization_barrier((parts[1], later))
    return parts, later


def gather_list(block, axis):
    parts, _ = gather_parts(block, axis, True)
    return [p[k] for p in parts for k in range(p.shape[0])]


def lay_out(parts, whole):
    at = 0
    for part in parts:
        for k in range(part.shape[0]):
            whole[at + k] = part[k]
        at += part.shape[0]


def target_cell(me, t, groups):
    return t * groups + lax.bitwise_xor(jnp.int32(t) if isinstance(t, int) else t, me)


def split(v):
    high = v.astype(jnp.bfloat16)
    return high, (v - high.astype(jnp.float32)).astype(jnp.bfloat16)


def dot_bf16(a, b):
    return lax.dot_general(a, b, (((1,), (1,)), ((), ())), preferred_element_type=jnp.float32)


def dot_split(v, w):
    vh, vl = split(v)
    wh, wl = split(w)
    rows = v.shape[0]
    both = dot_bf16(jnp.concatenate([vh, vl], axis=0), wh)
    return both[:rows] + both[rows:] + dot_bf16(vh, wl)


def lane_sums(v):
    high, low = split(v)
    ones = jnp.ones((ROWS, 2 * v.shape[1]), jnp.bfloat16)
    return dot_bf16(ones, jnp.concatenate([high, low], axis=1))[0:1, :]


def charge_kernel(meta, own, partial, *refs):
    z_low = meta[0].astype(jnp.float32) * cell_side
    fields, (out, density, cst) = refs[:-3], refs[-3:]
    put_basis(cst)
    total = partial[...]
    for phi in fields:
        for j in range(phi.shape[0]):
            v = phi[j]
            total = total + v * v
    density[...] = 2.0 * total
    acc = jnp.zeros((HALF, LANES), jnp.float32)
    for c in range(PLANE):
        point = own[:, c, :]
        charge = point[4:5] * density[c : c + 1, :]
        low = (cell_side * (c % 4), cell_side * (c // 4), z_low)
        acc = acc + weights(cst, point[0:1], point[1:2], point[2:3], (0.0, 0.0, z_low), (1.0, 1.0, cell_side)) * charge
        moments = lane_sums(weights(cst, point[0:1], point[1:2], point[2:3], low, (cell_side,) * 3) * charge)
        out[c, :5, :] = point[:5]
        out[c, 5:6, :] = charge
        out[c, 6:7, :] = jnp.concatenate([moments, moments], axis=1)
    moments = lane_sums(acc)
    for c in range(PLANE):
        out[c, 7:8, :] = jnp.concatenate([moments, moments], axis=1)


def live_planes(me, planes):
    below = jnp.maximum(me - 1, 0)
    return below, below + jnp.maximum(planes - 2 - me, 0)


def list_lengths(lists, cell, slots, me, planes):
    low, high = jnp.int32(0), jnp.int32(slots[0])
    for _ in range(slots[0].bit_length()):
        mid = (low + high) // 2
        live = (low < high) & (lists[cell, jnp.minimum(mid, slots[0] - 1)] >= 0)
        high = jnp.where(live | (low >= high), high, mid)
        low = jnp.where(live, mid + 1, low)
    around = 1 + (me > 0).astype(jnp.int32) + (me + 1 < planes).astype(jnp.int32)
    return low, around * PLANE - low


def list_blocks(me, cell, lists, slots, planes, put_near, put_far, put_none, multiple):
    window = 3 * PLANE
    base = (me - 1) * PLANE
    below, n_planes = live_planes(me, planes)
    near_slots, far_slots = slots
    n_near, n_far = list_lengths(lists, cell, slots, me, planes)
    n_items = n_far + n_planes
    n_pairs = (n_items + 1) // 2

    def near_step(j, c):
        put_near(j, lists[cell, j] - base)
        return c

    lax.fori_loop(0, n_near, near_step, 0)

    def item(j):
        j = jnp.minimum(j, n_items - 1)
        p = j - n_far
        level = jnp.where(p < below, p, p + (me + 2 - below))
        slot = lists[cell, near_slots + jnp.minimum(j, far_slots - 1)] - base
        return jnp.where(j < n_far, slot, window + level)

    def far_step(j, c):
        put_far(n_near + j, item(2 * j), item(2 * j + 1), 2 * j + 1 < n_items)
        return c

    lax.fori_loop(0, n_pairs, far_step, 0)
    for u in range(multiple - 1):
        put_none(n_near + n_pairs + u)
    return n_near + n_pairs


def in_low_half():
    return lax.broadcasted_iota(jnp.int32, (1, LANES), 1) < HALF


def put_targets(pts, cell, tgt):
    for d in range(3):
        tgt[d] = jnp.broadcast_to(pts[PLANE + cell, d : d + 1, :], (LANES, LANES)).T


def each_square(tgt, src, first, count, use):
    sources = [[src[first + u, d : d + 1, :] for d in range(3)] for u in range(count)]
    for r in range(LANES // ROWS):
        at = [tgt[d, r * ROWS : (r + 1) * ROWS, :] for d in range(3)]
        for u in range(count):
            dx, dy, dz = (a - b for a, b in zip(at, sources[u]))
            use(r, u, (dx * dx + dy * dy) + (dz * dz + soften))


def cell_fields(message, c, groups, kinds):
    rows = kinds * PLANE
    return jnp.concatenate([message[pl.ds(g * rows + c, kinds, stride=PLANE), :] for g in range(groups)], axis=0)


def hartree_kernel(groups, kinds, unroll, slots, meta, lists, marks, mine, *refs):
    parts, (out, pts, src, every, items, tgt, sums, cst) = refs[:-8], refs[-8:]
    lay_out(parts, every)
    planes = every.shape[0]
    cells = PLANE // groups
    me, group = meta[0], meta[1]
    window = 3 * PLANE
    put_basis(cst)
    for k in range(3):
        there = lax.bitwise_xor(me, jnp.clip(me - 1 + k, 0, planes - 1))
        for c in range(PLANE):
            pts[k * PLANE + c] = every[there, c]
    row = lax.broadcasted_iota(jnp.int32, (ROWS, 1), 0)

    offsets = node_offsets()

    def item_of(lows, sides, moments):
        made = jnp.where(row == 5, moments, 0.0)
        for d in range(3):
            made = jnp.where(row == d, lows[d] + offsets[d] * sides[d], made)
        return made

    def put_cell(c, carry):
        lows = (*cell_low(c), (me - 1 + c // PLANE).astype(jnp.float32) * cell_side)
        items[c] = item_of(lows, (cell_side,) * 3, pts[c, 6:7, :])
        return carry

    lax.fori_loop(0, window, put_cell, 0, unroll=8)

    def put_plane(g, c):
        lows = (0.0, 0.0, g.astype(jnp.float32) * cell_side)
        items[window + g] = item_of(lows, (1.0, 1.0, cell_side), every[lax.bitwise_xor(me, g), 0, 7:8, :])
        return c

    lax.fori_loop(0, planes, put_plane, 0)
    items[window + planes] = jnp.zeros((ROWS, LANES), jnp.float32)
    low_half = in_low_half()
    z_low = me.astype(jnp.float32) * cell_side
    out[0] = jnp.broadcast_to(marks[...], (ROWS, LANES))

    def per_cell(t, carry):
        cell = target_cell(group, t, groups)

        def put_near(j, slot):
            src[t, j] = pts[slot]

        def put_far(j, first, second, live):
            src[t, j] = jnp.where(low_half, items[first], items[jnp.where(live, second, window + planes)])

        def put_none(j):
            src[t, j] = jnp.zeros((ROWS, LANES), jnp.float32)

        n_blocks = list_blocks(me, cell, lists, slots, planes, put_near, put_far, put_none, unroll)
        put_targets(pts, cell, tgt)

        def step(i, accs):
            accs = list(accs)
            charges = [src[t, unroll * i + u, 5:6, :] for u in range(unroll)]

            def use(r, u, sq):
                accs[r] = accs[r] + lax.rsqrt(sq) * charges[u]

            each_square(tgt, src.at[t], unroll * i, unroll, use)
            return tuple(accs)

        zero = jnp.zeros((ROWS, LANES), jnp.float32)
        accs = lax.fori_loop(0, (n_blocks + unroll - 1) // unroll, step, (zero,) * (LANES // ROWS))
        sums[t] = jnp.concatenate(accs, axis=0)
        return carry

    lax.fori_loop(0, cells, per_cell, 0)
    ones = jnp.ones((ROWS, LANES), jnp.float32)
    found = dot_nt(ones, sums[...].reshape(cells * LANES, LANES))
    total = jnp.zeros((groups * kinds, LANES), jnp.float32)
    for t in range(cells):
        cell = target_cell(group, t, groups)
        potential = found[0:1, t * LANES : (t + 1) * LANES]
        out[0, t : t + 1, :] = potential
        point = pts[PLANE + cell]
        scaled = point[4:5] * (point[3:4] + potential)
        v = cell_fields(mine, cell, groups, kinds) * scaled
        w = weights(cst, point[0:1], point[1:2], point[2:3], (0.0, 0.0, z_low), (1.0, 1.0, cell_side))
        total = total + dot_split(v, twice(w))
    for k in range(groups):
        out[1 + lax.bitwise_xor(group, k), :kinds, :] = total[k * kinds : (k + 1) * kinds, :]


def pairs_kernel(first, groups, planes, unroll, slots, meta, lists, pts, src, out, tgt):
    group = meta[1]
    _, n_planes = live_planes(meta[0], planes)

    def per_cell(t, carry):
        cell = target_cell(group, first + t, groups)
        put_targets(pts, cell, tgt)
        n_near, n_far = list_lengths(lists, cell, slots, meta[0], planes)
        n_blocks = n_near + (n_far + n_planes + 1) // 2

        def measure(i, x):
            def use(r, u, sq):
                out[t, unroll * i + u, r * ROWS : (r + 1) * ROWS, :] = sq

            each_square(tgt, src.at[first + t], unroll * i, unroll, use)
            return x

        lax.fori_loop(0, (n_blocks + unroll - 1) // unroll, measure, 0)
        return carry

    lax.fori_loop(0, out.shape[0], per_cell, 0)


def combine_kernel(kinds, meta, *refs):
    shares, (hartree, out, total) = refs[:-3], refs[-3:]
    groups = len(shares)
    for k, share in enumerate(shares):
        for t in range(PLANE // groups):
            cell = target_cell(lax.bitwise_xor(meta[1], k), t, groups)
            out[pl.ds(cell, 1), :] = share[0, t : t + 1, :]
    hartree[...] = out[:PLANE, :]
    for g in range(groups):
        added = shares[0][1 + g, :kinds, :]
        for share in shares[1:]:
            added = added + share[1 + g, :kinds, :]
        total[g * kinds : (g + 1) * kinds, :] = added
    rows = groups * kinds // 2
    low_half = lax.broadcasted_iota(jnp.int32, (1, LANES), 1) < HALF
    out[PLANE:, :] = jnp.where(low_half, total[:rows, :], total[rows:, :])


def orbital_kernel(
    planes, batch, unit, steps, slots, n_squares, meta, lists, levels, rates_of,
    pts, before, mine, after, *refs,
):
    squares, refs = refs[:n_squares], refs[n_squares:]
    parts, (out, rate, slot_of, units, every, val, mom, srcv, dist, inv, acc, cst) = refs[:-12], refs[-12:]
    lay_out(parts, every)
    groups, cells, kinds, _ = out.shape
    orbs = groups * kinds
    n_rates = rates_of.shape[0]
    me, group = meta[0], meta[1]

    def clear(i, c):
        slot_of[i] = -1
        rate[i] = 0.0
        return c

    lax.fori_loop(0, n_rates, clear, 0)
    for q in range(2 * batch):
        rate[n_rates + q] = 0.0
    lane = lax.broadcasted_iota(jnp.int32, (1, LANES), 1) % orbs

    def rank(i, carry):
        found, lane_slot = carry
        level = levels[i]
        known = slot_of[level]
        slot = jnp.where(known < 0, found, known)
        slot_of[level] = slot
        rate[slot] = rates_of[level]
        return found + (known < 0).astype(jnp.int32), jnp.where(lane == i, slot, lane_slot)

    n_levels, lane_slot = lax.fori_loop(0, orbs, rank, (jnp.int32(0), jnp.zeros((1, LANES), jnp.int32)))
    n_batches = (n_levels + batch - 1) // batch
    first_half = lax.broadcasted_iota(jnp.int32, (1, 2 * orbs), 1) < orbs
    put_basis(cst)

    def flip(v):
        high = v.astype(jnp.bfloat16).astype(jnp.float32)
        square = jnp.concatenate([high, v - high, jnp.zeros((LANES - 2 * orbs, LANES), jnp.float32)], axis=0)
        return square.T[:, : 2 * orbs].astype(jnp.bfloat16)

    for k in range(3):
        message = (before, mine, after)[k]
        there = lax.bitwise_xor(me, jnp.clip(me - 1 + k, 0, planes - 1))

        def prepare(c, carry):
            at = k * PLANE + c
            point = pts[at]
            potential = point[3:4] + every[there, pl.ds(c, 1), :]
            v = cell_fields(message, c, groups, kinds) * (point[4:5] * potential)
            val[at] = flip(v)
            vh, vl = split(v)
            z_low = (me - 1 + k).astype(jnp.float32) * cell_side
            low = (*cell_low(c), z_low)
            wh, wl = split(weights(cst, point[0:1], point[1:2], point[2:3], low, (cell_side,) * 3))
            all_of = dot_bf16(jnp.concatenate([wh, wl], axis=0), jnp.concatenate([vh, vh, vl, vl], axis=0))
            m = all_of[:HALF] + all_of[HALF:]
            m = m[:, : 2 * orbs] + pltpu.roll(all_of[:HALF], 2 * orbs, 1)[:, : 2 * orbs]
            high = m.astype(jnp.bfloat16).astype(jnp.float32)
            mom[at] = jnp.where(first_half, high, m - high).astype(jnp.bfloat16)
            return carry

        lax.fori_loop(0, PLANE, prepare, 0, unroll=4)

    def put_plane(g, c):
        there = lax.bitwise_xor(me, g)
        rows = []
        for k in range(groups):
            row = lax.bitwise_xor(group, k) * kinds
            v = every[there, pl.ds(PLANE + lax.rem(row, orbs // 2), kinds), :]
            rows.append(jnp.where(row < orbs // 2, v, pltpu.roll(v, HALF, 1)))
        mom[3 * PLANE + g] = flip(jnp.concatenate(rows, axis=0))[:HALF]
        return c

    lax.fori_loop(0, planes, put_plane, 0)

    def products(g, b, first):
        rates = [rate[b * batch + q] for q in range(batch)]
        rows = []
        for q in range(batch):
            tiles = [
                (jnp.exp2(dist[g, first + h] * rates[q]) * inv[g, first + h]).astype(jnp.bfloat16) for h in range(unit)
            ]
            rows.append(jnp.concatenate(tiles, axis=1))
        v = jnp.concatenate([srcv[g, first + h] for h in range(unit)], axis=0)
        return jnp.dot(jnp.concatenate(rows, axis=0), v, preferred_element_type=jnp.float32)

    share = cells // n_squares

    def per_group(p, carry):
        def list_cell(g, x):
            def put_near(j, slot):
                srcv[g, j] = val[slot]

            def put_far(j, first, second, live):
                srcv[g, j, :HALF, :] = mom[first]
                srcv[g, j, HALF:, :] = jnp.where(live, mom[second], jnp.zeros_like(mom[second]))

            def put_none(j):
                srcv[g, j] = jnp.zeros(srcv.shape[2:], srcv.dtype)

            cell = target_cell(group, p * share + g, groups)
            n_blocks = list_blocks(me, cell, lists, slots, planes, put_near, put_far, put_none, unit)
            units[g] = (n_blocks + unit - 1) // unit

            def clear_acc(b, y):
                acc[g, b] = jnp.zeros(acc.shape[2:], jnp.float32)
                return y

            lax.fori_loop(0, n_batches, clear_acc, 0)
            return x

        lax.fori_loop(0, share, list_cell, 0)

        for k in range(n_squares):

            @pl.when(p == k)
            def _():
                for g in range(share):

                    def measure(i, x):
                        for u in range(unit):
                            sq = squares[k][g, unit * i + u]
                            one_over = lax.rsqrt(sq)
                            inv[g, unit * i + u] = one_over
                            dist[g, unit * i + u] = sq * one_over
                        return x

                    lax.fori_loop(0, units[g], measure, 0)

        def step(i, at):
            g, b, u = at
            for _ in range(steps):
                acc[g, b] = acc[g, b] + products(g, b, unit * u)
                wrap = u + 1 >= units[g]
                later = jnp.where(wrap, b + 1, b)
                over, last = later >= n_batches, g + 1 >= share
                u = jnp.where(wrap, 0, u + 1)
                b = jnp.where(over, jnp.where(last, n_batches, 0), later)
                g = jnp.where(over & jnp.logical_not(last), g + 1, g)
            return g, b, u

        work = sum(units[g] for g in range(share)) * n_batches
        zero = jnp.int32(0)
        lax.fori_loop(0, (work + steps - 1) // steps, step, (zero, zero, zero))

        def finish(g, x):
            def choose(b, add):
                for q in range(batch):
                    mine = lane_slot[:, : 2 * orbs] == b * batch + q
                    add = add + jnp.where(mine, acc[g, b, q * LANES : (q + 1) * LANES, :], 0.0)
                return add

            total = lax.fori_loop(0, n_batches, choose, jnp.zeros((LANES, 2 * orbs), jnp.float32))
            flipped = jnp.concatenate([total, jnp.zeros((LANES, LANES - 2 * orbs), jnp.float32)], axis=1).T
            rows = (flipped[:orbs] + flipped[orbs : 2 * orbs]) * green_scale
            for k in range(groups):
                out[k, p * share + g] = rows[k * kinds : (k + 1) * kinds]
            return x

        lax.fori_loop(0, share, finish, 0)
        return carry

    lax.fori_loop(0, n_squares, per_group, 0)


def place_kernel(meta, *refs):
    parts, out, ordered = refs[:-2], refs[-2], refs[-1]
    for k, part in enumerate(parts):
        for t in range(part.shape[0]):
            ordered[target_cell(lax.bitwise_xor(meta[1], k), t, len(parts))] = part[t]
    for c in range(PLANE):
        out[:, c, :] = ordered[c]


def smem():
    return pl.BlockSpec(memory_space=pltpu.SMEM)


def vmem():
    return pl.BlockSpec(memory_space=pltpu.VMEM)


def call(kernel, name, out_shape, smems, args, scratch=(), mib=8):
    return pl.pallas_call(
        kernel,
        out_shape=out_shape,
        in_specs=[smem()] * smems + [vmem()] * (len(args) - smems),
        out_specs=jax.tree.map(lambda _: vmem(), out_shape),
        scratch_shapes=scratch,
        compiler_params=pltpu.CompilerParams(vmem_limit_bytes=mib * 1024 * 1024),
        name=name,
    )(*args)


def body(orbitals, points, quad_weight, external, screening, level_index, near_cells, far_cells):
    kinds, cells, point_count = orbitals.shape
    planes, groups = lax.axis_size("space"), lax.axis_size("orb")
    orbs = kinds * groups
    window = 3 * PLANE
    share = cells // groups
    me, group = lax.axis_index("space"), lax.axis_index("orb")
    meta = jnp.stack([me, group]).astype(jnp.int32)
    f32, bf16 = jnp.float32, jnp.bfloat16

    fields = gather_list(orbitals, "orb")
    weight = quad_weight * (cell_side**3 / point_count)
    own = jnp.concatenate([points, external[None], weight[None], jnp.zeros((3, cells, LANES), f32)], axis=0)
    marks = jnp.pad(level_index.astype(f32), (0, LANES - kinds))[None]
    ends = planes - 1
    up = [(i, i + 1) for i in range(ends)]
    down = [(i + 1, i) for i in range(ends)]
    slots = (near_cells.shape[1], far_cells.shape[1])
    lists = jnp.concatenate([near_cells, far_cells], axis=1)
    partial = jnp.sum(orbitals * orbitals, axis=0)
    basis = pltpu.VMEM((3 * NODES, ROWS, LANES), f32)

    charges = call(
        charge_kernel,
        "charge",
        jax.ShapeDtypeStruct((cells, ROWS, LANES), f32),
        1,
        (meta, own, partial, *fields[1:]),
        [pltpu.VMEM((cells, LANES), f32), basis],
    )
    mine = jnp.concatenate([f.reshape(kinds * cells, LANES) for f in fields], axis=0)
    charges, mine = gather_parts(charges, "space", False, mine)
    before = lax.ppermute(mine, "space", up)

    batch, unit, steps = 4, 4, 18
    most = near_cells.shape[1]
    blocks = most + (window - most + planes - 2) // 2 + unit - 1
    blocks = -(-blocks // unit) * unit
    shares, pts, src = call(
        functools.partial(hartree_kernel, groups, kinds, unit, slots),
        "hartree",
        (
            jax.ShapeDtypeStruct((1 + groups, ROWS, LANES), f32),
            jax.ShapeDtypeStruct((window, ROWS, LANES), f32),
            jax.ShapeDtypeStruct((share, blocks, ROWS, LANES), f32),
        ),
        2,
        (meta, lists, marks, mine, *charges),
        [
            pltpu.VMEM((planes, cells, ROWS, LANES), f32),
            pltpu.VMEM((window + planes + 1, ROWS, LANES), f32),
            pltpu.VMEM((3, LANES, LANES), f32),
            pltpu.VMEM((share, LANES, LANES), f32),
            basis,
        ],
        12,
    )
    mine, shares = lax.optimization_barrier((mine, shares))
    after = lax.ppermute(mine, "space", down)
    n_squares = 2 if share % 2 == 0 else 1

    def distances(k, src):
        return call(
            functools.partial(pairs_kernel, k * share // n_squares, groups, planes, unit, slots),
            "pairs",
            jax.ShapeDtypeStruct((share // n_squares, blocks, LANES, LANES), f32),
            2,
            (meta, lists, pts, src),
            [pltpu.VMEM((3, LANES, LANES), f32)],
            4,
        )

    squares = [distances(0, src)]
    shares = gather_list(shares, "orb")
    levels = jnp.concatenate([share[0, ROWS - 1, :kinds] for share in shares]).astype(jnp.int32)
    hartree, combined = call(
        functools.partial(combine_kernel, kinds),
        "combine",
        (jax.ShapeDtypeStruct((cells, LANES), f32), jax.ShapeDtypeStruct((cells + orbs // 2, LANES), f32)),
        1,
        (meta, *shares),
        [pltpu.VMEM((orbs, LANES), f32)],
    )
    gathered, src = gather_parts(combined, "space", False, src)
    if n_squares > 1:
        squares.append(distances(1, src))

    levels_at_most = -(-screening.shape[0] // batch) + 1
    sent = call(
        functools.partial(orbital_kernel, planes, batch, unit, steps, slots, n_squares),
        "orbitals",
        jax.ShapeDtypeStruct((groups, share, kinds, LANES), f32),
        4,
        (meta, lists, levels, screening * (-log2e), pts, before, mine, after, *squares, *gathered),
        [
            pltpu.SMEM((screening.shape[0] + 2 * batch,), f32),
            pltpu.SMEM((screening.shape[0],), jnp.int32),
            pltpu.SMEM((share,), jnp.int32),
            pltpu.VMEM((planes, cells + orbs // 2, LANES), f32),
            pltpu.VMEM((window, LANES, 2 * orbs), bf16),
            pltpu.VMEM((window + planes, HALF, 2 * orbs), bf16),
            pltpu.VMEM((share // n_squares, blocks, LANES, 2 * orbs), bf16),
            pltpu.VMEM((share // n_squares, blocks, LANES, LANES), f32),
            pltpu.VMEM((share // n_squares, blocks, LANES, LANES), f32),
            pltpu.VMEM((share // n_squares, levels_at_most, batch * LANES, 2 * orbs), f32),
            basis,
        ],
        28,
    )
    parts = [sent[0]]
    for k in range(1, groups):
        parts.append(lax.ppermute(sent[k], "orb", [(i, i ^ k) for i in range(groups)]))
    updated = call(
        place_kernel,
        "place",
        jax.ShapeDtypeStruct((kinds, cells, LANES), f32),
        1,
        (meta, *parts),
        [pltpu.VMEM((cells, kinds, LANES), f32)],
    )
    return updated, hartree


def solution(mesh):
    in_specs = (
        P("orb", "space", None),
        P(None, "space", None),
        P("space", None),
        P("space", None),
        P(),
        P("orb"),
        P("space", None),
        P("space", None),
    )
    out_specs = (P("orb", "space", None), P("space", None))
    return jax.shard_map(body, mesh=mesh, in_specs=in_specs, out_specs=out_specs, check_vma=False)
```

```python
import functools
import math

import jax
import jax.numpy as jnp
import numpy as np
from jax import lax
from jax.experimental import pallas as pl
from jax.experimental.pallas import tpu as pltpu
from jax.sharding import PartitionSpec as P

NODES = 4
LANES = 128
PLANE = 16
ROWS = 8
HALF = NODES**3

cell_side = 0.25
soften = 6.25e-06
green_scale = -0.5 / math.pi
log2e = math.log2(math.e)
highest = lax.Precision.HIGHEST

node_set = np.cos((2.0 * np.arange(NODES) + 1.0) * (math.pi / (2.0 * NODES)))
roots = [[node_set[m] for m in range(NODES) if m != a] for a in range(NODES)]
scales = [1.0 / np.prod([node_set[a] - r for r in roots[a]]) for a in range(NODES)]


def put_basis(cst):
    row = lax.broadcasted_iota(jnp.int32, (ROWS, LANES), 0)
    for i, pick in enumerate((row // 4, 2 + row // 4, row % 4)):
        for k in range(NODES):
            values = [float(scales[a] if k == NODES - 1 else roots[a][k]) for a in range(NODES)]
            made = jnp.full((ROWS, LANES), values[0], jnp.float32)
            for a in range(1, NODES):
                made = jnp.where(pick == a, values[a], made)
            cst[NODES * i + k] = made


def node_offsets():
    lane = lax.broadcasted_iota(jnp.int32, (1, LANES), 1) % HALF
    out = []
    for pick in (lane // 16, lane // 4 % 4, lane % 4):
        made = jnp.full((1, LANES), 0.5 * (node_set[0] + 1.0), jnp.float32)
        for a in range(1, NODES):
            made = jnp.where(pick == a, float(0.5 * (node_set[a] + 1.0)), made)
        out.append(made)
    return out


def poly(u, r0, r1, r2, scale):
    return ((u - r0) * (u - r1)) * ((u - r2) * scale)


def weights(cst, x, y, z, lows, sides):
    ux, uy, uz = (
        jnp.broadcast_to(2.0 * (c - lo) / e - 1.0, (ROWS, LANES)) for c, lo, e in zip((x, y, z), lows, sides)
    )
    pz = poly(uz, cst[8], cst[9], cst[10], cst[11])
    pyz = [poly(uy, cst[4 * k], cst[4 * k + 1], cst[4 * k + 2], cst[4 * k + 3]) * pz for k in range(2)]
    parts = []
    for a in range(NODES):
        px = poly(ux, *(float(r) for r in roots[a]), float(scales[a]))
        parts += [px * pyz[0], px * pyz[1]]
    return jnp.concatenate(parts, axis=0)


def twice(w):
    return jnp.concatenate([w, w], axis=0)


def cell_low(cell):
    return [(cell % 4).astype(jnp.float32) * cell_side, (cell // 4 % 4).astype(jnp.float32) * cell_side]


def dot_nt(a, b):
    return lax.dot_general(a, b, (((1,), (1,)), ((), ())), precision=highest, preferred_element_type=jnp.float32)


def gather_parts(block, axis, pairs, later=None):
    count = lax.axis_size(axis)
    parts = [block[None]]
    while sum(p.shape[0] for p in parts) < count:
        held = parts[0] if len(parts) == 1 else jnp.concatenate(parts, axis=0)
        have = held.shape[0]
        steps = range(1, 4 if (have > 1 or pairs) and have * 4 <= count else 2)
        parts = [held] + [lax.ppermute(held, axis, [(i, i ^ (have * j)) for i in range(count)]) for j in steps]
        if later is not None and have == 1:
            parts[1], later = lax.optimization_barrier((parts[1], later))
    return parts, later


def gather_list(block, axis):
    parts, _ = gather_parts(block, axis, True)
    return [p[k] for p in parts for k in range(p.shape[0])]


def lay_out(parts, whole):
    at = 0
    for part in parts:
        for k in range(part.shape[0]):
            whole[at + k] = part[k]
        at += part.shape[0]


def target_cell(me, t, groups):
    return t * groups + lax.bitwise_xor(jnp.int32(t) if isinstance(t, int) else t, me)


def split(v):
    high = v.astype(jnp.bfloat16)
    return high, (v - high.astype(jnp.float32)).astype(jnp.bfloat16)


def dot_bf16(a, b):
    return lax.dot_general(a, b, (((1,), (1,)), ((), ())), preferred_element_type=jnp.float32)


def dot_split(v, w):
    vh, vl = split(v)
    wh, wl = split(w)
    rows = v.shape[0]
    both = dot_bf16(jnp.concatenate([vh, vl], axis=0), wh)
    return both[:rows] + both[rows:] + dot_bf16(vh, wl)


def lane_sums(v):
    high, low = split(v)
    ones = jnp.ones((ROWS, 2 * v.shape[1]), jnp.bfloat16)
    return dot_bf16(ones, jnp.concatenate([high, low], axis=1))[0:1, :]


def charge_kernel(meta, own, partial, *refs):
    z_low = meta[0].astype(jnp.float32) * cell_side
    fields, (out, density, cst) = refs[:-3], refs[-3:]
    put_basis(cst)
    total = partial[...]
    for phi in fields:
        for j in range(phi.shape[0]):
            v = phi[j]
            total = total + v * v
    density[...] = 2.0 * total
    acc = jnp.zeros((HALF, LANES), jnp.float32)
    for c in range(PLANE):
        point = own[:, c, :]
        charge = point[4:5] * density[c : c + 1, :]
        low = (cell_side * (c % 4), cell_side * (c // 4), z_low)
        acc = acc + weights(cst, point[0:1], point[1:2], point[2:3], (0.0, 0.0, z_low), (1.0, 1.0, cell_side)) * charge
        moments = lane_sums(weights(cst, point[0:1], point[1:2], point[2:3], low, (cell_side,) * 3) * charge)
        out[c, :5, :] = point[:5]
        out[c, 5:6, :] = charge
        out[c, 6:7, :] = jnp.concatenate([moments, moments], axis=1)
    moments = lane_sums(acc)
    for c in range(PLANE):
        out[c, 7:8, :] = jnp.concatenate([moments, moments], axis=1)


def live_planes(me, planes):
    below = jnp.maximum(me - 1, 0)
    return below, below + jnp.maximum(planes - 2 - me, 0)


def list_lengths(lists, cell, slots, me, planes):
    low, high = jnp.int32(0), jnp.int32(slots[0])
    for _ in range(slots[0].bit_length()):
        mid = (low + high) // 2
        live = (low < high) & (lists[cell, jnp.minimum(mid, slots[0] - 1)] >= 0)
        high = jnp.where(live | (low >= high), high, mid)
        low = jnp.where(live, mid + 1, low)
    around = 1 + (me > 0).astype(jnp.int32) + (me + 1 < planes).astype(jnp.int32)
    return low, around * PLANE - low


def list_blocks(me, cell, lists, slots, planes, put_near, put_far, put_none, multiple):
    window = 3 * PLANE
    base = (me - 1) * PLANE
    below, n_planes = live_planes(me, planes)
    near_slots, far_slots = slots
    n_near, n_far = list_lengths(lists, cell, slots, me, planes)
    n_items = n_far + n_planes
    n_pairs = (n_items + 1) // 2

    def near_step(j, c):
        put_near(j, lists[cell, j] - base)
        return c

    lax.fori_loop(0, n_near, near_step, 0)

    def item(j):
        j = jnp.minimum(j, n_items - 1)
        p = j - n_far
        level = jnp.where(p < below, p, p + (me + 2 - below))
        slot = lists[cell, near_slots + jnp.minimum(j, far_slots - 1)] - base
        return jnp.where(j < n_far, slot, window + level)

    def far_step(j, c):
        put_far(n_near + j, item(2 * j), item(2 * j + 1), 2 * j + 1 < n_items)
        return c

    lax.fori_loop(0, n_pairs, far_step, 0)
    for u in range(multiple - 1):
        put_none(n_near + n_pairs + u)
    return n_near + n_pairs


def in_low_half():
    return lax.broadcasted_iota(jnp.int32, (1, LANES), 1) < HALF


def put_targets(pts, cell, tgt):
    for d in range(3):
        tgt[d] = jnp.broadcast_to(pts[PLANE + cell, d : d + 1, :], (LANES, LANES)).T


def each_square(tgt, src, first, count, use):
    sources = [[src[first + u, d : d + 1, :] for d in range(3)] for u in range(count)]
    for r in range(LANES // ROWS):
        at = [tgt[d, r * ROWS : (r + 1) * ROWS, :] for d in range(3)]
        for u in range(count):
            dx, dy, dz = (a - b for a, b in zip(at, sources[u]))
            use(r, u, (dx * dx + dy * dy) + (dz * dz + soften))


def cell_fields(message, c, groups, kinds):
    rows = kinds * PLANE
    return jnp.concatenate([message[pl.ds(g * rows + c, kinds, stride=PLANE), :] for g in range(groups)], axis=0)


def hartree_kernel(groups, kinds, unroll, slots, meta, lists, marks, mine, *refs):
    parts, (out, pts, src, every, items, tgt, sums, cst) = refs[:-8], refs[-8:]
    lay_out(parts, every)
    planes = every.shape[0]
    cells = PLANE // groups
    me, group = meta[0], meta[1]
    window = 3 * PLANE
    put_basis(cst)
    for k in range(3):
        there = lax.bitwise_xor(me, jnp.clip(me - 1 + k, 0, planes - 1))
        for c in range(PLANE):
            pts[k * PLANE + c] = every[there, c]
    row = lax.broadcasted_iota(jnp.int32, (ROWS, 1), 0)

    offsets = node_offsets()

    def item_of(lows, sides, moments):
        made = jnp.where(row == 5, moments, 0.0)
        for d in range(3):
            made = jnp.where(row == d, lows[d] + offsets[d] * sides[d], made)
        return made

    def put_cell(c, carry):
        lows = (*cell_low(c), (me - 1 + c // PLANE).astype(jnp.float32) * cell_side)
        items[c] = item_of(lows, (cell_side,) * 3, pts[c, 6:7, :])
        return carry

    lax.fori_loop(0, window, put_cell, 0, unroll=8)

    def put_plane(g, c):
        lows = (0.0, 0.0, g.astype(jnp.float32) * cell_side)
        items[window + g] = item_of(lows, (1.0, 1.0, cell_side), every[lax.bitwise_xor(me, g), 0, 7:8, :])
        return c

    lax.fori_loop(0, planes, put_plane, 0)
    items[window + planes] = jnp.zeros((ROWS, LANES), jnp.float32)
    low_half = in_low_half()
    z_low = me.astype(jnp.float32) * cell_side
    out[0] = jnp.broadcast_to(marks[...], (ROWS, LANES))

    def per_cell(t, carry):
        cell = target_cell(group, t, groups)

        def put_near(j, slot):
            src[t, j] = pts[slot]

        def put_far(j, first, second, live):
            src[t, j] = jnp.where(low_half, items[first], items[jnp.where(live, second, window + planes)])

        def put_none(j):
            src[t, j] = jnp.zeros((ROWS, LANES), jnp.float32)

        n_blocks = list_blocks(me, cell, lists, slots, planes, put_near, put_far, put_none, unroll)
        put_targets(pts, cell, tgt)

        def step(i, accs):
            accs = list(accs)
            charges = [src[t, unroll * i + u, 5:6, :] for u in range(unroll)]

            def use(r, u, sq):
                accs[r] = accs[r] + lax.rsqrt(sq) * charges[u]

            each_square(tgt, src.at[t], unroll * i, unroll, use)
            return tuple(accs)

        zero = jnp.zeros((ROWS, LANES), jnp.float32)
        accs = lax.fori_loop(0, (n_blocks + unroll - 1) // unroll, step, (zero,) * (LANES // ROWS))
        sums[t] = jnp.concatenate(accs, axis=0)
        return carry

    lax.fori_loop(0, cells, per_cell, 0)
    ones = jnp.ones((ROWS, LANES), jnp.float32)
    found = dot_nt(ones, sums[...].reshape(cells * LANES, LANES))
    total = jnp.zeros((groups * kinds, LANES), jnp.float32)
    for t in range(cells):
        cell = target_cell(group, t, groups)
        potential = found[0:1, t * LANES : (t + 1) * LANES]
        out[0, t : t + 1, :] = potential
        point = pts[PLANE + cell]
        scaled = point[4:5] * (point[3:4] + potential)
        v = cell_fields(mine, cell, groups, kinds) * scaled
        w = weights(cst, point[0:1], point[1:2], point[2:3], (0.0, 0.0, z_low), (1.0, 1.0, cell_side))
        total = total + dot_split(v, twice(w))
    for k in range(groups):
        out[1 + lax.bitwise_xor(group, k), :kinds, :] = total[k * kinds : (k + 1) * kinds, :]


def pairs_kernel(first, groups, planes, unroll, slots, meta, lists, pts, src, out, tgt):
    group = meta[1]
    _, n_planes = live_planes(meta[0], planes)

    def per_cell(t, carry):
        cell = target_cell(group, first + t, groups)
        put_targets(pts, cell, tgt)
        n_near, n_far = list_lengths(lists, cell, slots, meta[0], planes)
        n_blocks = n_near + (n_far + n_planes + 1) // 2

        def measure(i, x):
            def use(r, u, sq):
                out[t, unroll * i + u, r * ROWS : (r + 1) * ROWS, :] = sq

            each_square(tgt, src.at[first + t], unroll * i, unroll, use)
            return x

        lax.fori_loop(0, (n_blocks + unroll - 1) // unroll, measure, 0)
        return carry

    lax.fori_loop(0, out.shape[0], per_cell, 0)


def combine_kernel(kinds, meta, *refs):
    shares, (hartree, out, total) = refs[:-3], refs[-3:]
    groups = len(shares)
    for k, share in enumerate(shares):
        for t in range(PLANE // groups):
            cell = target_cell(lax.bitwise_xor(meta[1], k), t, groups)
            out[pl.ds(cell, 1), :] = share[0, t : t + 1, :]
    hartree[...] = out[:PLANE, :]
    for g in range(groups):
        added = shares[0][1 + g, :kinds, :]
        for share in shares[1:]:
            added = added + share[1 + g, :kinds, :]
        total[g * kinds : (g + 1) * kinds, :] = added
    rows = groups * kinds // 2
    low_half = lax.broadcasted_iota(jnp.int32, (1, LANES), 1) < HALF
    out[PLANE:, :] = jnp.where(low_half, total[:rows, :], total[rows:, :])


def orbital_kernel(
    planes, batch, unit, steps, slots, n_squares, meta, lists, levels, rates_of,
    pts, before, mine, after, *refs,
):
    squares, refs = refs[:n_squares], refs[n_squares:]
    parts, (out, rate, slot_of, units, every, val, mom, srcv, dist, inv, acc, cst) = refs[:-12], refs[-12:]
    lay_out(parts, every)
    groups, cells, kinds, _ = out.shape
    orbs = groups * kinds
    n_rates = rates_of.shape[0]
    me, group = meta[0], meta[1]

    def clear(i, c):
        slot_of[i] = -1
        rate[i] = 0.0
        return c

    lax.fori_loop(0, n_rates, clear, 0)
    for q in range(2 * batch):
        rate[n_rates + q] = 0.0
    lane = lax.broadcasted_iota(jnp.int32, (1, LANES), 1) % orbs

    def rank(i, carry):
        found, lane_slot = carry
        level = levels[i]
        known = slot_of[level]
        slot = jnp.where(known < 0, found, known)
        slot_of[level] = slot
        rate[slot] = rates_of[level]
        return found + (known < 0).astype(jnp.int32), jnp.where(lane == i, slot, lane_slot)

    n_levels, lane_slot = lax.fori_loop(0, orbs, rank, (jnp.int32(0), jnp.zeros((1, LANES), jnp.int32)))
    left = lax.rem(n_levels, batch)
    short = (left > 0) & (left <= batch // 2)
    n_whole = n_levels // batch + ((left > 0) & jnp.logical_not(short)).astype(jnp.int32)
    n_batches = n_whole + short.astype(jnp.int32)
    first_half = lax.broadcasted_iota(jnp.int32, (1, 2 * orbs), 1) < orbs
    put_basis(cst)

    def flip(v):
        high = v.astype(jnp.bfloat16).astype(jnp.float32)
        square = jnp.concatenate([high, v - high, jnp.zeros((LANES - 2 * orbs, LANES), jnp.float32)], axis=0)
        return square.T[:, : 2 * orbs].astype(jnp.bfloat16)

    for k in range(3):
        message = (before, mine, after)[k]
        there = lax.bitwise_xor(me, jnp.clip(me - 1 + k, 0, planes - 1))

        def prepare(c, carry):
            at = k * PLANE + c
            point = pts[at]
            potential = point[3:4] + every[there, pl.ds(c, 1), :]
            v = cell_fields(message, c, groups, kinds) * (point[4:5] * potential)
            val[at] = flip(v)
            vh, vl = split(v)
            z_low = (me - 1 + k).astype(jnp.float32) * cell_side
            low = (*cell_low(c), z_low)
            wh, wl = split(weights(cst, point[0:1], point[1:2], point[2:3], low, (cell_side,) * 3))
            all_of = dot_bf16(jnp.concatenate([wh, wl], axis=0), jnp.concatenate([vh, vh, vl, vl], axis=0))
            m = all_of[:HALF] + all_of[HALF:]
            m = m[:, : 2 * orbs] + pltpu.roll(all_of[:HALF], 2 * orbs, 1)[:, : 2 * orbs]
            high = m.astype(jnp.bfloat16).astype(jnp.float32)
            mom[at] = jnp.where(first_half, high, m - high).astype(jnp.bfloat16)
            return carry

        lax.fori_loop(0, PLANE, prepare, 0, unroll=8)

    def put_plane(g, c):
        there = lax.bitwise_xor(me, g)
        rows = []
        for k in range(groups):
            row = lax.bitwise_xor(group, k) * kinds
            v = every[there, pl.ds(PLANE + lax.rem(row, orbs // 2), kinds), :]
            rows.append(jnp.where(row < orbs // 2, v, pltpu.roll(v, HALF, 1)))
        mom[3 * PLANE + g] = flip(jnp.concatenate(rows, axis=0))[:HALF]
        return c

    lax.fori_loop(0, planes, put_plane, 0)

    def products(g, b, first, width):
        rates = [rate[b * batch + q] for q in range(width)]
        rows = []
        for q in range(width):
            tiles = [
                (jnp.exp2(dist[g, first + h] * rates[q]) * inv[g, first + h]).astype(jnp.bfloat16) for h in range(unit)
            ]
            rows.append(jnp.concatenate(tiles, axis=1))
        v = jnp.concatenate([srcv[g, first + h] for h in range(unit)], axis=0)
        return jnp.dot(jnp.concatenate(rows, axis=0), v, preferred_element_type=jnp.float32)

    share = cells // n_squares

    def per_group(p, carry):
        def list_cell(g, x):
            def put_near(j, slot):
                srcv[g, j] = val[slot]

            def put_far(j, first, second, live):
                srcv[g, j, :HALF, :] = mom[first]
                srcv[g, j, HALF:, :] = jnp.where(live, mom[second], jnp.zeros_like(mom[second]))

            def put_none(j):
                srcv[g, j] = jnp.zeros(srcv.shape[2:], srcv.dtype)

            cell = target_cell(group, p * share + g, groups)
            n_blocks = list_blocks(me, cell, lists, slots, planes, put_near, put_far, put_none, unit)
            units[g] = (n_blocks + unit - 1) // unit

            def clear_acc(b, y):
                acc[g, b] = jnp.zeros(acc.shape[2:], jnp.float32)
                return y

            lax.fori_loop(0, n_batches, clear_acc, 0)
            return x

        lax.fori_loop(0, share, list_cell, 0)

        for k in range(n_squares):

            @pl.when(p == k)
            def _():
                for g in range(share):

                    def measure(i, x):
                        for u in range(unit):
                            sq = squares[k][g, unit * i + u]
                            one_over = lax.rsqrt(sq)
                            inv[g, unit * i + u] = one_over
                            dist[g, unit * i + u] = sq * one_over
                        return x

                    lax.fori_loop(0, units[g], measure, 0)

        nowhere = acc.shape[1] - 1

        def step(i, at):
            g, b, u = at
            for _ in range(steps):
                acc[g, b] = acc[g, b] + products(g, b, unit * u, batch)
                wrap = u + 1 >= units[g]
                later = jnp.where(wrap, b + 1, b)
                over, last = later >= n_whole, g + 1 >= share
                u = jnp.where(wrap, 0, u + 1)
                b = jnp.where(over, jnp.where(last, nowhere, 0), later)
                g = jnp.where(over & jnp.logical_not(last), g + 1, g)
            return g, b, u

        def short_step(i, at):
            g, u, b = at
            for _ in range(steps):
                at_rows = (g, b, slice(0, batch // 2 * LANES))
                acc[at_rows] = acc[at_rows] + products(g, b, unit * u, batch // 2)
                wrap, last = u + 1 >= units[g], g + 1 >= share
                u = jnp.where(wrap, 0, u + 1)
                b = jnp.where(wrap & last, nowhere, b)
                g = jnp.where(wrap & jnp.logical_not(last), g + 1, g)
            return g, u, b

        work = sum(units[g] for g in range(share))
        zero = jnp.int32(0)
        lax.fori_loop(0, (work * n_whole + steps - 1) // steps, step, (zero, zero, zero))
        rest = jnp.where(short, (work + steps - 1) // steps, 0)
        lax.fori_loop(0, rest, short_step, (zero, zero, n_whole))

        def finish(g, x):
            def choose(b, add):
                for q in range(batch):
                    mine = lane_slot[:, : 2 * orbs] == b * batch + q
                    add = add + jnp.where(mine, acc[g, b, q * LANES : (q + 1) * LANES, :], 0.0)
                return add

            total = lax.fori_loop(0, n_batches, choose, jnp.zeros((LANES, 2 * orbs), jnp.float32))
            flipped = jnp.concatenate([total, jnp.zeros((LANES, LANES - 2 * orbs), jnp.float32)], axis=1).T
            rows = (flipped[:orbs] + flipped[orbs : 2 * orbs]) * green_scale
            for k in range(groups):
                out[k, p * share + g] = rows[k * kinds : (k + 1) * kinds]
            return x

        lax.fori_loop(0, share, finish, 0)
        return carry

    lax.fori_loop(0, n_squares, per_group, 0)


def place_kernel(meta, *refs):
    parts, out, ordered = refs[:-2], refs[-2], refs[-1]
    for k, part in enumerate(parts):
        for t in range(part.shape[0]):
            ordered[target_cell(lax.bitwise_xor(meta[1], k), t, len(parts))] = part[t]
    for c in range(PLANE):
        out[:, c, :] = ordered[c]


def smem():
    return pl.BlockSpec(memory_space=pltpu.SMEM)


def vmem():
    return pl.BlockSpec(memory_space=pltpu.VMEM)


def call(kernel, name, out_shape, smems, args, scratch=(), mib=8):
    return pl.pallas_call(
        kernel,
        out_shape=out_shape,
        in_specs=[smem()] * smems + [vmem()] * (len(args) - smems),
        out_specs=jax.tree.map(lambda _: vmem(), out_shape),
        scratch_shapes=scratch,
        compiler_params=pltpu.CompilerParams(vmem_limit_bytes=mib * 1024 * 1024),
        name=name,
    )(*args)


def body(orbitals, points, quad_weight, external, screening, level_index, near_cells, far_cells):
    kinds, cells, point_count = orbitals.shape
    planes, groups = lax.axis_size("space"), lax.axis_size("orb")
    orbs = kinds * groups
    window = 3 * PLANE
    share = cells // groups
    me, group = lax.axis_index("space"), lax.axis_index("orb")
    meta = jnp.stack([me, group]).astype(jnp.int32)
    f32, bf16 = jnp.float32, jnp.bfloat16

    fields = gather_list(orbitals, "orb")
    weight = quad_weight * (cell_side**3 / point_count)
    own = jnp.concatenate([points, external[None], weight[None], jnp.zeros((3, cells, LANES), f32)], axis=0)
    marks = jnp.pad(level_index.astype(f32), (0, LANES - kinds))[None]
    ends = planes - 1
    up = [(i, i + 1) for i in range(ends)]
    down = [(i + 1, i) for i in range(ends)]
    slots = (near_cells.shape[1], far_cells.shape[1])
    lists = jnp.concatenate([near_cells, far_cells], axis=1)
    partial = jnp.sum(orbitals * orbitals, axis=0)
    basis = pltpu.VMEM((3 * NODES, ROWS, LANES), f32)

    charges = call(
        charge_kernel,
        "charge",
        jax.ShapeDtypeStruct((cells, ROWS, LANES), f32),
        1,
        (meta, own, partial, *fields[1:]),
        [pltpu.VMEM((cells, LANES), f32), basis],
    )
    mine = jnp.concatenate([f.reshape(kinds * cells, LANES) for f in fields], axis=0)
    charges, mine = gather_parts(charges, "space", False, mine)
    before = lax.ppermute(mine, "space", up)

    batch, unit, steps = 4, 4, 18
    most = near_cells.shape[1]
    blocks = most + (window - most + planes - 2) // 2 + unit - 1
    blocks = -(-blocks // unit) * unit
    shares, pts, src = call(
        functools.partial(hartree_kernel, groups, kinds, unit, slots),
        "hartree",
        (
            jax.ShapeDtypeStruct((1 + groups, ROWS, LANES), f32),
            jax.ShapeDtypeStruct((window, ROWS, LANES), f32),
            jax.ShapeDtypeStruct((share, blocks, ROWS, LANES), f32),
        ),
        2,
        (meta, lists, marks, mine, *charges),
        [
            pltpu.VMEM((planes, cells, ROWS, LANES), f32),
            pltpu.VMEM((window + planes + 1, ROWS, LANES), f32),
            pltpu.VMEM((3, LANES, LANES), f32),
            pltpu.VMEM((share, LANES, LANES), f32),
            basis,
        ],
        12,
    )
    mine, shares = lax.optimization_barrier((mine, shares))
    after = lax.ppermute(mine, "space", down)
    n_squares = 2 if share % 2 == 0 else 1

    def distances(k, src):
        return call(
            functools.partial(pairs_kernel, k * share // n_squares, groups, planes, unit, slots),
            "pairs",
            jax.ShapeDtypeStruct((share // n_squares, blocks, LANES, LANES), f32),
            2,
            (meta, lists, pts, src),
            [pltpu.VMEM((3, LANES, LANES), f32)],
            4,
        )

    squares = [distances(0, src)]
    shares = gather_list(shares, "orb")
    levels = jnp.concatenate([share[0, ROWS - 1, :kinds] for share in shares]).astype(jnp.int32)
    hartree, combined = call(
        functools.partial(combine_kernel, kinds),
        "combine",
        (jax.ShapeDtypeStruct((cells, LANES), f32), jax.ShapeDtypeStruct((cells + orbs // 2, LANES), f32)),
        1,
        (meta, *shares),
        [pltpu.VMEM((orbs, LANES), f32)],
    )
    gathered, src = gather_parts(combined, "space", False, src)
    if n_squares > 1:
        squares.append(distances(1, src))

    levels_at_most = -(-screening.shape[0] // batch) + 1
    sent = call(
        functools.partial(orbital_kernel, planes, batch, unit, steps, slots, n_squares),
        "orbitals",
        jax.ShapeDtypeStruct((groups, share, kinds, LANES), f32),
        4,
        (meta, lists, levels, screening * (-log2e), pts, before, mine, after, *squares, *gathered),
        [
            pltpu.SMEM((screening.shape[0] + 2 * batch,), f32),
            pltpu.SMEM((screening.shape[0],), jnp.int32),
            pltpu.SMEM((share,), jnp.int32),
            pltpu.VMEM((planes, cells + orbs // 2, LANES), f32),
            pltpu.VMEM((window, LANES, 2 * orbs), bf16),
            pltpu.VMEM((window + planes, HALF, 2 * orbs), bf16),
            pltpu.VMEM((share // n_squares, blocks, LANES, 2 * orbs), bf16),
            pltpu.VMEM((share // n_squares, blocks, LANES, LANES), f32),
            pltpu.VMEM((share // n_squares, blocks, LANES, LANES), f32),
            pltpu.VMEM((share // n_squares, levels_at_most, batch * LANES, 2 * orbs), f32),
            basis,
        ],
        28,
    )
    parts = [sent[0]]
    for k in range(1, groups):
        parts.append(lax.ppermute(sent[k], "orb", [(i, i ^ k) for i in range(groups)]))
    updated = call(
        place_kernel,
        "place",
        jax.ShapeDtypeStruct((kinds, cells, LANES), f32),
        1,
        (meta, *parts),
        [pltpu.VMEM((cells, kinds, LANES), f32)],
    )
    return updated, hartree


def solution(mesh):
    in_specs = (
        P("orb", "space", None),
        P(None, "space", None),
        P("space", None),
        P("space", None),
        P(),
        P("orb"),
        P("space", None),
        P("space", None),
    )
    out_specs = (P("orb", "space", None), P("space", None))
    return jax.shard_map(body, mesh=mesh, in_specs=in_specs, out_specs=out_specs, check_vma=False)
```

```python
import functools
import math

import jax
import jax.numpy as jnp
import numpy as np
from jax import lax
from jax.experimental import pallas as pl
from jax.experimental.pallas import tpu as pltpu
from jax.sharding import PartitionSpec as P

NODES = 4
LANES = 128
PLANE = 16
ROWS = 8
HALF = NODES**3

cell_side = 0.25
soften = 6.25e-06
green_scale = -0.5 / math.pi
log2e = math.log2(math.e)
highest = lax.Precision.HIGHEST

node_set = np.cos((2.0 * np.arange(NODES) + 1.0) * (math.pi / (2.0 * NODES)))
roots = [[node_set[m] for m in range(NODES) if m != a] for a in range(NODES)]
scales = [1.0 / np.prod([node_set[a] - r for r in roots[a]]) for a in range(NODES)]


def put_basis(cst):
    row = lax.broadcasted_iota(jnp.int32, (ROWS, LANES), 0)
    for i, pick in enumerate((row // 4, 2 + row // 4, row % 4)):
        for k in range(NODES):
            values = [float(scales[a] if k == NODES - 1 else roots[a][k]) for a in range(NODES)]
            made = jnp.full((ROWS, LANES), values[0], jnp.float32)
            for a in range(1, NODES):
                made = jnp.where(pick == a, values[a], made)
            cst[NODES * i + k] = made


def node_offsets():
    lane = lax.broadcasted_iota(jnp.int32, (1, LANES), 1) % HALF
    out = []
    for pick in (lane // 16, lane // 4 % 4, lane % 4):
        made = jnp.full((1, LANES), 0.5 * (node_set[0] + 1.0), jnp.float32)
        for a in range(1, NODES):
            made = jnp.where(pick == a, float(0.5 * (node_set[a] + 1.0)), made)
        out.append(made)
    return out


def poly(u, r0, r1, r2, scale):
    return ((u - r0) * (u - r1)) * ((u - r2) * scale)


def weights(cst, x, y, z, lows, sides):
    ux, uy, uz = (
        jnp.broadcast_to(2.0 * (c - lo) / e - 1.0, (ROWS, LANES)) for c, lo, e in zip((x, y, z), lows, sides)
    )
    pz = poly(uz, cst[8], cst[9], cst[10], cst[11])
    pyz = [poly(uy, cst[4 * k], cst[4 * k + 1], cst[4 * k + 2], cst[4 * k + 3]) * pz for k in range(2)]
    parts = []
    for a in range(NODES):
        px = poly(ux, *(float(r) for r in roots[a]), float(scales[a]))
        parts += [px * pyz[0], px * pyz[1]]
    return jnp.concatenate(parts, axis=0)


def twice(w):
    return jnp.concatenate([w, w], axis=0)


def cell_low(cell):
    return [(cell % 4).astype(jnp.float32) * cell_side, (cell // 4 % 4).astype(jnp.float32) * cell_side]


def dot_nt(a, b):
    return lax.dot_general(a, b, (((1,), (1,)), ((), ())), precision=highest, preferred_element_type=jnp.float32)


def gather_parts(block, axis, pairs, later=None):
    count = lax.axis_size(axis)
    parts = [block[None]]
    while sum(p.shape[0] for p in parts) < count:
        held = parts[0] if len(parts) == 1 else jnp.concatenate(parts, axis=0)
        have = held.shape[0]
        steps = range(1, 4 if (have > 1 or pairs) and have * 4 <= count else 2)
        parts = [held] + [lax.ppermute(held, axis, [(i, i ^ (have * j)) for i in range(count)]) for j in steps]
        if later is not None and have == 1:
            parts[1], later = lax.optimization_barrier((parts[1], later))
    return parts, later


def gather_list(block, axis):
    parts, _ = gather_parts(block, axis, True)
    return [p[k] for p in parts for k in range(p.shape[0])]


def lay_out(parts, whole):
    at = 0
    for part in parts:
        for k in range(part.shape[0]):
            whole[at + k] = part[k]
        at += part.shape[0]


def target_cell(me, t, groups):
    return t * groups + lax.bitwise_xor(jnp.int32(t) if isinstance(t, int) else t, me)


def split(v):
    high = v.astype(jnp.bfloat16)
    return high, (v - high.astype(jnp.float32)).astype(jnp.bfloat16)


def dot_bf16(a, b):
    return lax.dot_general(a, b, (((1,), (1,)), ((), ())), preferred_element_type=jnp.float32)


def dot_split(v, w):
    vh, vl = split(v)
    wh, wl = split(w)
    rows = v.shape[0]
    both = dot_bf16(jnp.concatenate([vh, vl], axis=0), wh)
    return both[:rows] + both[rows:] + dot_bf16(vh, wl)


def lane_sums(v):
    high, low = split(v)
    ones = jnp.ones((ROWS, 2 * v.shape[1]), jnp.bfloat16)
    return dot_bf16(ones, jnp.concatenate([high, low], axis=1))[0:1, :]


def charge_kernel(meta, own, partial, *refs):
    z_low = meta[0].astype(jnp.float32) * cell_side
    fields, (out, density, cst) = refs[:-3], refs[-3:]
    put_basis(cst)
    total = partial[...]
    for phi in fields:
        for j in range(phi.shape[0]):
            v = phi[j]
            total = total + v * v
    density[...] = 2.0 * total
    acc = jnp.zeros((HALF, LANES), jnp.float32)
    for c in range(PLANE):
        point = own[:, c, :]
        charge = point[4:5] * density[c : c + 1, :]
        low = (cell_side * (c % 4), cell_side * (c // 4), z_low)
        acc = acc + weights(cst, point[0:1], point[1:2], point[2:3], (0.0, 0.0, z_low), (1.0, 1.0, cell_side)) * charge
        moments = lane_sums(weights(cst, point[0:1], point[1:2], point[2:3], low, (cell_side,) * 3) * charge)
        out[c, :5, :] = point[:5]
        out[c, 5:6, :] = charge
        out[c, 6:7, :] = jnp.concatenate([moments, moments], axis=1)
    moments = lane_sums(acc)
    for c in range(PLANE):
        out[c, 7:8, :] = jnp.concatenate([moments, moments], axis=1)


def live_planes(me, planes):
    below = jnp.maximum(me - 1, 0)
    return below, below + jnp.maximum(planes - 2 - me, 0)


def list_lengths(lists, cell, slots, me, planes):
    low, high = jnp.int32(0), jnp.int32(slots[0])
    for _ in range(slots[0].bit_length()):
        mid = (low + high) // 2
        live = (low < high) & (lists[cell, jnp.minimum(mid, slots[0] - 1)] >= 0)
        high = jnp.where(live | (low >= high), high, mid)
        low = jnp.where(live, mid + 1, low)
    around = 1 + (me > 0).astype(jnp.int32) + (me + 1 < planes).astype(jnp.int32)
    return low, around * PLANE - low


def list_blocks(me, cell, lists, slots, planes, put_near, put_far, put_none, multiple):
    window = 3 * PLANE
    base = (me - 1) * PLANE
    below, n_planes = live_planes(me, planes)
    near_slots, far_slots = slots
    n_near, n_far = list_lengths(lists, cell, slots, me, planes)
    n_items = n_far + n_planes
    n_pairs = (n_items + 1) // 2

    def near_step(i, c):
        for j in (2 * i, 2 * i + 1):
            put_near(j, jnp.clip(lists[cell, j] - base, 0, window - 1))
        return c

    lax.fori_loop(0, (n_near + 1) // 2, near_step, 0)

    def item(j):
        j = jnp.minimum(j, n_items - 1)
        p = j - n_far
        level = jnp.where(p < below, p, p + (me + 2 - below))
        slot = lists[cell, near_slots + jnp.minimum(j, far_slots - 1)] - base
        return jnp.where(j < n_far, slot, window + level)

    def far_step(i, c):
        for j in (2 * i, 2 * i + 1):
            put_far(n_near + j, item(2 * j), item(2 * j + 1), 2 * j + 1 < n_items)
        return c

    lax.fori_loop(0, (n_pairs + 1) // 2, far_step, 0)
    for u in range(multiple - 1):
        put_none(n_near + n_pairs + u)
    return n_near + n_pairs


def in_low_half():
    return lax.broadcasted_iota(jnp.int32, (1, LANES), 1) < HALF


def put_targets(pts, cell, tgt):
    for d in range(3):
        tgt[d] = jnp.broadcast_to(pts[PLANE + cell, d : d + 1, :], (LANES, LANES)).T


def each_square(tgt, src, first, count, use):
    sources = [[src[first + u, d : d + 1, :] for d in range(3)] for u in range(count)]
    for r in range(LANES // ROWS):
        at = [tgt[d, r * ROWS : (r + 1) * ROWS, :] for d in range(3)]
        for u in range(count):
            dx, dy, dz = (a - b for a, b in zip(at, sources[u]))
            use(r, u, (dx * dx + dy * dy) + (dz * dz + soften))


def cell_fields(message, c, groups, kinds):
    rows = kinds * PLANE
    return jnp.concatenate([message[pl.ds(g * rows + c, kinds, stride=PLANE), :] for g in range(groups)], axis=0)


def hartree_kernel(groups, kinds, unroll, slots, meta, lists, marks, mine, *refs):
    parts, (out, pts, src, every, items, tgt, sums, cst) = refs[:-8], refs[-8:]
    lay_out(parts, every)
    planes = every.shape[0]
    cells = PLANE // groups
    me, group = meta[0], meta[1]
    window = 3 * PLANE
    put_basis(cst)
    for k in range(3):
        there = lax.bitwise_xor(me, jnp.clip(me - 1 + k, 0, planes - 1))
        for c in range(PLANE):
            pts[k * PLANE + c] = every[there, c]
    row = lax.broadcasted_iota(jnp.int32, (ROWS, 1), 0)

    offsets = node_offsets()

    def item_of(lows, sides, moments):
        made = jnp.where(row == 5, moments, 0.0)
        for d in range(3):
            made = jnp.where(row == d, lows[d] + offsets[d] * sides[d], made)
        return made

    def put_cell(c, carry):
        lows = (*cell_low(c), (me - 1 + c // PLANE).astype(jnp.float32) * cell_side)
        items[c] = item_of(lows, (cell_side,) * 3, pts[c, 6:7, :])
        return carry

    lax.fori_loop(0, window, put_cell, 0, unroll=8)

    def put_plane(g, c):
        lows = (0.0, 0.0, g.astype(jnp.float32) * cell_side)
        items[window + g] = item_of(lows, (1.0, 1.0, cell_side), every[lax.bitwise_xor(me, g), 0, 7:8, :])
        return c

    lax.fori_loop(0, planes, put_plane, 0)
    items[window + planes] = jnp.zeros((ROWS, LANES), jnp.float32)
    low_half = in_low_half()
    z_low = me.astype(jnp.float32) * cell_side
    out[0] = jnp.broadcast_to(marks[...], (ROWS, LANES))

    def per_cell(t, carry):
        cell = target_cell(group, t, groups)

        def put_near(j, slot):
            src[t, j] = pts[slot]

        def put_far(j, first, second, live):
            src[t, j] = jnp.where(low_half, items[first], items[jnp.where(live, second, window + planes)])

        def put_none(j):
            src[t, j] = jnp.zeros((ROWS, LANES), jnp.float32)

        n_blocks = list_blocks(me, cell, lists, slots, planes, put_near, put_far, put_none, unroll)
        put_targets(pts, cell, tgt)

        def step(i, accs):
            accs = list(accs)
            charges = [src[t, unroll * i + u, 5:6, :] for u in range(unroll)]

            def use(r, u, sq):
                accs[r] = accs[r] + lax.rsqrt(sq) * charges[u]

            each_square(tgt, src.at[t], unroll * i, unroll, use)
            return tuple(accs)

        zero = jnp.zeros((ROWS, LANES), jnp.float32)
        accs = lax.fori_loop(0, (n_blocks + unroll - 1) // unroll, step, (zero,) * (LANES // ROWS))
        sums[t] = jnp.concatenate(accs, axis=0)
        return carry

    lax.fori_loop(0, cells, per_cell, 0)
    ones = jnp.ones((ROWS, LANES), jnp.float32)
    found = dot_nt(ones, sums[...].reshape(cells * LANES, LANES))
    total = jnp.zeros((groups * kinds, LANES), jnp.float32)
    for t in range(cells):
        cell = target_cell(group, t, groups)
        potential = found[0:1, t * LANES : (t + 1) * LANES]
        out[0, t : t + 1, :] = potential
        point = pts[PLANE + cell]
        scaled = point[4:5] * (point[3:4] + potential)
        v = cell_fields(mine, cell, groups, kinds) * scaled
        w = weights(cst, point[0:1], point[1:2], point[2:3], (0.0, 0.0, z_low), (1.0, 1.0, cell_side))
        total = total + dot_split(v, twice(w))
    for k in range(groups):
        out[1 + lax.bitwise_xor(group, k), :kinds, :] = total[k * kinds : (k + 1) * kinds, :]


def pairs_kernel(first, groups, planes, unroll, slots, meta, lists, pts, src, out, tgt):
    group = meta[1]
    _, n_planes = live_planes(meta[0], planes)

    def per_cell(t, carry):
        cell = target_cell(group, first + t, groups)
        put_targets(pts, cell, tgt)
        n_near, n_far = list_lengths(lists, cell, slots, meta[0], planes)
        n_blocks = n_near + (n_far + n_planes + 1) // 2

        def measure(i, x):
            def use(r, u, sq):
                out[t, unroll * i + u, r * ROWS : (r + 1) * ROWS, :] = sq

            each_square(tgt, src.at[first + t], unroll * i, unroll, use)
            return x

        lax.fori_loop(0, (n_blocks + unroll - 1) // unroll, measure, 0)
        return carry

    lax.fori_loop(0, out.shape[0], per_cell, 0)


def combine_kernel(kinds, meta, *refs):
    shares, (hartree, out, total) = refs[:-3], refs[-3:]
    groups = len(shares)
    for k, share in enumerate(shares):
        for t in range(PLANE // groups):
            cell = target_cell(lax.bitwise_xor(meta[1], k), t, groups)
            out[pl.ds(cell, 1), :] = share[0, t : t + 1, :]
    hartree[...] = out[:PLANE, :]
    for g in range(groups):
        added = shares[0][1 + g, :kinds, :]
        for share in shares[1:]:
            added = added + share[1 + g, :kinds, :]
        total[g * kinds : (g + 1) * kinds, :] = added
    rows = groups * kinds // 2
    low_half = lax.broadcasted_iota(jnp.int32, (1, LANES), 1) < HALF
    out[PLANE:, :] = jnp.where(low_half, total[:rows, :], total[rows:, :])


def orbital_kernel(
    planes, batch, unit, steps, slots, n_squares, meta, lists, levels, rates_of,
    pts, before, mine, after, *refs,
):
    squares, refs = refs[:n_squares], refs[n_squares:]
    parts, (out, rate, slot_of, units, every, val, mom, srcv, dist, inv, acc, cst) = refs[:-12], refs[-12:]
    lay_out(parts, every)
    groups, cells, kinds, _ = out.shape
    orbs = groups * kinds
    n_rates = rates_of.shape[0]
    me, group = meta[0], meta[1]

    def clear(i, c):
        slot_of[i] = -1
        rate[i] = 0.0
        return c

    lax.fori_loop(0, n_rates, clear, 0)
    for q in range(2 * batch):
        rate[n_rates + q] = 0.0
    lane = lax.broadcasted_iota(jnp.int32, (1, LANES), 1) % orbs

    def rank(i, carry):
        found, lane_slot = carry
        level = levels[i]
        known = slot_of[level]
        slot = jnp.where(known < 0, found, known)
        slot_of[level] = slot
        rate[slot] = rates_of[level]
        return found + (known < 0).astype(jnp.int32), jnp.where(lane == i, slot, lane_slot)

    n_levels, lane_slot = lax.fori_loop(0, orbs, rank, (jnp.int32(0), jnp.zeros((1, LANES), jnp.int32)))
    left = lax.rem(n_levels, batch)
    short = (left > 0) & (left <= batch // 2)
    n_whole = n_levels // batch + ((left > 0) & jnp.logical_not(short)).astype(jnp.int32)
    n_batches = n_whole + short.astype(jnp.int32)
    first_half = lax.broadcasted_iota(jnp.int32, (1, 2 * orbs), 1) < orbs
    put_basis(cst)

    def flip(v):
        high = v.astype(jnp.bfloat16).astype(jnp.float32)
        square = jnp.concatenate([high, v - high, jnp.zeros((LANES - 2 * orbs, LANES), jnp.float32)], axis=0)
        return square.T[:, : 2 * orbs].astype(jnp.bfloat16)

    for k in range(3):
        message = (before, mine, after)[k]
        there = lax.bitwise_xor(me, jnp.clip(me - 1 + k, 0, planes - 1))

        def prepare(c, carry):
            at = k * PLANE + c
            point = pts[at]
            potential = point[3:4] + every[there, pl.ds(c, 1), :]
            v = cell_fields(message, c, groups, kinds) * (point[4:5] * potential)
            val[at] = flip(v)
            vh, vl = split(v)
            z_low = (me - 1 + k).astype(jnp.float32) * cell_side
            low = (*cell_low(c), z_low)
            wh, wl = split(weights(cst, point[0:1], point[1:2], point[2:3], low, (cell_side,) * 3))
            all_of = dot_bf16(jnp.concatenate([wh, wl], axis=0), jnp.concatenate([vh, vh, vl, vl], axis=0))
            m = all_of[:HALF] + all_of[HALF:]
            m = m[:, : 2 * orbs] + pltpu.roll(all_of[:HALF], 2 * orbs, 1)[:, : 2 * orbs]
            high = m.astype(jnp.bfloat16).astype(jnp.float32)
            mom[at] = jnp.where(first_half, high, m - high).astype(jnp.bfloat16)
            return carry

        lax.fori_loop(0, PLANE, prepare, 0, unroll=16)

    def put_plane(g, c):
        there = lax.bitwise_xor(me, g)
        rows = []
        for k in range(groups):
            row = lax.bitwise_xor(group, k) * kinds
            v = every[there, pl.ds(PLANE + lax.rem(row, orbs // 2), kinds), :]
            rows.append(jnp.where(row < orbs // 2, v, pltpu.roll(v, HALF, 1)))
        mom[3 * PLANE + g] = flip(jnp.concatenate(rows, axis=0))[:HALF]
        return c

    lax.fori_loop(0, planes, put_plane, 0)

    def products(g, b, first, width):
        rates = [rate[b * batch + q] for q in range(width)]
        rows = []
        for q in range(width):
            tiles = [
                (jnp.exp2(dist[g, first + h] * rates[q]) * inv[g, first + h]).astype(jnp.bfloat16) for h in range(unit)
            ]
            rows.append(jnp.concatenate(tiles, axis=1))
        v = jnp.concatenate([srcv[g, first + h] for h in range(unit)], axis=0)
        return jnp.dot(jnp.concatenate(rows, axis=0), v, preferred_element_type=jnp.float32)

    share = cells // n_squares

    def per_group(p, carry):
        def list_cell(g, x):
            def put_near(j, slot):
                srcv[g, j] = val[slot]

            def put_far(j, first, second, live):
                srcv[g, j, :HALF, :] = mom[first]
                srcv[g, j, HALF:, :] = jnp.where(live, mom[second], jnp.zeros_like(mom[second]))

            def put_none(j):
                srcv[g, j] = jnp.zeros(srcv.shape[2:], srcv.dtype)

            cell = target_cell(group, p * share + g, groups)
            n_blocks = list_blocks(me, cell, lists, slots, planes, put_near, put_far, put_none, unit)
            units[g] = (n_blocks + unit - 1) // unit

            def clear_acc(b, y):
                acc[g, b] = jnp.zeros(acc.shape[2:], jnp.float32)
                return y

            lax.fori_loop(0, n_batches, clear_acc, 0)
            return x

        lax.fori_loop(0, share, list_cell, 0)

        for k in range(n_squares):

            @pl.when(p == k)
            def _():
                for g in range(share):

                    def measure(i, x):
                        for u in range(unit):
                            sq = squares[k][g, unit * i + u]
                            one_over = lax.rsqrt(sq)
                            inv[g, unit * i + u] = one_over
                            dist[g, unit * i + u] = sq * one_over
                        return x

                    lax.fori_loop(0, units[g], measure, 0)

        nowhere = acc.shape[1] - 1

        def step(i, at):
            g, b, u = at
            for _ in range(steps):
                acc[g, b] = acc[g, b] + products(g, b, unit * u, batch)
                wrap = u + 1 >= units[g]
                later = jnp.where(wrap, b + 1, b)
                over, last = later >= n_whole, g + 1 >= share
                u = jnp.where(wrap, 0, u + 1)
                b = jnp.where(over, jnp.where(last, nowhere, 0), later)
                g = jnp.where(over & jnp.logical_not(last), g + 1, g)
            return g, b, u

        def short_step(i, at):
            g, u, b = at
            for _ in range(steps):
                at_rows = (g, b, slice(0, batch // 2 * LANES))
                acc[at_rows] = acc[at_rows] + products(g, b, unit * u, batch // 2)
                wrap, last = u + 1 >= units[g], g + 1 >= share
                u = jnp.where(wrap, 0, u + 1)
                b = jnp.where(wrap & last, nowhere, b)
                g = jnp.where(wrap & jnp.logical_not(last), g + 1, g)
            return g, u, b

        work = sum(units[g] for g in range(share))
        zero = jnp.int32(0)
        lax.fori_loop(0, (work * n_whole + steps - 1) // steps, step, (zero, zero, zero))
        rest = jnp.where(short, (work + steps - 1) // steps, 0)
        lax.fori_loop(0, rest, short_step, (zero, zero, n_whole))

        def finish(g, x):
            def choose(b, add):
                for q in range(batch):
                    mine = lane_slot[:, : 2 * orbs] == b * batch + q
                    add = add + jnp.where(mine, acc[g, b, q * LANES : (q + 1) * LANES, :], 0.0)
                return add

            total = lax.fori_loop(0, n_batches, choose, jnp.zeros((LANES, 2 * orbs), jnp.float32))
            flipped = jnp.concatenate([total, jnp.zeros((LANES, LANES - 2 * orbs), jnp.float32)], axis=1).T
            rows = (flipped[:orbs] + flipped[orbs : 2 * orbs]) * green_scale
            for k in range(groups):
                out[k, p * share + g] = rows[k * kinds : (k + 1) * kinds]
            return x

        lax.fori_loop(0, share, finish, 0)
        return carry

    lax.fori_loop(0, n_squares, per_group, 0)


def place_kernel(meta, *refs):
    parts, out, ordered = refs[:-2], refs[-2], refs[-1]
    for k, part in enumerate(parts):
        for t in range(part.shape[0]):
            ordered[target_cell(lax.bitwise_xor(meta[1], k), t, len(parts))] = part[t]
    for c in range(PLANE):
        out[:, c, :] = ordered[c]


def smem():
    return pl.BlockSpec(memory_space=pltpu.SMEM)


def vmem():
    return pl.BlockSpec(memory_space=pltpu.VMEM)


def call(kernel, name, out_shape, smems, args, scratch=(), mib=8):
    return pl.pallas_call(
        kernel,
        out_shape=out_shape,
        in_specs=[smem()] * smems + [vmem()] * (len(args) - smems),
        out_specs=jax.tree.map(lambda _: vmem(), out_shape),
        scratch_shapes=scratch,
        compiler_params=pltpu.CompilerParams(vmem_limit_bytes=mib * 1024 * 1024),
        name=name,
    )(*args)


def body(orbitals, points, quad_weight, external, screening, level_index, near_cells, far_cells):
    kinds, cells, point_count = orbitals.shape
    planes, groups = lax.axis_size("space"), lax.axis_size("orb")
    orbs = kinds * groups
    window = 3 * PLANE
    share = cells // groups
    me, group = lax.axis_index("space"), lax.axis_index("orb")
    meta = jnp.stack([me, group]).astype(jnp.int32)
    f32, bf16 = jnp.float32, jnp.bfloat16

    fields = gather_list(orbitals, "orb")
    weight = quad_weight * (cell_side**3 / point_count)
    own = jnp.concatenate([points, external[None], weight[None], jnp.zeros((3, cells, LANES), f32)], axis=0)
    marks = jnp.pad(level_index.astype(f32), (0, LANES - kinds))[None]
    ends = planes - 1
    up = [(i, i + 1) for i in range(ends)]
    down = [(i + 1, i) for i in range(ends)]
    slots = (near_cells.shape[1], far_cells.shape[1])
    lists = jnp.concatenate([near_cells, far_cells], axis=1)
    partial = jnp.sum(orbitals * orbitals, axis=0)
    basis = pltpu.VMEM((3 * NODES, ROWS, LANES), f32)

    charges = call(
        charge_kernel,
        "charge",
        jax.ShapeDtypeStruct((cells, ROWS, LANES), f32),
        1,
        (meta, own, partial, *fields[1:]),
        [pltpu.VMEM((cells, LANES), f32), basis],
    )
    mine = jnp.concatenate([f.reshape(kinds * cells, LANES) for f in fields], axis=0)
    charges, mine = gather_parts(charges, "space", False, mine)
    before = lax.ppermute(mine, "space", up)

    batch, unit, steps = 4, 4, 18
    most = near_cells.shape[1]
    blocks = most + (window - most + planes - 2) // 2 + unit - 1
    blocks = -(-blocks // unit) * unit
    shares, pts, src = call(
        functools.partial(hartree_kernel, groups, kinds, unit, slots),
        "hartree",
        (
            jax.ShapeDtypeStruct((1 + groups, ROWS, LANES), f32),
            jax.ShapeDtypeStruct((window, ROWS, LANES), f32),
            jax.ShapeDtypeStruct((share, blocks, ROWS, LANES), f32),
        ),
        2,
        (meta, lists, marks, mine, *charges),
        [
            pltpu.VMEM((planes, cells, ROWS, LANES), f32),
            pltpu.VMEM((window + planes + 1, ROWS, LANES), f32),
            pltpu.VMEM((3, LANES, LANES), f32),
            pltpu.VMEM((share, LANES, LANES), f32),
            basis,
        ],
        12,
    )
    mine, shares = lax.optimization_barrier((mine, shares))
    after = lax.ppermute(mine, "space", down)
    n_squares = 2 if share % 2 == 0 else 1

    def distances(k, src):
        return call(
            functools.partial(pairs_kernel, k * share // n_squares, groups, planes, unit, slots),
            "pairs",
            jax.ShapeDtypeStruct((share // n_squares, blocks, LANES, LANES), f32),
            2,
            (meta, lists, pts, src),
            [pltpu.VMEM((3, LANES, LANES), f32)],
            4,
        )

    squares = [distances(0, src)]
    shares = gather_list(shares, "orb")
    levels = jnp.concatenate([share[0, ROWS - 1, :kinds] for share in shares]).astype(jnp.int32)
    hartree, combined = call(
        functools.partial(combine_kernel, kinds),
        "combine",
        (jax.ShapeDtypeStruct((cells, LANES), f32), jax.ShapeDtypeStruct((cells + orbs // 2, LANES), f32)),
        1,
        (meta, *shares),
        [pltpu.VMEM((orbs, LANES), f32)],
    )
    gathered, src = gather_parts(combined, "space", False, src)
    if n_squares > 1:
        squares.append(distances(1, src))

    levels_at_most = -(-screening.shape[0] // batch) + 1
    sent = call(
        functools.partial(orbital_kernel, planes, batch, unit, steps, slots, n_squares),
        "orbitals",
        jax.ShapeDtypeStruct((groups, share, kinds, LANES), f32),
        4,
        (meta, lists, levels, screening * (-log2e), pts, before, mine, after, *squares, *gathered),
        [
            pltpu.SMEM((screening.shape[0] + 2 * batch,), f32),
            pltpu.SMEM((screening.shape[0],), jnp.int32),
            pltpu.SMEM((share,), jnp.int32),
            pltpu.VMEM((planes, cells + orbs // 2, LANES), f32),
            pltpu.VMEM((window, LANES, 2 * orbs), bf16),
            pltpu.VMEM((window + planes, HALF, 2 * orbs), bf16),
            pltpu.VMEM((share // n_squares, blocks, LANES, 2 * orbs), bf16),
            pltpu.VMEM((share // n_squares, blocks, LANES, LANES), f32),
            pltpu.VMEM((share // n_squares, blocks, LANES, LANES), f32),
            pltpu.VMEM((share // n_squares, levels_at_most, batch * LANES, 2 * orbs), f32),
            basis,
        ],
        28,
    )
    parts = [sent[0]]
    for k in range(1, groups):
        parts.append(lax.ppermute(sent[k], "orb", [(i, i ^ k) for i in range(groups)]))
    updated = call(
        place_kernel,
        "place",
        jax.ShapeDtypeStruct((kinds, cells, LANES), f32),
        1,
        (meta, *parts),
        [pltpu.VMEM((cells, kinds, LANES), f32)],
    )
    return updated, hartree


def solution(mesh):
    in_specs = (
        P("orb", "space", None),
        P(None, "space", None),
        P("space", None),
        P("space", None),
        P(),
        P("orb"),
        P("space", None),
        P("space", None),
    )
    out_specs = (P("orb", "space", None), P("space", None))
    return jax.shard_map(body, mesh=mesh, in_specs=in_specs, out_specs=out_specs, check_vma=False)
```

```python
import functools
import math

import jax
import jax.numpy as jnp
import numpy as np
from jax import lax
from jax.experimental import pallas as pl
from jax.experimental.pallas import tpu as pltpu
from jax.sharding import PartitionSpec as P

NODES = 4
LANES = 128
PLANE = 16
ROWS = 8
HALF = NODES**3

cell_side = 0.25
soften = 6.25e-06
green_scale = -0.5 / math.pi
log2e = math.log2(math.e)
highest = lax.Precision.HIGHEST

node_set = np.cos((2.0 * np.arange(NODES) + 1.0) * (math.pi / (2.0 * NODES)))
roots = [[node_set[m] for m in range(NODES) if m != a] for a in range(NODES)]
scales = [1.0 / np.prod([node_set[a] - r for r in roots[a]]) for a in range(NODES)]


def put_basis(cst):
    row = lax.broadcasted_iota(jnp.int32, (ROWS, LANES), 0)
    for i, pick in enumerate((row // 4, 2 + row // 4, row % 4)):
        for k in range(NODES):
            values = [float(scales[a] if k == NODES - 1 else roots[a][k]) for a in range(NODES)]
            made = jnp.full((ROWS, LANES), values[0], jnp.float32)
            for a in range(1, NODES):
                made = jnp.where(pick == a, values[a], made)
            cst[NODES * i + k] = made


def node_offsets():
    lane = lax.broadcasted_iota(jnp.int32, (1, LANES), 1) % HALF
    out = []
    for pick in (lane // 16, lane // 4 % 4, lane % 4):
        made = jnp.full((1, LANES), 0.5 * (node_set[0] + 1.0), jnp.float32)
        for a in range(1, NODES):
            made = jnp.where(pick == a, float(0.5 * (node_set[a] + 1.0)), made)
        out.append(made)
    return out


def poly(u, r0, r1, r2, scale):
    return ((u - r0) * (u - r1)) * ((u - r2) * scale)


def weights(cst, x, y, z, lows, sides):
    ux, uy, uz = (
        jnp.broadcast_to(2.0 * (c - lo) / e - 1.0, (ROWS, LANES)) for c, lo, e in zip((x, y, z), lows, sides)
    )
    pz = poly(uz, cst[8], cst[9], cst[10], cst[11])
    pyz = [poly(uy, cst[4 * k], cst[4 * k + 1], cst[4 * k + 2], cst[4 * k + 3]) * pz for k in range(2)]
    parts = []
    for a in range(NODES):
        px = poly(ux, *(float(r) for r in roots[a]), float(scales[a]))
        parts += [px * pyz[0], px * pyz[1]]
    return jnp.concatenate(parts, axis=0)


def twice(w):
    return jnp.concatenate([w, w], axis=0)


def cell_low(cell):
    return [(cell % 4).astype(jnp.float32) * cell_side, (cell // 4 % 4).astype(jnp.float32) * cell_side]


def dot_nt(a, b):
    return lax.dot_general(a, b, (((1,), (1,)), ((), ())), precision=highest, preferred_element_type=jnp.float32)


def gather_parts(block, axis, pairs, later=None):
    count = lax.axis_size(axis)
    parts = [block[None]]
    while sum(p.shape[0] for p in parts) < count:
        held = parts[0] if len(parts) == 1 else jnp.concatenate(parts, axis=0)
        have = held.shape[0]
        steps = range(1, 4 if (have > 1 or pairs) and have * 4 <= count else 2)
        parts = [held] + [lax.ppermute(held, axis, [(i, i ^ (have * j)) for i in range(count)]) for j in steps]
        if later is not None and have == 1:
            parts[1], later = lax.optimization_barrier((parts[1], later))
    return parts, later


def gather_list(block, axis):
    parts, _ = gather_parts(block, axis, True)
    return [p[k] for p in parts for k in range(p.shape[0])]


def lay_out(parts, whole):
    at = 0
    for part in parts:
        for k in range(part.shape[0]):
            whole[at + k] = part[k]
        at += part.shape[0]


def target_cell(me, t, groups):
    return t * groups + lax.bitwise_xor(jnp.int32(t) if isinstance(t, int) else t, me)


def split(v):
    high = v.astype(jnp.bfloat16)
    return high, (v - high.astype(jnp.float32)).astype(jnp.bfloat16)


def dot_bf16(a, b):
    return lax.dot_general(a, b, (((1,), (1,)), ((), ())), preferred_element_type=jnp.float32)


def dot_split(v, w):
    vh, vl = split(v)
    wh, wl = split(w)
    rows = v.shape[0]
    both = dot_bf16(jnp.concatenate([vh, vl], axis=0), wh)
    return both[:rows] + both[rows:] + dot_bf16(vh, wl)


def lane_sums(v):
    high, low = split(v)
    ones = jnp.ones((ROWS, 2 * v.shape[1]), jnp.bfloat16)
    return dot_bf16(ones, jnp.concatenate([high, low], axis=1))[0:1, :]


def charge_kernel(meta, own, partial, *refs):
    z_low = meta[0].astype(jnp.float32) * cell_side
    fields, (out, density, cst) = refs[:-3], refs[-3:]
    put_basis(cst)
    total = partial[...]
    for phi in fields:
        for j in range(phi.shape[0]):
            v = phi[j]
            total = total + v * v
    density[...] = 2.0 * total
    acc = jnp.zeros((HALF, LANES), jnp.float32)
    for c in range(PLANE):
        point = own[:, c, :]
        charge = point[4:5] * density[c : c + 1, :]
        low = (cell_side * (c % 4), cell_side * (c // 4), z_low)
        acc = acc + weights(cst, point[0:1], point[1:2], point[2:3], (0.0, 0.0, z_low), (1.0, 1.0, cell_side)) * charge
        moments = lane_sums(weights(cst, point[0:1], point[1:2], point[2:3], low, (cell_side,) * 3) * charge)
        out[c, :5, :] = point[:5]
        out[c, 5:6, :] = charge
        out[c, 6:7, :] = jnp.concatenate([moments, moments], axis=1)
    moments = lane_sums(acc)
    for c in range(PLANE):
        out[c, 7:8, :] = jnp.concatenate([moments, moments], axis=1)


def live_planes(me, planes):
    below = jnp.maximum(me - 1, 0)
    return below, below + jnp.maximum(planes - 2 - me, 0)


def list_lengths(lists, cell, slots, me, planes):
    low, high = jnp.int32(0), jnp.int32(slots[0])
    for _ in range(slots[0].bit_length()):
        mid = (low + high) // 2
        live = (low < high) & (lists[cell, jnp.minimum(mid, slots[0] - 1)] >= 0)
        high = jnp.where(live | (low >= high), high, mid)
        low = jnp.where(live, mid + 1, low)
    around = 1 + (me > 0).astype(jnp.int32) + (me + 1 < planes).astype(jnp.int32)
    return low, around * PLANE - low


def list_blocks(me, cell, lists, slots, planes, put_near, put_far, put_none, multiple):
    window = 3 * PLANE
    base = (me - 1) * PLANE
    below, n_planes = live_planes(me, planes)
    near_slots, far_slots = slots
    n_near, n_far = list_lengths(lists, cell, slots, me, planes)
    n_items = n_far + n_planes
    n_pairs = (n_items + 1) // 2

    def near_step(i, c):
        for j in (2 * i, 2 * i + 1):
            put_near(j, jnp.clip(lists[cell, j] - base, 0, window - 1))
        return c

    lax.fori_loop(0, (n_near + 1) // 2, near_step, 0)

    def item(j):
        j = jnp.minimum(j, n_items - 1)
        p = j - n_far
        level = jnp.where(p < below, p, p + (me + 2 - below))
        slot = lists[cell, near_slots + jnp.minimum(j, far_slots - 1)] - base
        return jnp.where(j < n_far, slot, window + level)

    def far_step(i, c):
        for j in (2 * i, 2 * i + 1):
            put_far(n_near + j, item(2 * j), item(2 * j + 1), 2 * j + 1 < n_items)
        return c

    lax.fori_loop(0, (n_pairs + 1) // 2, far_step, 0)
    for u in range(multiple - 1):
        put_none(n_near + n_pairs + u)
    return n_near + n_pairs


def in_low_half():
    return lax.broadcasted_iota(jnp.int32, (1, LANES), 1) < HALF


def put_targets(pts, cell, tgt):
    for d in range(3):
        tgt[d] = jnp.broadcast_to(pts[PLANE + cell, d : d + 1, :], (LANES, LANES)).T


def each_square(tgt, src, first, count, use):
    sources = [[src[first + u, d : d + 1, :] for d in range(3)] for u in range(count)]
    for r in range(LANES // ROWS):
        at = [tgt[d, r * ROWS : (r + 1) * ROWS, :] for d in range(3)]
        for u in range(count):
            dx, dy, dz = (a - b for a, b in zip(at, sources[u]))
            use(r, u, (dx * dx + dy * dy) + (dz * dz + soften))


def cell_fields(message, c, groups, kinds):
    rows = kinds * PLANE
    return jnp.concatenate([message[pl.ds(g * rows + c, kinds, stride=PLANE), :] for g in range(groups)], axis=0)


def hartree_kernel(groups, kinds, unroll, slots, meta, lists, marks, mine, *refs):
    parts, (out, pts, src, every, items, tgt, sums, cst) = refs[:-8], refs[-8:]
    lay_out(parts, every)
    planes = every.shape[0]
    cells = PLANE // groups
    me, group = meta[0], meta[1]
    window = 3 * PLANE
    put_basis(cst)
    for k in range(3):
        there = lax.bitwise_xor(me, jnp.clip(me - 1 + k, 0, planes - 1))
        for c in range(PLANE):
            pts[k * PLANE + c] = every[there, c]
    row = lax.broadcasted_iota(jnp.int32, (ROWS, 1), 0)

    offsets = node_offsets()

    def item_of(lows, sides, moments):
        made = jnp.where(row == 5, moments, 0.0)
        for d in range(3):
            made = jnp.where(row == d, lows[d] + offsets[d] * sides[d], made)
        return made

    def put_cell(c, carry):
        lows = (*cell_low(c), (me - 1 + c // PLANE).astype(jnp.float32) * cell_side)
        items[c] = item_of(lows, (cell_side,) * 3, pts[c, 6:7, :])
        return carry

    lax.fori_loop(0, window, put_cell, 0, unroll=16)

    def put_plane(g, c):
        lows = (0.0, 0.0, g.astype(jnp.float32) * cell_side)
        items[window + g] = item_of(lows, (1.0, 1.0, cell_side), every[lax.bitwise_xor(me, g), 0, 7:8, :])
        return c

    lax.fori_loop(0, planes, put_plane, 0, unroll=8)
    items[window + planes] = jnp.zeros((ROWS, LANES), jnp.float32)
    low_half = in_low_half()
    z_low = me.astype(jnp.float32) * cell_side
    out[0] = jnp.broadcast_to(marks[...], (ROWS, LANES))

    def per_cell(t, carry):
        cell = target_cell(group, t, groups)

        def put_near(j, slot):
            src[t, j] = pts[slot]

        def put_far(j, first, second, live):
            src[t, j] = jnp.where(low_half, items[first], items[jnp.where(live, second, window + planes)])

        def put_none(j):
            src[t, j] = jnp.zeros((ROWS, LANES), jnp.float32)

        n_blocks = list_blocks(me, cell, lists, slots, planes, put_near, put_far, put_none, unroll)
        put_targets(pts, cell, tgt)

        def step(i, accs):
            accs = list(accs)
            charges = [src[t, unroll * i + u, 5:6, :] for u in range(unroll)]

            def use(r, u, sq):
                accs[r] = accs[r] + lax.rsqrt(sq) * charges[u]

            each_square(tgt, src.at[t], unroll * i, unroll, use)
            return tuple(accs)

        zero = jnp.zeros((ROWS, LANES), jnp.float32)
        accs = lax.fori_loop(0, (n_blocks + unroll - 1) // unroll, step, (zero,) * (LANES // ROWS))
        sums[t] = jnp.concatenate(accs, axis=0)
        return carry

    lax.fori_loop(0, cells, per_cell, 0)
    ones = jnp.ones((ROWS, LANES), jnp.float32)
    found = dot_nt(ones, sums[...].reshape(cells * LANES, LANES))
    total = jnp.zeros((groups * kinds, LANES), jnp.float32)
    for t in range(cells):
        cell = target_cell(group, t, groups)
        potential = found[0:1, t * LANES : (t + 1) * LANES]
        out[0, t : t + 1, :] = potential
        point = pts[PLANE + cell]
        scaled = point[4:5] * (point[3:4] + potential)
        v = cell_fields(mine, cell, groups, kinds) * scaled
        w = weights(cst, point[0:1], point[1:2], point[2:3], (0.0, 0.0, z_low), (1.0, 1.0, cell_side))
        total = total + dot_split(v, twice(w))
    for k in range(groups):
        out[1 + lax.bitwise_xor(group, k), :kinds, :] = total[k * kinds : (k + 1) * kinds, :]


def pairs_kernel(first, groups, planes, unroll, slots, meta, lists, pts, src, out, tgt):
    group = meta[1]
    _, n_planes = live_planes(meta[0], planes)

    def per_cell(t, carry):
        cell = target_cell(group, first + t, groups)
        put_targets(pts, cell, tgt)
        n_near, n_far = list_lengths(lists, cell, slots, meta[0], planes)
        n_blocks = n_near + (n_far + n_planes + 1) // 2

        def measure(i, x):
            def use(r, u, sq):
                out[t, unroll * i + u, r * ROWS : (r + 1) * ROWS, :] = sq

            each_square(tgt, src.at[first + t], unroll * i, unroll, use)
            return x

        lax.fori_loop(0, (n_blocks + unroll - 1) // unroll, measure, 0)
        return carry

    lax.fori_loop(0, out.shape[0], per_cell, 0)


def combine_kernel(kinds, meta, *refs):
    shares, (hartree, out, total) = refs[:-3], refs[-3:]
    groups = len(shares)
    for k, share in enumerate(shares):
        for t in range(PLANE // groups):
            cell = target_cell(lax.bitwise_xor(meta[1], k), t, groups)
            out[pl.ds(cell, 1), :] = share[0, t : t + 1, :]
    hartree[...] = out[:PLANE, :]
    for g in range(groups):
        added = shares[0][1 + g, :kinds, :]
        for share in shares[1:]:
            added = added + share[1 + g, :kinds, :]
        total[g * kinds : (g + 1) * kinds, :] = added
    rows = groups * kinds // 2
    low_half = lax.broadcasted_iota(jnp.int32, (1, LANES), 1) < HALF
    out[PLANE:, :] = jnp.where(low_half, total[:rows, :], total[rows:, :])


def orbital_kernel(
    planes, batch, unit, steps, slots, n_squares, meta, lists, levels, rates_of,
    pts, before, mine, after, *refs,
):
    squares, refs = refs[:n_squares], refs[n_squares:]
    parts, (out, rate, slot_of, units, every, val, mom, srcv, dist, inv, acc, cst) = refs[:-12], refs[-12:]
    lay_out(parts, every)
    groups, cells, kinds, _ = out.shape
    orbs = groups * kinds
    n_rates = rates_of.shape[0]
    me, group = meta[0], meta[1]

    def clear(i, c):
        slot_of[i] = -1
        rate[i] = 0.0
        return c

    lax.fori_loop(0, n_rates, clear, 0)
    for q in range(2 * batch):
        rate[n_rates + q] = 0.0
    lane = lax.broadcasted_iota(jnp.int32, (1, LANES), 1) % orbs

    def rank(i, carry):
        found, lane_slot = carry
        level = levels[i]
        known = slot_of[level]
        slot = jnp.where(known < 0, found, known)
        slot_of[level] = slot
        rate[slot] = rates_of[level]
        return found + (known < 0).astype(jnp.int32), jnp.where(lane == i, slot, lane_slot)

    n_levels, lane_slot = lax.fori_loop(0, orbs, rank, (jnp.int32(0), jnp.zeros((1, LANES), jnp.int32)), unroll=4)
    left = lax.rem(n_levels, batch)
    short = (left > 0) & (left <= batch // 2)
    n_whole = n_levels // batch + ((left > 0) & jnp.logical_not(short)).astype(jnp.int32)
    n_batches = n_whole + short.astype(jnp.int32)
    first_half = lax.broadcasted_iota(jnp.int32, (1, 2 * orbs), 1) < orbs
    put_basis(cst)

    def flip(v):
        high = v.astype(jnp.bfloat16).astype(jnp.float32)
        square = jnp.concatenate([high, v - high, jnp.zeros((LANES - 2 * orbs, LANES), jnp.float32)], axis=0)
        return square.T[:, : 2 * orbs].astype(jnp.bfloat16)

    for k in range(3):
        message = (before, mine, after)[k]
        there = lax.bitwise_xor(me, jnp.clip(me - 1 + k, 0, planes - 1))

        def prepare(c, carry):
            at = k * PLANE + c
            point = pts[at]
            potential = point[3:4] + every[there, pl.ds(c, 1), :]
            v = cell_fields(message, c, groups, kinds) * (point[4:5] * potential)
            val[at] = flip(v)
            vh, vl = split(v)
            z_low = (me - 1 + k).astype(jnp.float32) * cell_side
            low = (*cell_low(c), z_low)
            wh, wl = split(weights(cst, point[0:1], point[1:2], point[2:3], low, (cell_side,) * 3))
            all_of = dot_bf16(jnp.concatenate([wh, wl], axis=0), jnp.concatenate([vh, vh, vl, vl], axis=0))
            m = all_of[:HALF] + all_of[HALF:]
            m = m[:, : 2 * orbs] + pltpu.roll(all_of[:HALF], 2 * orbs, 1)[:, : 2 * orbs]
            high = m.astype(jnp.bfloat16).astype(jnp.float32)
            mom[at] = jnp.where(first_half, high, m - high).astype(jnp.bfloat16)
            return carry

        lax.fori_loop(0, PLANE, prepare, 0, unroll=16)

    def put_plane(g, c):
        there = lax.bitwise_xor(me, g)
        rows = []
        for k in range(groups):
            row = lax.bitwise_xor(group, k) * kinds
            v = every[there, pl.ds(PLANE + lax.rem(row, orbs // 2), kinds), :]
            rows.append(jnp.where(row < orbs // 2, v, pltpu.roll(v, HALF, 1)))
        mom[3 * PLANE + g] = flip(jnp.concatenate(rows, axis=0))[:HALF]
        return c

    lax.fori_loop(0, planes, put_plane, 0, unroll=8)

    def products(g, b, first, width):
        rates = [rate[b * batch + q] for q in range(width)]
        rows = []
        for q in range(width):
            tiles = [
                (jnp.exp2(dist[g, first + h] * rates[q]) * inv[g, first + h]).astype(jnp.bfloat16) for h in range(unit)
            ]
            rows.append(jnp.concatenate(tiles, axis=1))
        v = jnp.concatenate([srcv[g, first + h] for h in range(unit)], axis=0)
        return jnp.dot(jnp.concatenate(rows, axis=0), v, preferred_element_type=jnp.float32)

    share = cells // n_squares

    def per_group(p, carry):
        def list_cell(g, x):
            def put_near(j, slot):
                srcv[g, j] = val[slot]

            def put_far(j, first, second, live):
                srcv[g, j, :HALF, :] = mom[first]
                srcv[g, j, HALF:, :] = jnp.where(live, mom[second], jnp.zeros_like(mom[second]))

            def put_none(j):
                srcv[g, j] = jnp.zeros(srcv.shape[2:], srcv.dtype)

            cell = target_cell(group, p * share + g, groups)
            n_blocks = list_blocks(me, cell, lists, slots, planes, put_near, put_far, put_none, unit)
            units[g] = (n_blocks + unit - 1) // unit

            def clear_acc(b, y):
                acc[g, b] = jnp.zeros(acc.shape[2:], jnp.float32)
                return y

            lax.fori_loop(0, n_batches, clear_acc, 0)
            return x

        lax.fori_loop(0, share, list_cell, 0)

        for k in range(n_squares):

            @pl.when(p == k)
            def _():
                for g in range(share):

                    def measure(i, x):
                        for u in range(unit):
                            sq = squares[k][g, unit * i + u]
                            one_over = lax.rsqrt(sq)
                            inv[g, unit * i + u] = one_over
                            dist[g, unit * i + u] = sq * one_over
                        return x

                    lax.fori_loop(0, units[g], measure, 0)

        nowhere = acc.shape[1] - 1

        def step(i, at):
            g, b, u = at
            for _ in range(steps):
                acc[g, b] = acc[g, b] + products(g, b, unit * u, batch)
                wrap = u + 1 >= units[g]
                later = jnp.where(wrap, b + 1, b)
                over, last = later >= n_whole, g + 1 >= share
                u = jnp.where(wrap, 0, u + 1)
                b = jnp.where(over, jnp.where(last, nowhere, 0), later)
                g = jnp.where(over & jnp.logical_not(last), g + 1, g)
            return g, b, u

        def short_step(i, at):
            g, u, b = at
            for _ in range(steps):
                at_rows = (g, b, slice(0, batch // 2 * LANES))
                acc[at_rows] = acc[at_rows] + products(g, b, unit * u, batch // 2)
                wrap, last = u + 1 >= units[g], g + 1 >= share
                u = jnp.where(wrap, 0, u + 1)
                b = jnp.where(wrap & last, nowhere, b)
                g = jnp.where(wrap & jnp.logical_not(last), g + 1, g)
            return g, u, b

        work = sum(units[g] for g in range(share))
        zero = jnp.int32(0)
        lax.fori_loop(0, (work * n_whole + steps - 1) // steps, step, (zero, zero, zero))
        rest = jnp.where(short, (work + steps - 1) // steps, 0)
        lax.fori_loop(0, rest, short_step, (zero, zero, n_whole))

        def finish(g, x):
            def choose(b, add):
                for q in range(batch):
                    mine = lane_slot[:, : 2 * orbs] == b * batch + q
                    add = add + jnp.where(mine, acc[g, b, q * LANES : (q + 1) * LANES, :], 0.0)
                return add

            total = lax.fori_loop(0, n_batches, choose, jnp.zeros((LANES, 2 * orbs), jnp.float32))
            flipped = jnp.concatenate([total, jnp.zeros((LANES, LANES - 2 * orbs), jnp.float32)], axis=1).T
            rows = (flipped[:orbs] + flipped[orbs : 2 * orbs]) * green_scale
            for k in range(groups):
                out[k, p * share + g] = rows[k * kinds : (k + 1) * kinds]
            return x

        lax.fori_loop(0, share, finish, 0)
        return carry

    lax.fori_loop(0, n_squares, per_group, 0)


def place_kernel(meta, *refs):
    parts, out, ordered = refs[:-2], refs[-2], refs[-1]
    for k, part in enumerate(parts):
        for t in range(part.shape[0]):
            ordered[target_cell(lax.bitwise_xor(meta[1], k), t, len(parts))] = part[t]
    for c in range(PLANE):
        out[:, c, :] = ordered[c]


def smem():
    return pl.BlockSpec(memory_space=pltpu.SMEM)


def vmem():
    return pl.BlockSpec(memory_space=pltpu.VMEM)


def call(kernel, name, out_shape, smems, args, scratch=(), mib=8):
    return pl.pallas_call(
        kernel,
        out_shape=out_shape,
        in_specs=[smem()] * smems + [vmem()] * (len(args) - smems),
        out_specs=jax.tree.map(lambda _: vmem(), out_shape),
        scratch_shapes=scratch,
        compiler_params=pltpu.CompilerParams(vmem_limit_bytes=mib * 1024 * 1024),
        name=name,
    )(*args)


def body(orbitals, points, quad_weight, external, screening, level_index, near_cells, far_cells):
    kinds, cells, point_count = orbitals.shape
    planes, groups = lax.axis_size("space"), lax.axis_size("orb")
    orbs = kinds * groups
    window = 3 * PLANE
    share = cells // groups
    me, group = lax.axis_index("space"), lax.axis_index("orb")
    meta = jnp.stack([me, group]).astype(jnp.int32)
    f32, bf16 = jnp.float32, jnp.bfloat16

    fields = gather_list(orbitals, "orb")
    weight = quad_weight * (cell_side**3 / point_count)
    own = jnp.concatenate([points, external[None], weight[None], jnp.zeros((3, cells, LANES), f32)], axis=0)
    marks = jnp.pad(level_index.astype(f32), (0, LANES - kinds))[None]
    ends = planes - 1
    up = [(i, i + 1) for i in range(ends)]
    down = [(i + 1, i) for i in range(ends)]
    slots = (near_cells.shape[1], far_cells.shape[1])
    lists = jnp.concatenate([near_cells, far_cells], axis=1)
    partial = jnp.sum(orbitals * orbitals, axis=0)
    basis = pltpu.VMEM((3 * NODES, ROWS, LANES), f32)

    charges = call(
        charge_kernel,
        "charge",
        jax.ShapeDtypeStruct((cells, ROWS, LANES), f32),
        1,
        (meta, own, partial, *fields[1:]),
        [pltpu.VMEM((cells, LANES), f32), basis],
    )
    mine = jnp.concatenate([f.reshape(kinds * cells, LANES) for f in fields], axis=0)
    charges, mine = gather_parts(charges, "space", False, mine)
    before = lax.ppermute(mine, "space", up)

    batch, unit, steps = 4, 4, 18
    most = near_cells.shape[1]
    blocks = most + (window - most + planes - 2) // 2 + unit - 1
    blocks = -(-blocks // unit) * unit
    shares, pts, src = call(
        functools.partial(hartree_kernel, groups, kinds, unit, slots),
        "hartree",
        (
            jax.ShapeDtypeStruct((1 + groups, ROWS, LANES), f32),
            jax.ShapeDtypeStruct((window, ROWS, LANES), f32),
            jax.ShapeDtypeStruct((share, blocks, ROWS, LANES), f32),
        ),
        2,
        (meta, lists, marks, mine, *charges),
        [
            pltpu.VMEM((planes, cells, ROWS, LANES), f32),
            pltpu.VMEM((window + planes + 1, ROWS, LANES), f32),
            pltpu.VMEM((3, LANES, LANES), f32),
            pltpu.VMEM((share, LANES, LANES), f32),
            basis,
        ],
        12,
    )
    mine, shares = lax.optimization_barrier((mine, shares))
    after = lax.ppermute(mine, "space", down)
    n_squares = 2 if share % 2 == 0 else 1

    def distances(k, src):
        return call(
            functools.partial(pairs_kernel, k * share // n_squares, groups, planes, unit, slots),
            "pairs",
            jax.ShapeDtypeStruct((share // n_squares, blocks, LANES, LANES), f32),
            2,
            (meta, lists, pts, src),
            [pltpu.VMEM((3, LANES, LANES), f32)],
            4,
        )

    squares = [distances(0, src)]
    shares = gather_list(shares, "orb")
    levels = jnp.concatenate([share[0, ROWS - 1, :kinds] for share in shares]).astype(jnp.int32)
    hartree, combined = call(
        functools.partial(combine_kernel, kinds),
        "combine",
        (jax.ShapeDtypeStruct((cells, LANES), f32), jax.ShapeDtypeStruct((cells + orbs // 2, LANES), f32)),
        1,
        (meta, *shares),
        [pltpu.VMEM((orbs, LANES), f32)],
    )
    gathered, src = gather_parts(combined, "space", False, src)
    if n_squares > 1:
        squares.append(distances(1, src))

    levels_at_most = -(-screening.shape[0] // batch) + 1
    sent = call(
        functools.partial(orbital_kernel, planes, batch, unit, steps, slots, n_squares),
        "orbitals",
        jax.ShapeDtypeStruct((groups, share, kinds, LANES), f32),
        4,
        (meta, lists, levels, screening * (-log2e), pts, before, mine, after, *squares, *gathered),
        [
            pltpu.SMEM((screening.shape[0] + 2 * batch,), f32),
            pltpu.SMEM((screening.shape[0],), jnp.int32),
            pltpu.SMEM((share,), jnp.int32),
            pltpu.VMEM((planes, cells + orbs // 2, LANES), f32),
            pltpu.VMEM((window, LANES, 2 * orbs), bf16),
            pltpu.VMEM((window + planes, HALF, 2 * orbs), bf16),
            pltpu.VMEM((share // n_squares, blocks, LANES, 2 * orbs), bf16),
            pltpu.VMEM((share // n_squares, blocks, LANES, LANES), f32),
            pltpu.VMEM((share // n_squares, blocks, LANES, LANES), f32),
            pltpu.VMEM((share // n_squares, levels_at_most, batch * LANES, 2 * orbs), f32),
            basis,
        ],
        28,
    )
    parts = [sent[0]]
    for k in range(1, groups):
        parts.append(lax.ppermute(sent[k], "orb", [(i, i ^ k) for i in range(groups)]))
    updated = call(
        place_kernel,
        "place",
        jax.ShapeDtypeStruct((kinds, cells, LANES), f32),
        1,
        (meta, *parts),
        [pltpu.VMEM((cells, kinds, LANES), f32)],
    )
    return updated, hartree


def solution(mesh):
    in_specs = (
        P("orb", "space", None),
        P(None, "space", None),
        P("space", None),
        P("space", None),
        P(),
        P("orb"),
        P("space", None),
        P("space", None),
    )
    out_specs = (P("orb", "space", None), P("space", None))
    return jax.shard_map(body, mesh=mesh, in_specs=in_specs, out_specs=out_specs, check_vma=False)
```
